32 devices in a mesh: sec: 4 (over x, core), tile: 8 (over z, y).
Axes of the slice: x: 2, y: 2, z: 4, core: 2. Of those that a mesh axis runs over, the one named last changes fastest.
Arguments:
- ocean_u: float32 [64, 16384], P(None, ('sec', 'tile')), may hold values from -2 to 2
- ocean_b: float32 [64, 16384], P(None, ('sec', 'tile')), may hold values from -4 to 4
- tracers: bfloat16 [17, 64, 12288], P(None, None, ('sec', 'tile')), may hold values from 0.099609375 to 2
- wet_tiles: int32 [96], replicated, may hold values from 0 to 127, as said below
- kinetic_matrix: float32 [17, 17], replicated, may hold values from -0.42 to 1.5
Outputs:
- tracers_out: bfloat16 [17, 64, 12288], P(None, None, ('sec', 'tile'))
- ocean_u_out: float32 [64, 16384], P(None, ('sec', 'tile'))
- ocean_b_out: float32 [64, 16384], P(None, ('sec', 'tile'))
The draws below stay inside these ranges and needn't reach their ends.
Inputs may be any that keep to these rules, and one draw needn't show every extreme that they name: `wet_tiles`: increasing tile numbers. For every k, of the tiles k * 4 to k * 4 + 3 either 2 or 4 are listed, and for every even k the tiles of k and k + 1 hold 6 listed tiles together.
All inputs are finite; a program needn't handle non-finite values.
Results may differ from the reference program's by a relative error of at most 0.001.
Values sent between devices are 32-bit elements; how exact they have to be, the bound alone decides.
No kernel may reach another device: no remote copies, remote signals or barrier semaphores. Data moves between devices by JAX's collectives and lax.ppermute only.
A program may use at most 64 MiB of HBM per device.

```python
import jax
import jax.numpy as jnp
from jax import lax

LEVELS = 64
TRACERS = 17
TILE_COLS = 128
STEPS = 2
WET = 96
TILES = 128
NCOL = 16384
WCOL = 12288


def draw_wet_tiles(key, part):
    devices = TILES // 4
    pair_key = jax.random.fold_in(key, 11)
    rank_key = jax.random.fold_in(key, 12)
    heavier = jax.random.randint(pair_key, (devices // 2,), 0, 2)
    counts = jnp.stack([2 + 2 * heavier, 4 - 2 * heavier], axis=1).reshape(devices)
    scores = jax.random.randint(rank_key, (devices, 4), 0, 1 << 20) * 4 + jnp.arange(4)[None, :]
    ranking = jnp.argsort(jnp.argsort(scores, axis=1), axis=1)
    wet_flags = (ranking < counts[:, None]).reshape(TILES)
    sort_keys = jnp.where(wet_flags, 0, TILES) + jnp.arange(TILES)
    ordering = jnp.argsort(sort_keys)
    return ordering[:WET].astype(jnp.int32)


def draw_kinetic_matrix(key, part):
    lead_key = jax.random.fold_in(key, 21)
    rest_key = jax.random.fold_in(key, 22)
    lead_row = jax.random.uniform(lead_key, (1, TRACERS), jnp.float32, 1.0, 1.5)
    rest_rows = jax.random.uniform(rest_key, (TRACERS - 1, TRACERS), jnp.float32, -0.42, 0.42)
    return jnp.concatenate([lead_row, rest_rows], axis=0)


def levels(rng, extent, split, low, high):
    def one(axis_at, blocks):
        draws = jax.random.uniform(jax.random.fold_in(jax.random.fold_in(rng, 6), axis_at), (blocks,), jnp.float32, low / len(split), high / len(split))
        return jnp.repeat(jnp.exp(draws), extent[axis_at] // blocks).reshape((-1,) + (1,) * (len(extent) - axis_at - 1))

    factor_of = one(*split[0])
    for cut in split[1:]:
        factor_of = factor_of * one(*cut)
    return factor_of


def centred(rng, shape, width, limit, pieces=(), dtype=jnp.bfloat16):
    result = jax.random.normal(rng, shape, jnp.float32) * width
    if len(pieces) > 0:
        result = levels(rng, shape, pieces, -0.22, 0.18) * result
    return jnp.clip(result, min=-limit, max=limit).astype(dtype)


def setup_inputs(seed: int = 0) -> dict:
    key_of = jax.random.split(jax.random.key(seed), 6)
    ocean_u = centred(key_of[0], (LEVELS, NCOL), 0.5, 2.0, ((1, 32),), jnp.float32)
    ocean_b = centred(key_of[1], (LEVELS, NCOL), 1.0, 4.0, ((1, 32),), jnp.float32)
    tracers = jnp.clip(0.099609375 + 1.9003906 * jax.random.uniform(key_of[2], (TRACERS, LEVELS, WCOL), jnp.float32) ** levels(key_of[2], (TRACERS, LEVELS, WCOL), ((2, 32),), -0.2, 0.2), 0.099609375, 2.0).astype(jnp.bfloat16)
    wet_tiles = draw_wet_tiles(jax.random.fold_in(key_of[5], 71), 0)
    kinetic_matrix = draw_kinetic_matrix(jax.random.fold_in(key_of[5], 71), 0)
    return {"ocean_u": ocean_u, "ocean_b": ocean_b, "tracers": tracers, "wet_tiles": wet_tiles, "kinetic_matrix": kinetic_matrix}


DT_OCEAN = 0.25
PRESSURE = 1.0
HORIZ_VISC = 0.2
VERT_VISC = 0.2
HEATING = 0.2
KAPPA_BASE = 0.05
KAPPA_SPAN = 0.35
DT_TRACER = 0.3
DT_MIX = 1.0
KINETIC_DELTA = 0.5
SURFACE_LIGHT = 10.0
WATER_ATT = 0.04
PIGMENT_ATT = 0.08
GROWTH = 0.05
THERMAL_GAIN = 0.1


def vertical_term(field):
    upper_cells = jnp.concatenate([field[:1], field[:-1]], axis=0)
    lower_cells = jnp.concatenate([field[1:], field[-1:]], axis=0)
    return upper_cells + lower_cells - 2.0 * field


def ocean_core(vel_ext, buoy_ext):
    velocity = vel_ext[:, 1:-1]
    buoyancy = buoy_ext[:, 1:-1]
    horiz_term = vel_ext[:, :-2] + vel_ext[:, 2:] - 2.0 * velocity
    press_term = buoy_ext[:, 2:] - buoyancy
    updated = velocity + DT_OCEAN * (HORIZ_VISC * horiz_term + VERT_VISC * vertical_term(velocity) - PRESSURE * press_term)
    return updated, buoyancy


def diffusivity_of(velocity, buoyancy):
    shear_sq = (velocity[:-1] - velocity[1:]) ** 2
    stratified = buoyancy[:-1] - buoyancy[1:]
    interior = KAPPA_BASE + KAPPA_SPAN * jax.nn.sigmoid(4.0 * (shear_sq - stratified))
    return jnp.concatenate([interior, jnp.zeros_like(interior[:1])], axis=0)


def absorption_of(tracer_state):
    pigment = tracer_state[0]
    attenuation = WATER_ATT + PIGMENT_ATT * pigment * pigment
    optical_depth = jnp.cumsum(attenuation, axis=0)
    return SURFACE_LIGHT * (jnp.exp(attenuation - optical_depth) - jnp.exp(-optical_depth))


def profile_change(transported_solutes, turbulent_spreading, seawater_warmth, captured_radiance, kinetic_matrix):
    lower_cells = jnp.concatenate([transported_solutes[:, 1:], transported_solutes[:, -1:]], axis=1)
    vert_flux = turbulent_spreading[None] * (lower_cells - transported_solutes)
    upper_flux = jnp.concatenate([jnp.zeros_like(vert_flux[:, :1]), vert_flux[:, :-1]], axis=1)
    depth_blended_fields = transported_solutes + DT_MIX * (vert_flux - upper_flux)
    kinetic_drift = jnp.einsum("ij,jlc->ilc", kinetic_matrix, depth_blended_fields, precision=lax.Precision.HIGHEST)
    converted_solutes = depth_blended_fields + KINETIC_DELTA * jnp.exp(THERMAL_GAIN * seawater_warmth)[None] * kinetic_drift
    return jnp.concatenate([converted_solutes[:1] + GROWTH * captured_radiance[None], converted_solutes[1:]], axis=0)


def wrap_columns(field):
    return jnp.concatenate([field[:, -1:], field, field[:, :1]], axis=1)


def reference(ocean_u, ocean_b, tracers, wet_tiles, kinetic_matrix):
    following = jnp.roll(wet_tiles, -1)
    adjacent = (jnp.mod(following - wet_tiles, TILES) == 1).astype(jnp.float32)
    face_open = jnp.ones((WET, TILE_COLS), jnp.float32).at[:, TILE_COLS - 1].set(adjacent).reshape(WCOL)
    tracer_state = tracers.astype(jnp.float32)
    velocity = ocean_u
    buoyancy = ocean_b
    for step_index in range(STEPS):
        captured_radiance = absorption_of(tracer_state)
        heating_term = jnp.zeros((LEVELS, TILES, TILE_COLS), jnp.float32).at[:, wet_tiles].set(captured_radiance.reshape(LEVELS, WET, TILE_COLS)).reshape(LEVELS, NCOL)
        buoyancy = buoyancy + HEATING * heating_term
        velocity, buoyancy = ocean_core(wrap_columns(velocity), wrap_columns(buoyancy))
        turbulent_spreading = diffusivity_of(velocity, buoyancy)
        stacked = jnp.stack([velocity, turbulent_spreading, buoyancy]).reshape(3, LEVELS, TILES, TILE_COLS)
        coupled = stacked[:, :, wet_tiles].reshape(3, LEVELS, WCOL)
        face_u = coupled[0]
        following_state = jnp.roll(tracer_state, -1, axis=2)
        face_flux = (jnp.maximum(face_u, 0.0) * tracer_state + jnp.minimum(face_u, 0.0) * following_state) * face_open
        transported_solutes = tracer_state - DT_TRACER * (face_flux - jnp.roll(face_flux, 1, axis=2))
        tracer_state = profile_change(transported_solutes, coupled[1], coupled[2], captured_radiance, kinetic_matrix)
    return tracer_state.astype(jnp.bfloat16), velocity, buoyancy
```

```python
import functools

import jax
import jax.numpy as jnp
from jax import lax
from jax.experimental import pallas as pl
from jax.experimental.pallas import tpu as pltpu
from jax.sharding import PartitionSpec as P

LANES = 128
STEPS = 2
WET_DEV = 3
OCEAN_DEV = 4

DT_OCEAN = 0.25
PRESSURE = 1.0
HORIZ_VISC = 0.2
VERT_VISC = 0.2
HEATING = 0.2
KAPPA_BASE = 0.05
KAPPA_SPAN = 0.35
DT_TRACER = 0.3
DT_MIX = 1.0
KINETIC_DELTA = 0.5
SURFACE_LIGHT = 10.0
WATER_ATT = 0.04
PIGMENT_ATT = 0.08
GROWTH = 0.05
THERMAL_GAIN = 0.1

SEG = 40
HALF = SEG // 2
FIX = 8
PAD = 8
F32, BF16 = jnp.float32, jnp.bfloat16


def facts(dev_ref, wet_ref):
    f = {}
    k = dev_ref[0]
    odd = lax.rem(k, 2)
    first, base = WET_DEV * k, OCEAN_DEV * k
    listed = wet_ref.shape[0]
    tiles = listed // WET_DEV * OCEAN_DEV
    is_odd = odd == 1
    w = [wet_ref[first + s] for s in range(WET_DEV)]
    probe = wet_ref[first + jnp.where(is_odd, -1, 3)]
    gives = jnp.logical_and(probe >= base, probe < base + OCEAN_DEV)
    before = jnp.where(k == 0, listed - 1, first - 1)
    after = jnp.where(first + WET_DEV == listed, 0, first + WET_DEV)
    outer_tile = jnp.where(
        is_odd,
        jnp.where(base + OCEAN_DEV == tiles, 0, base + OCEAN_DEV),
        jnp.where(k == 0, tiles - 1, base - 1),
    )
    f["odd"], f["is_odd"], f["gives"], f["w"], f["base"] = odd, is_odd, gives, w, base
    f["outer_far_wet"] = wet_ref[jnp.where(is_odd, after, before)] == outer_tile
    f["outer_own_wet"] = jnp.where(is_odd, w[2] == base + 3, w[0] == base)
    f["x_slot"] = 2 - 2 * odd
    f["x_tile"] = 3 - 3 * odd
    f["outer_slot"] = 2 * odd
    f["outer_tile"] = 3 * odd
    f["beside_tile"] = jnp.where(gives, 2 - odd, 3 - 3 * odd)
    f["beside_slot"] = jnp.where(gives, 2 - 2 * odd, 1)
    f["beside_wet"] = jnp.logical_or(gives, w[1] == base + 3 - 3 * odd)
    far_listed = wet_ref[first + jnp.where(is_odd, -2, 4)] == base + jnp.where(is_odd, -1, 4)
    f["beyond_wet"] = jnp.logical_or(jnp.logical_not(gives), far_listed)
    return f


def lane_of(rows):
    return lax.broadcasted_iota(jnp.int32, (rows, LANES), 1)


def lane_roll(x, shift):
    return pltpu.roll(x, shift, x.ndim - 1)


def upper(x):
    row = lax.broadcasted_iota(jnp.int32, x.shape, 0)
    return jnp.where(row == 0, x, pltpu.roll(x, 1, 0))


def lower(x):
    n = x.shape[0]
    row = lax.broadcasted_iota(jnp.int32, x.shape, 0)
    return jnp.where(row == n - 1, x, pltpu.roll(x, n - 1, 0))


def absorbed_light(pigment):
    att = WATER_ATT + PIGMENT_ATT * pigment * pigment
    depth = att
    rows = att.shape[0]
    row = lax.broadcasted_iota(jnp.int32, att.shape, 0)
    step = 1
    while step < rows:
        depth = depth + jnp.where(row >= step, pltpu.roll(depth, step, 0), 0.0)
        step *= 2
    return SURFACE_LIGHT * (jnp.exp(att - depth) - jnp.exp(-depth))


def new_velocity(u, u_left, u_right, b, b_right):
    horiz = u_left + u_right - 2.0 * u
    vert = upper(u) + lower(u) - 2.0 * u
    return u + DT_OCEAN * (HORIZ_VISC * horiz + VERT_VISC * vert - PRESSURE * (b_right - b))


def diffusivity(u, b):
    rows = u.shape[0]
    row = lax.broadcasted_iota(jnp.int32, u.shape, 0)
    shear = u - lower(u)
    strat = b - lower(b)
    kappa = KAPPA_BASE + KAPPA_SPAN * (1.0 / (1.0 + jnp.exp(-4.0 * (shear * shear - strat))))
    return jnp.where(row == rows - 1, 0.0, kappa)


def face_parts(u, face_open):
    w = DT_TRACER * u * face_open
    return jnp.maximum(w, 0.0), jnp.minimum(w, 0.0)


def advect(state, adv, t, left, right, coeffs, fields, levels):
    centre, from_left, from_right = coeffs
    chunk = 16
    lane = lane_of(chunk)
    for r in range(0, levels, chunk):
        here = state[:fields, t, r : r + chunk, :]
        to_left, to_right = here, here
        if right != t:
            to_left = jnp.where(lane == 0, state[:fields, right, r : r + chunk, :], here)
        if left != t:
            to_right = jnp.where(lane == LANES - 1, state[:fields, left, r : r + chunk, :], here)
        s = slice(r, r + chunk)
        adv[:fields, t, PAD + r : PAD + r + chunk, :] = (
            here * centre[s] + lane_roll(to_left, LANES - 1) * from_right[s] + lane_roll(to_right, 1) * from_left[s]
        )


def mix_and_react(adv, t, kappa, warmth, light, kron, fields, levels, emit):
    chunk = 16
    above = jnp.where(lax.broadcasted_iota(jnp.int32, kappa.shape, 0) == 0, 0.0, pltpu.roll(kappa, 1, 0))
    stay = 1.0 - DT_MIX * (kappa + above)
    rows = (fields + (18 - fields)) * 8
    k_hi = kron[:rows, :]
    k_both = kron[...]
    for r in range(0, levels, chunk):
        s = slice(r, r + chunk)
        at = PAD + r
        here = adv[:fields, t, at : at + chunk, :]
        up = adv[:fields, t, at - 1 : at - 1 + chunk, :]
        down = adv[:fields, t, at + 1 : at + 1 + chunk, :]
        mixed = here * stay[s] + (DT_MIX * kappa[s]) * down + (DT_MIX * above[s]) * up
        halves = []
        for h in range(2):
            part = mixed[:, 8 * h : 8 * h + 8, :].reshape(fields * 8, LANES)
            if fields < 18:
                part = jnp.concatenate([part, jnp.zeros(((18 - fields) * 8, LANES), F32)], axis=0)
            halves.append(part)
        wide = jnp.concatenate(halves, axis=1)
        hi = wide.astype(BF16)
        lo = (wide - hi.astype(F32)).astype(BF16)
        by_hi = jnp.dot(k_both, hi, preferred_element_type=F32)
        by_lo = jnp.dot(k_hi, lo, preferred_element_type=F32)
        drift = by_hi[:rows] + (by_hi[rows:] + by_lo)
        out = []
        for h in range(2):
            d = drift[:, LANES * h : LANES * h + LANES].reshape(18, 8, LANES)[:fields]
            sh = slice(r + 8 * h, r + 8 * h + 8)
            new = mixed[:, 8 * h : 8 * h + 8, :] + warmth[sh] * d
            first = new[:1] + GROWTH * light[sh][None]
            out.append(jnp.concatenate([first, new[1:]], axis=0))
        emit(r, jnp.concatenate(out, axis=1))


def pack_kernel(dev, wet, kin, u, b, tracers, inner, outer):
    f = facts(dev, wet)
    levels = u.shape[0]
    half = levels // 2
    n = tracers.shape[0]
    lane = lane_of(half)
    combos = []
    for s in range(WET_DEV):
        total = None
        for j in range(n):
            term = kin[0, j] * tracers[j, :, LANES * s : LANES * (s + 1)].astype(F32)
            total = term if total is None else total + term
        combos.append(total)

    def tile_of(ref, index):
        return ref[:, pl.ds(pl.multiple_of(index * LANES, LANES), LANES)]

    def strip(slot, tile, right):
        acc = jnp.zeros((half, LANES), F32)

        def put(acc, value, at, width):
            shift = at + (width if right else 0)
            for h in range(2):
                part = value[half * h : half * (h + 1)]
                to = at + 64 * h
                here = jnp.logical_and(lane >= to, lane < to + width)
                acc = jnp.where(here, lane_roll(part, (shift + 64 * h) % LANES), acc)
            return acc

        for j in range(n):
            acc = put(acc, tracers[j, :, LANES * slot : LANES * (slot + 1)].astype(F32), 2 * j, 2)
        acc = put(acc, combos[slot], 2 * n, 2)
        at = 2 * (n + 1)
        acc = put(acc, tile_of(u, tile), at, 3)
        acc = put(acc, tile_of(b, tile), at + 3, 3)
        acc = put(acc, tracers[0, :, LANES : 2 * LANES].astype(F32), at + 6, 2)
        acc = put(acc, combos[1], at + 8, 2)
        return acc

    odd_gives = jnp.logical_and(f["is_odd"], f["gives"])
    even_gives = jnp.logical_and(jnp.logical_not(f["is_odd"]), f["gives"])
    facing_left = strip(0, jnp.where(odd_gives, 1, 0), False)
    facing_right = strip(2, jnp.where(even_gives, 2, 3), True)
    outer[...] = jnp.where(f["is_odd"], facing_right, facing_left)
    inner[:half] = jnp.where(f["is_odd"], facing_left, facing_right)
    t0 = jnp.where(f["is_odd"], tracers[0, :, :LANES].astype(F32), tracers[0, :, 2 * LANES :].astype(F32))
    tk = jnp.where(f["is_odd"], combos[0], combos[2])
    inner[half : half + levels] = jnp.where(f["gives"], tile_of(u, f["x_tile"]), t0)
    inner[half + levels :] = jnp.where(f["gives"], tile_of(b, f["x_tile"]), tk)


def expand_kinetics(kin, kron):
    n = kin.shape[0]
    rows = (n + 1) * 8
    to_rows = lax.broadcasted_iota(jnp.int32, (rows, n), 0) // 8 == lax.broadcasted_iota(jnp.int32, (rows, n), 1)
    to_cols = lax.broadcasted_iota(jnp.int32, (n, rows), 1) // 8 == lax.broadcasted_iota(jnp.int32, (n, rows), 0)
    tall = jnp.dot(to_rows.astype(F32), kin[...], precision=lax.Precision.HIGHEST, preferred_element_type=F32)
    full = jnp.dot(tall, to_cols.astype(F32), precision=lax.Precision.HIGHEST, preferred_element_type=F32)
    row = lax.broadcasted_iota(jnp.int32, (rows, rows), 0)
    col = lax.broadcasted_iota(jnp.int32, (rows, rows), 1)
    full = jnp.where(lax.rem(row, 8) == lax.rem(col, 8), full, 0.0)
    with_combo = jnp.where(row < 8, jnp.where(col - 8 * n == row, 1.0, 0.0), full)
    for i, m in enumerate((with_combo, full)):
        hi = m.astype(BF16)
        kron[i, :rows, :] = hi
        kron[i, rows:, :] = (m - hi.astype(F32)).astype(BF16)


def own_kernel(dev, wet, kin, u0, b0, tracers, u_out, b_out, t_out, kron, u, b, state, adv):
    f = facts(dev, wet)
    levels = u0.shape[0]
    n = tracers.shape[0]
    lane = lane_of(levels)
    expand_kinetics(kin, kron)
    takes = jnp.logical_not(f["gives"])
    is_x = [jnp.logical_and(takes, f["x_slot"] == s) for s in range(WET_DEV)]
    tile = [jnp.clip(f["w"][s] - f["base"], 0, OCEAN_DEV - 1) for s in range(WET_DEV)]
    joined = []
    for s in range(WET_DEV - 1):
        apart = jnp.logical_or(is_x[s], is_x[s + 1])
        joined.append(jnp.logical_and(f["w"][s + 1] - f["w"][s] == 1, jnp.logical_not(apart)))
    joined.append(jnp.zeros((), jnp.bool_))
    for t in range(OCEAN_DEV):
        u[t] = u0[:, LANES * t : LANES * (t + 1)]
        b[t] = b0[:, LANES * t : LANES * (t + 1)]
    for s in range(WET_DEV):
        state[:, s] = tracers[:, :, LANES * s : LANES * (s + 1)].astype(F32)
        for row in (0, PAD + levels):
            adv[:, s, row : row + 8, :] = jnp.zeros((n, 8, LANES), F32)
    for step in range(STEPS):
        last = step == STEPS - 1
        light = []
        for s in range(WET_DEV):
            light.append(absorbed_light(state[0, s]))
            b[tile[s]] = b[tile[s]] + jnp.where(is_x[s], 0.0, HEATING) * light[s]
        us = [u[t] for t in range(OCEAN_DEV)]
        bs = [b[t] for t in range(OCEAN_DEV)]
        for t in range(OCEAN_DEV):
            nxt, prv = (t + 1) % OCEAN_DEV, (t - 1) % OCEAN_DEV
            u_right = lane_roll(jnp.where(lane == 0, us[nxt], us[t]), LANES - 1)
            u_left = lane_roll(jnp.where(lane == LANES - 1, us[prv], us[t]), 1)
            b_right = lane_roll(jnp.where(lane == 0, bs[nxt], bs[t]), LANES - 1)
            u[t] = new_velocity(us[t], u_left, u_right, bs[t], b_right)
            if last:
                u_out[:, LANES * t : LANES * (t + 1)] = u[t]
                b_out[:, LANES * t : LANES * (t + 1)] = bs[t]
        parts = []
        for s in range(WET_DEV):
            shut = jnp.logical_and(lane == LANES - 1, jnp.logical_not(joined[s]))
            parts.append(face_parts(u[tile[s]], jnp.where(shut, 0.0, 1.0)))
        for s in range(WET_DEV):
            pos, neg = parts[s]
            before = parts[s - 1] if s else (jnp.zeros_like(pos), jnp.zeros_like(neg))
            pos_left = lane_roll(jnp.where(lane == LANES - 1, before[0], pos), 1)
            neg_left = lane_roll(jnp.where(lane == LANES - 1, before[1], neg), 1)
            coeffs = (1.0 - pos + neg_left, pos_left, -neg)
            advect(state, adv, s, max(s - 1, 0), min(s + 1, WET_DEV - 1), coeffs, n, levels)
        for s in range(WET_DEV):
            ub, bb = u[tile[s]], b[tile[s]]
            kappa = diffusivity(ub, bb)
            warmth = KINETIC_DELTA * jnp.exp(THERMAL_GAIN * bb)

            def emit(r, values, s=s):
                if last:
                    t_out[:, r : r + 16, LANES * s : LANES * (s + 1)] = values.astype(BF16)
                else:
                    state[:, s, r : r + 16, :] = values

            mix_and_react(adv, s, kappa, warmth, light[s], kron.at[1], n, levels, emit)


def edge_kernel(
    dev, wet, kin, kron, u0, b0, tracers, inner, outer, u_in, b_in, t_in, u_out, b_out, t_out, u, b, state, adv
):
    f = facts(dev, wet)
    levels = u0.shape[0]
    half = levels // 2
    n = tracers.shape[0]
    fields = n + 1
    lane = lane_of(levels)
    gives, is_odd = f["gives"], f["is_odd"]
    X, PATCH = 0, 1

    def tile_of(ref, index):
        return ref[:, pl.ds(pl.multiple_of(index * LANES, LANES), LANES)]

    def slot_of(j, index):
        return tracers[j, :, pl.ds(pl.multiple_of(index * LANES, LANES), LANES)].astype(F32)

    def combo_of(index):
        total = None
        for j in range(n):
            term = kin[0, j] * slot_of(j, index)
            total = term if total is None else total + term
        return total

    def from_strip(ref, at, width, to_right_half):
        shift = jnp.where(to_right_half, 0, width)
        parts = []
        for h in range(2):
            amount = lax.rem(2 * LANES - at - 64 * h - shift, LANES)
            parts.append(lane_roll(ref[:half], amount))
        return jnp.concatenate(parts, axis=0)

    from_outer = functools.partial(from_strip, outer, to_right_half=is_odd)
    from_inner = functools.partial(from_strip, inner, to_right_half=jnp.logical_not(is_odd))
    in_right = jnp.where(is_odd, LANES - 1 - lane, lane) < LANES // 2
    in_1 = jnp.logical_and(lane >= HALF, lane < HALF + SEG)
    in_2 = jnp.logical_and(lane >= HALF + SEG, lane < HALF + 2 * SEG)

    def patch_of(own, far, beside, x_side, x, beyond):
        seg0 = jnp.where(in_right, own, far)
        seg1 = jnp.where(in_right, x_side, beside)
        seg2 = jnp.where(in_right, beyond, x)
        return jnp.where(in_1, lane_roll(seg1, SEG), jnp.where(in_2, lane_roll(seg2, 2 * SEG), seg0))

    tile1 = inner[half : half + levels]
    tile2 = inner[half + levels :]
    at = 2 * fields
    x_u = jnp.where(gives, tile_of(u0, f["x_tile"]), tile1)
    x_b = jnp.where(gives, tile_of(b0, f["x_tile"]), tile2)
    u[X] = x_u
    b[X] = x_b
    u[PATCH] = patch_of(
        tile_of(u0, f["outer_tile"]),
        from_outer(at, 3),
        tile_of(u0, f["beside_tile"]),
        x_u,
        x_u,
        from_inner(at, 3),
    )
    b[PATCH] = patch_of(
        tile_of(b0, f["outer_tile"]),
        from_outer(at + 3, 3),
        tile_of(b0, f["beside_tile"]),
        x_b,
        x_b,
        from_inner(at + 3, 3),
    )
    for j in range(fields):
        load = (lambda index, j=j: slot_of(j, index)) if j < n else combo_of
        x = load(f["x_slot"])
        own = load(f["outer_slot"])
        beside = load(f["beside_slot"])
        strip = from_inner(2 * j, 2)
        x_side = jnp.where(gives, strip, x)
        beyond = strip
        if j in (0, n):
            x = x_side = jnp.where(gives, tile1 if j == 0 else tile2, x)
            beyond = jnp.where(gives, from_inner(at + (6 if j == 0 else 8), 2), strip)
        state[j, X] = x
        state[j, PATCH] = patch_of(own, from_outer(2 * j, 2), beside, x_side, x, beyond)
    for t in range(2):
        for row in (0, PAD + levels):
            adv[:, t, row : row + 8, :] = jnp.zeros((fields, 8, LANES), F32)

    def flag(x):
        return jnp.where(x, 1.0, 0.0) * jnp.ones((levels, LANES), F32)

    one = jnp.ones((levels, LANES), F32)
    wet_here = patch_of(
        flag(f["outer_own_wet"]), flag(f["outer_far_wet"]), flag(f["beside_wet"]), one, one, flag(f["beyond_wet"])
    )
    open_0 = jnp.logical_and(f["outer_own_wet"], f["outer_far_wet"])
    patch_open = jnp.where(
        lane == LANES - 1,
        flag(open_0),
        jnp.where(
            lane == SEG - 1,
            flag(f["beside_wet"]),
            jnp.where(lane == 2 * SEG - 1, flag(f["beyond_wet"]), 1.0),
        ),
    )
    x_open = jnp.where(lane == LANES - 1, 0.0, 1.0)
    heat = (one, wet_here)
    opens = (x_open, patch_open)
    results = [[None] * 2, [None] * 2]
    for step in range(STEPS):
        last = step == STEPS - 1
        light = []
        for t in range(2):
            light.append(absorbed_light(state[0, t]))
            bb = b[t] + HEATING * heat[t] * light[t]
            b[t] = bb
            uu = u[t]
            uu = new_velocity(uu, lane_roll(uu, 1), lane_roll(uu, LANES - 1), bb, lane_roll(bb, LANES - 1))
            u[t] = uu
        count = n if last else fields
        for t in range(2):
            pos, neg = face_parts(u[t], opens[t])
            pos_left, neg_left = lane_roll(pos, 1), lane_roll(neg, 1)
            advect(state, adv, t, t, t, (1.0 - pos + neg_left, pos_left, -neg), count, levels)
        for t in range(2):
            kappa = diffusivity(u[t], b[t])
            warmth = KINETIC_DELTA * jnp.exp(THERMAL_GAIN * b[t])

            def emit(r, values, t=t):
                state[:n, t, r : r + 16, :] = values[:n]

            mix_and_react(adv, t, kappa, warmth, light[t], kron.at[step], count, levels, emit)

    def fix_mask(rows, at_left):
        here = lane_of(rows)
        return jnp.where(at_left, here, LANES - 1 - here) < FIX

    not_odd = jnp.logical_not(is_odd)

    def ocean_fix(final, incoming, out, scratch):
        out[...] = incoming[...]
        patch = scratch[PATCH]
        seg1 = lane_roll(patch, LANES - SEG)
        seg2 = lane_roll(patch, LANES - 2 * SEG)

        def put(index, value):
            out[:, pl.ds(pl.multiple_of(index * LANES, LANES), LANES)] = value

        put(f["outer_tile"], jnp.where(fix_mask(levels, not_odd), patch, tile_of(incoming, f["outer_tile"])))
        put(f["beside_tile"], jnp.where(fix_mask(levels, is_odd), seg1, tile_of(incoming, f["beside_tile"])))
        x = jnp.where(fix_mask(levels, not_odd), seg1, jnp.where(fix_mask(levels, is_odd), seg2, scratch[X]))

        @pl.when(gives)
        def _():
            put(f["x_tile"], x)

    ocean_fix(None, u_in, u_out, u)
    ocean_fix(None, b_in, b_out, b)

    rows = 16
    t_out[...] = t_in[...]
    takes = jnp.logical_not(gives)
    outer_fix = jnp.logical_and(fix_mask(rows, not_odd), f["outer_own_wet"])
    beside_fix = jnp.logical_and(fix_mask(rows, is_odd), f["beside_wet"])
    near_fix, far_fix = fix_mask(rows, not_odd), fix_mask(rows, is_odd)

    def slot_at(index):
        return pl.ds(pl.multiple_of(index * LANES, LANES), LANES)

    for r in range(0, levels, rows):
        s = slice(r, r + rows)
        patch = state[:n, PATCH, s, :]
        seg1 = lane_roll(patch, LANES - SEG)
        where = slot_at(f["outer_slot"])
        t_out[:, s, where] = jnp.where(outer_fix, patch, t_in[:, s, where].astype(F32)).astype(BF16)
        where = slot_at(f["beside_slot"])
        t_out[:, s, where] = jnp.where(beside_fix, seg1, t_in[:, s, where].astype(F32)).astype(BF16)

    @pl.when(takes)
    def _():
        for r in range(0, levels, rows):
            s = slice(r, r + rows)
            patch = state[:n, PATCH, s, :]
            seg1 = lane_roll(patch, LANES - SEG)
            seg2 = lane_roll(patch, LANES - 2 * SEG)
            x = jnp.where(near_fix, seg1, jnp.where(far_fix, seg2, state[:n, X, s, :]))
            t_out[:, s, slot_at(f["x_slot"])] = x.astype(BF16)


def call(kernel, outs, scratch, args, spaces, aliases=None, flops=0, name=None):
    where = {"s": pltpu.SMEM, "v": pltpu.VMEM}
    return pl.pallas_call(
        kernel,
        out_shape=tuple(jax.ShapeDtypeStruct(s, d) for s, d in outs),
        in_specs=[pl.BlockSpec(memory_space=where[c]) for c in spaces],
        out_specs=tuple(pl.BlockSpec(memory_space=pltpu.VMEM) for _ in outs),
        scratch_shapes=[pltpu.VMEM(s, F32) for s in scratch],
        input_output_aliases=aliases or {},
        compiler_params=pltpu.CompilerParams(vmem_limit_bytes=48 * 2**20),
        cost_estimate=pl.CostEstimate(flops=flops, bytes_accessed=4_000_000, transcendentals=0),
        name=name,
    )(*args)


def on_device(ocean_u, ocean_b, tracers, wet_tiles, kinetic):
    axes = ("sec", "tile")
    devices = lax.axis_size("sec") * lax.axis_size("tile")
    levels, n = ocean_u.shape[0], tracers.shape[0]
    dev = (lax.axis_index("sec") * lax.axis_size("tile") + lax.axis_index("tile")).astype(jnp.int32).reshape(1)
    strip = levels // 2
    inner, outer = call(
        pack_kernel,
        [((strip + 2 * levels, LANES), F32), ((strip, LANES), F32)],
        [],
        (dev, wet_tiles, kinetic, ocean_u, ocean_b, tracers),
        "sssvvv",
        flops=10_000_000,
        name="pack",
    )
    in_pairs = [(i, i ^ 1) for i in range(devices)]
    across = [(i, (i + 1) % devices if i % 2 else (i - 1) % devices) for i in range(devices)]
    inner = lax.ppermute(inner, axes, in_pairs)
    outer = lax.ppermute(outer, axes, across)
    fields = n + 1
    u, b, t, kron = call(
        own_kernel,
        [
            (ocean_u.shape, F32),
            (ocean_b.shape, F32),
            (tracers.shape, BF16),
            ((2, 2 * fields * 8, fields * 8), BF16),
        ],
        [
            (OCEAN_DEV, levels, LANES),
            (OCEAN_DEV, levels, LANES),
            (n, WET_DEV, levels, LANES),
            (n, WET_DEV, levels + 2 * PAD, LANES),
        ],
        (dev, wet_tiles, kinetic, ocean_u, ocean_b, tracers),
        "ssvvvv",
        flops=2_000_000_000,
        name="own_tiles",
    )
    return tuple(
        call(
            edge_kernel,
            [(ocean_u.shape, F32), (ocean_b.shape, F32), (tracers.shape, BF16)],
            [
                (2, levels, LANES),
                (2, levels, LANES),
                (fields, 2, levels, LANES),
                (fields, 2, levels + 2 * PAD, LANES),
            ],
            (dev, wet_tiles, kinetic, kron, ocean_u, ocean_b, tracers, inner, outer, u, b, t),
            "sss" + "v" * 9,
            flops=1_000_000_000,
            name="edges",
        )
    )


def solution(mesh):
    spread = P(None, ("sec", "tile"))
    tracer_spread = P(None, None, ("sec", "tile"))

    def program(ocean_u, ocean_b, tracers, wet_tiles, kinetic_matrix):
        u, b, t = jax.shard_map(
            on_device,
            mesh=mesh,
            in_specs=(spread, spread, tracer_spread, P(), P()),
            out_specs=(spread, spread, tracer_spread),
            check_vma=False,
        )(ocean_u, ocean_b, tracers, wet_tiles, kinetic_matrix)
        return t, u, b

    return program
```

```python
import functools

import jax
import jax.numpy as jnp
from jax import lax
from jax.experimental import pallas as pl
from jax.experimental.pallas import tpu as pltpu
from jax.sharding import PartitionSpec as P

LANES = 128
STEPS = 2
WET_DEV = 3
OCEAN_DEV = 4

DT_OCEAN = 0.25
PRESSURE = 1.0
HORIZ_VISC = 0.2
VERT_VISC = 0.2
HEATING = 0.2
KAPPA_BASE = 0.05
KAPPA_SPAN = 0.35
DT_TRACER = 0.3
DT_MIX = 1.0
KINETIC_DELTA = 0.5
SURFACE_LIGHT = 10.0
WATER_ATT = 0.04
PIGMENT_ATT = 0.08
GROWTH = 0.05
THERMAL_GAIN = 0.1

SEG = 40
HALF = SEG // 2
FIX = 8
PAD = 8
F32, BF16 = jnp.float32, jnp.bfloat16


FACTS = (
    "odd",
    "gives",
    "x_slot",
    "x_tile",
    "outer_slot",
    "outer_tile",
    "beside_slot",
    "beside_tile",
    "outer_own_wet",
    "outer_far_wet",
    "beside_wet",
    "beyond_wet",
    "tile0",
    "tile1",
    "tile2",
    "joined0",
    "joined1",
)


def find_facts(dev_ref, wet_ref, out_ref):
    k = dev_ref[0]
    odd = lax.rem(k, 2)
    first, base = WET_DEV * k, OCEAN_DEV * k
    listed = wet_ref.shape[0]
    tiles = listed // WET_DEV * OCEAN_DEV
    is_odd = odd == 1
    w = [wet_ref[first + s] for s in range(WET_DEV)]
    probe = wet_ref[first + jnp.where(is_odd, -1, 3)]
    gives = jnp.logical_and(probe >= base, probe < base + OCEAN_DEV)
    before = jnp.where(k == 0, listed - 1, first - 1)
    after = jnp.where(first + WET_DEV == listed, 0, first + WET_DEV)
    outer_far = jnp.where(
        is_odd,
        jnp.where(base + OCEAN_DEV == tiles, 0, base + OCEAN_DEV),
        jnp.where(k == 0, tiles - 1, base - 1),
    )
    far_listed = wet_ref[first + jnp.where(is_odd, -2, 4)] == base + jnp.where(is_odd, -1, 4)
    f = {"odd": odd, "gives": gives, "x_slot": 2 - 2 * odd, "x_tile": 3 - 3 * odd}
    f["outer_slot"], f["outer_tile"] = 2 * odd, 3 * odd
    f["beside_slot"] = jnp.where(gives, 2 - 2 * odd, 1)
    f["beside_tile"] = jnp.where(gives, 2 - odd, 3 - 3 * odd)
    f["outer_own_wet"] = jnp.where(is_odd, w[2] == base + 3, w[0] == base)
    f["outer_far_wet"] = wet_ref[jnp.where(is_odd, after, before)] == outer_far
    f["beside_wet"] = jnp.logical_or(gives, w[1] == base + 3 - 3 * odd)
    f["beyond_wet"] = jnp.logical_or(jnp.logical_not(gives), far_listed)
    for s in range(WET_DEV):
        f[f"tile{s}"] = jnp.clip(w[s] - base, 0, OCEAN_DEV - 1)
    for s in range(WET_DEV - 1):
        x_here = jnp.logical_or(f["x_slot"] == s, f["x_slot"] == s + 1)
        f[f"joined{s}"] = jnp.logical_and(w[s + 1] - w[s] == 1, jnp.logical_or(gives, jnp.logical_not(x_here)))
    for i, name in enumerate(FACTS):
        out_ref[i] = f[name].astype(jnp.int32)


def read_facts(ref):
    return {name: ref[i] for i, name in enumerate(FACTS)}


def lane_of(rows):
    return lax.broadcasted_iota(jnp.int32, (rows, LANES), 1)


def lane_roll(x, shift):
    return pltpu.roll(x, shift, x.ndim - 1)


def upper(x):
    row = lax.broadcasted_iota(jnp.int32, x.shape, 0)
    return jnp.where(row == 0, x, pltpu.roll(x, 1, 0))


def lower(x):
    n = x.shape[0]
    row = lax.broadcasted_iota(jnp.int32, x.shape, 0)
    return jnp.where(row == n - 1, x, pltpu.roll(x, n - 1, 0))


def absorbed_light(pigment):
    att = WATER_ATT + PIGMENT_ATT * pigment * pigment
    depth = att
    rows = att.shape[0]
    row = lax.broadcasted_iota(jnp.int32, att.shape, 0)
    step = 1
    while step < rows:
        depth = depth + jnp.where(row >= step, pltpu.roll(depth, step, 0), 0.0)
        step *= 2
    return SURFACE_LIGHT * (jnp.exp(att - depth) - jnp.exp(-depth))


def new_velocity(u, u_left, u_right, b, b_right):
    horiz = u_left + u_right - 2.0 * u
    vert = upper(u) + lower(u) - 2.0 * u
    return u + DT_OCEAN * (HORIZ_VISC * horiz + VERT_VISC * vert - PRESSURE * (b_right - b))


def diffusivity(u, b):
    rows = u.shape[0]
    row = lax.broadcasted_iota(jnp.int32, u.shape, 0)
    shear = u - lower(u)
    strat = b - lower(b)
    kappa = KAPPA_BASE + KAPPA_SPAN * (1.0 / (1.0 + jnp.exp(-4.0 * (shear * shear - strat))))
    return jnp.where(row == rows - 1, 0.0, kappa)


def face_parts(u, face_open):
    w = DT_TRACER * u * face_open
    return jnp.maximum(w, 0.0), jnp.minimum(w, 0.0)


def advect(state, adv, t, left, right, coeffs, fields, levels):
    centre, from_left, from_right = coeffs
    chunk = 16
    lane = lane_of(chunk)
    for r in range(0, levels, chunk):
        here = state[:fields, t, r : r + chunk, :]
        to_left, to_right = here, here
        if right != t:
            to_left = jnp.where(lane == 0, state[:fields, right, r : r + chunk, :], here)
        if left != t:
            to_right = jnp.where(lane == LANES - 1, state[:fields, left, r : r + chunk, :], here)
        s = slice(r, r + chunk)
        adv[:fields, t, PAD + r : PAD + r + chunk, :] = (
            here * centre[s] + lane_roll(to_left, LANES - 1) * from_right[s] + lane_roll(to_right, 1) * from_left[s]
        )


def mix_and_react(adv, t, kappa, warmth, light, kron, fields, levels, emit):
    chunk = 16
    above = jnp.where(lax.broadcasted_iota(jnp.int32, kappa.shape, 0) == 0, 0.0, pltpu.roll(kappa, 1, 0))
    stay = 1.0 - DT_MIX * (kappa + above)
    rows = (fields + (18 - fields)) * 8
    k_hi = kron[:rows, :]
    k_both = kron[...]
    for r in range(0, levels, chunk):
        s = slice(r, r + chunk)
        at = PAD + r
        here = adv[:fields, t, at : at + chunk, :]
        up = adv[:fields, t, at - 1 : at - 1 + chunk, :]
        down = adv[:fields, t, at + 1 : at + 1 + chunk, :]
        mixed = here * stay[s] + (DT_MIX * kappa[s]) * down + (DT_MIX * above[s]) * up
        halves = []
        for h in range(2):
            part = mixed[:, 8 * h : 8 * h + 8, :].reshape(fields * 8, LANES)
            if fields < 18:
                part = jnp.concatenate([part, jnp.zeros(((18 - fields) * 8, LANES), F32)], axis=0)
            halves.append(part)
        wide = jnp.concatenate(halves, axis=1)
        hi = wide.astype(BF16)
        lo = (wide - hi.astype(F32)).astype(BF16)
        by_hi = jnp.dot(k_both, hi, preferred_element_type=F32)
        by_lo = jnp.dot(k_hi, lo, preferred_element_type=F32)
        drift = by_hi[:rows] + (by_hi[rows:] + by_lo)
        out = []
        for h in range(2):
            d = drift[:, LANES * h : LANES * h + LANES].reshape(18, 8, LANES)[:fields]
            sh = slice(r + 8 * h, r + 8 * h + 8)
            new = mixed[:, 8 * h : 8 * h + 8, :] + warmth[sh] * d
            first = new[:1] + GROWTH * light[sh][None]
            out.append(jnp.concatenate([first, new[1:]], axis=0))
        emit(r, jnp.concatenate(out, axis=1))


def tile_of(ref, index):
    return ref[:, pl.ds(pl.multiple_of(index * LANES, LANES), LANES)]


def slot_of(ref, j, index):
    return ref[j, :, pl.ds(pl.multiple_of(index * LANES, LANES), LANES)].astype(F32)


U_AT, B_AT, T0_AT, COMBO_AT, WIDE = 40, 44, 48, 50, 3


def pack_kernel(dev, wet_hbm, kin_hbm, u_hbm, b_hbm, t_hbm, inner, outer, u, b, tracers, kin_v, found, wet, kin, sems):
    pairs = ((wet_hbm, wet), (kin_hbm, kin), (t_hbm, tracers), (u_hbm, u), (b_hbm, b), (kin_hbm, kin_v))
    copies = [pltpu.make_async_copy(src, dst, sems.at[i]) for i, (src, dst) in enumerate(pairs)]
    for c in copies:
        c.start()
    for c in copies:
        c.wait()
    find_facts(dev, wet, found)
    f = read_facts(found)
    levels = u.shape[0]
    half = levels // 2
    n = tracers.shape[0]
    lane = lane_of(half)

    def combo_of(index):
        total = None
        for j in range(n):
            term = kin[0, j] * slot_of(tracers, j, index)
            total = term if total is None else total + term
        return total

    def put(acc, value, at, width, right):
        for h in range(2):
            to = at + 64 * h
            here = jnp.bitwise_and(lane + right * width - to, LANES - 1) < width
            acc = jnp.where(here, lane_roll(value[half * h : half * (h + 1)], to), acc)
        return acc

    def strip(slot, tile, combo, right):
        acc = jnp.zeros((half, LANES), F32)
        for j in range(n):
            acc = put(acc, slot_of(tracers, j, slot), 2 * j, 2, right)
        acc = put(acc, combo, 2 * n, 2, right)
        acc = put(acc, tile_of(u, tile), U_AT, WIDE, right)
        return put(acc, tile_of(b, tile), B_AT, WIDE, right)

    outer[...] = strip(f["outer_slot"], f["outer_tile"], combo_of(f["outer_slot"]), f["odd"])
    x_combo = combo_of(f["x_slot"])
    acc = strip(f["x_slot"], f["beside_tile"], x_combo, 1 - f["odd"])
    acc = put(acc, slot_of(tracers, 0, 1), T0_AT, 2, 1 - f["odd"])
    inner[:half] = put(acc, combo_of(1), COMBO_AT, 2, 1 - f["odd"])
    gives = f["gives"] == 1
    inner[half : half + levels] = jnp.where(gives, tile_of(u, f["x_tile"]), slot_of(tracers, 0, f["x_slot"]))
    inner[half + levels :] = jnp.where(gives, tile_of(b, f["x_tile"]), x_combo)


def patch_masks(f, rows):
    lane = lane_of(rows)
    near = jnp.where(f["odd"] == 1, LANES - 1 - lane, lane) < LANES // 2
    in_1 = jnp.logical_and(lane >= HALF, lane < HALF + SEG)
    in_2 = jnp.logical_and(lane >= HALF + SEG, lane < HALF + 2 * SEG)
    return near, in_1, in_2


def expand_kinetics(kin, kron):
    n = kin.shape[0]
    rows = (n + 1) * 8
    to_rows = lax.broadcasted_iota(jnp.int32, (rows, n), 0) // 8 == lax.broadcasted_iota(jnp.int32, (rows, n), 1)
    to_cols = lax.broadcasted_iota(jnp.int32, (n, rows), 1) // 8 == lax.broadcasted_iota(jnp.int32, (n, rows), 0)
    tall = jnp.dot(to_rows.astype(F32), kin[...], precision=lax.Precision.HIGHEST, preferred_element_type=F32)
    full = jnp.dot(tall, to_cols.astype(F32), precision=lax.Precision.HIGHEST, preferred_element_type=F32)
    row = lax.broadcasted_iota(jnp.int32, (rows, rows), 0)
    col = lax.broadcasted_iota(jnp.int32, (rows, rows), 1)
    full = jnp.where(lax.rem(row, 8) == lax.rem(col, 8), full, 0.0)
    with_combo = jnp.where(row < 8, jnp.where(col - 8 * n == row, 1.0, 0.0), full)
    for i, m in enumerate((with_combo, full)):
        hi = m.astype(BF16)
        kron[i, :rows, :] = hi
        kron[i, rows:, :] = (m - hi.astype(F32)).astype(BF16)


def start_tile(state, adv, t, fields, levels):
    for row in (0, PAD + levels):
        adv[:, t, row : row + 8, :] = jnp.zeros((fields, 8, LANES), F32)


def own_kernel(
    facts, kin, u0, b0, tracers, u_out, b_out, t_out, kron, p_state, p_u, p_b, u, b, state, adv
):
    f = read_facts(facts)
    levels = u0.shape[0]
    n = tracers.shape[0]
    lane = lane_of(levels)
    expand_kinetics(kin, kron)
    gives = f["gives"] == 1
    is_x = [jnp.logical_and(f["gives"] == 0, f["x_slot"] == s) for s in range(WET_DEV)]
    tile = [f[f"tile{s}"] for s in range(WET_DEV)]
    joined = [f["joined0"] == 1, f["joined1"] == 1, None]
    for t in range(OCEAN_DEV):
        u[t] = u0[:, LANES * t : LANES * (t + 1)]
        b[t] = b0[:, LANES * t : LANES * (t + 1)]
    for s in range(WET_DEV):
        state[:, s] = tracers[:, :, LANES * s : LANES * (s + 1)].astype(F32)
        start_tile(state, adv, s, n, levels)

    near, in_1, in_2 = patch_masks(f, levels)

    def lay(own, beside, x):
        seg1 = lane_roll(jnp.where(near, x, beside), SEG)
        return jnp.where(in_1, seg1, jnp.where(in_2, lane_roll(x, 2 * SEG), own))

    for p, field in ((p_u, u), (p_b, b)):
        p[...] = lay(field[f["outer_tile"]], field[f["beside_tile"]], field[f["x_tile"]])
    combos = [None] * 3
    for j in range(n):
        tiles = [state[j, f[name]] for name in ("outer_slot", "beside_slot", "x_slot")]
        p_state[j] = lay(*tiles)
        combos = [
            kin[0:1, j : j + 1] * x if c is None else c + kin[0:1, j : j + 1] * x for c, x in zip(combos, tiles)
        ]
    p_state[n] = lay(*combos)

    for step in range(STEPS):
        last = step == STEPS - 1
        light = []
        for s in range(WET_DEV):
            light.append(absorbed_light(state[0, s]))
            b[tile[s]] = b[tile[s]] + jnp.where(is_x[s], 0.0, HEATING) * light[s]
        us = [u[t] for t in range(OCEAN_DEV)]
        bs = [b[t] for t in range(OCEAN_DEV)]
        for t in range(OCEAN_DEV):
            nxt, prv = (t + 1) % OCEAN_DEV, (t - 1) % OCEAN_DEV
            u_right = lane_roll(jnp.where(lane == 0, us[nxt], us[t]), LANES - 1)
            u_left = lane_roll(jnp.where(lane == LANES - 1, us[prv], us[t]), 1)
            b_right = lane_roll(jnp.where(lane == 0, bs[nxt], bs[t]), LANES - 1)
            u[t] = new_velocity(us[t], u_left, u_right, bs[t], b_right)
            if last:
                u_out[t] = u[t]
                b_out[t] = bs[t]
        parts = []
        for s in range(WET_DEV):
            shut = lane == LANES - 1
            if joined[s] is not None:
                shut = jnp.logical_and(shut, jnp.logical_not(joined[s]))
            parts.append(face_parts(u[tile[s]], jnp.where(shut, 0.0, 1.0)))
        for s in range(WET_DEV):
            pos, neg = parts[s]
            before = parts[s - 1] if s else (jnp.zeros_like(pos), jnp.zeros_like(neg))
            pos_left = lane_roll(jnp.where(lane == LANES - 1, before[0], pos), 1)
            neg_left = lane_roll(jnp.where(lane == LANES - 1, before[1], neg), 1)
            coeffs = (1.0 - pos + neg_left, pos_left, -neg)
            advect(state, adv, s, max(s - 1, 0), min(s + 1, WET_DEV - 1), coeffs, n, levels)
        for s in range(WET_DEV):
            ub, bb = u[tile[s]], b[tile[s]]
            kappa = diffusivity(ub, bb)
            warmth = KINETIC_DELTA * jnp.exp(THERMAL_GAIN * bb)

            def emit(r, values, s=s):
                if last:
                    t_out[:, s, r : r + 16, :] = values.astype(BF16)
                else:
                    state[:, s, r : r + 16, :] = values

            mix_and_react(adv, s, kappa, warmth, light[s], kron.at[1], n, levels, emit)


def advance_alone(state, adv, u, b, heat, face_open, kron, n, levels, emit):
    for step in range(STEPS):
        last = step == STEPS - 1
        light = absorbed_light(state[0, 0])
        b = b + HEATING * heat * light
        u = new_velocity(u, lane_roll(u, 1), lane_roll(u, LANES - 1), b, lane_roll(b, LANES - 1))
        if last:
            emit(None, (u, b))
        count = n if last else n + 1
        pos, neg = face_parts(u, face_open)
        pos_left, neg_left = lane_roll(pos, 1), lane_roll(neg, 1)
        advect(state, adv, 0, 0, 0, (1.0 - pos + neg_left, pos_left, -neg), count, levels)
        kappa = diffusivity(u, b)
        warmth = KINETIC_DELTA * jnp.exp(THERMAL_GAIN * b)

        def put(r, values):
            state[:n, 0, r : r + 16, :] = values[:n]

        mix_and_react(adv, 0, kappa, warmth, light, kron.at[step], count, levels, emit if last else put)


def from_strip(ref, half, shift):
    return jnp.concatenate(
        [lane_roll(ref[:half], lax.rem(shift + 3 * LANES - 64 * h, LANES)) for h in range(2)], axis=0
    )


def x_kernel(
    facts, kin, kron, u0, b0, tracers, inner, pre_state, pre_u, pre_b, x_t, x_u, x_b, p_state, p_u, p_b, state, adv
):
    f = read_facts(facts)
    levels = u0.shape[0]
    half = levels // 2
    n = tracers.shape[0]
    gives = f["gives"] == 1
    lane = lane_of(levels)
    tile1 = inner[half : half + levels]
    tile2 = inner[half + levels :]
    u = jnp.where(gives, tile_of(u0, f["x_tile"]), tile1)
    b = jnp.where(gives, tile_of(b0, f["x_tile"]), tile2)
    start_tile(state, adv, 0, n + 1, levels)

    near, in_1, in_2 = patch_masks(f, levels)
    x_in_1 = jnp.logical_and(in_1, pltpu.roll(jnp.where(near, 1, 0), SEG, 1) == 1)
    beyond = jnp.logical_and(in_2, pltpu.roll(jnp.where(near, 1, 0), 2 * SEG, 1) == 1)
    strip_goes = jnp.where(gives, jnp.where(x_in_1, 1, 0), jnp.where(beyond, 1, 0)) == 1
    strip_seg = jnp.where(gives, SEG, 2 * SEG)

    def x_whole(patch, x):
        patch = jnp.where(x_in_1, lane_roll(x, SEG), patch)
        return jnp.where(in_2, lane_roll(x, 2 * SEG), patch)

    for p, pre, x, at in ((p_u, pre_u, u, U_AT), (p_b, pre_b, b, B_AT)):
        p[...] = jnp.where(beyond, from_strip(inner, half, 2 * SEG - at), x_whole(pre[...], x))
    for j in range(n):
        x = slot_of(tracers, j, f["x_slot"])
        patch = jnp.where(strip_goes, from_strip(inner, half, strip_seg - 2 * j), pre_state[j])
        if j == 0:
            x = jnp.where(gives, tile1, x)
            far = from_strip(inner, half, 2 * SEG - jnp.where(gives, T0_AT, 0))
            patch = jnp.where(beyond, far, x_whole(pre_state[j], x))
        p_state[j] = patch
        state[j, 0] = x
    far = from_strip(inner, half, 2 * SEG - jnp.where(gives, COMBO_AT, 2 * n))
    total = None
    for j in range(n):
        term = kin[0:1, j : j + 1] * slot_of(tracers, j, f["x_slot"])
        total = term if total is None else total + term
    combo = jnp.where(gives, tile2, total)
    state[n, 0] = combo
    p_state[n] = jnp.where(beyond, far, x_whole(pre_state[n], combo))

    def emit(r, values):
        if r is None:
            x_u[...], x_b[...] = values
        else:
            x_t[:, r : r + 16, :] = values

    face_open = jnp.where(lane == LANES - 1, 0.0, 1.0)
    advance_alone(state, adv, u, b, 1.0, face_open, kron, n, levels, emit)


def last_kernel(
    facts, kron, outer, pre_state, p_u, p_b, own_u, own_b, own_t, x_u, x_b, x_t,
    u_out, b_out, t_out, state, adv, whole_u, whole_b, merged, sems,
):
    f = read_facts(facts)
    levels = p_u.shape[0]
    half = levels // 2
    n = own_t.shape[0]
    gives, odd = f["gives"] == 1, f["odd"] == 1
    lane = lane_of(levels)
    near, in_1, in_2 = patch_masks(f, levels)
    halo = jnp.logical_not(jnp.logical_or(near, jnp.logical_or(in_1, in_2)))
    start_tile(state, adv, 0, n + 1, levels)
    u = jnp.where(halo, from_strip(outer, half, -U_AT), p_u[...])
    b = jnp.where(halo, from_strip(outer, half, -B_AT), p_b[...])
    for j in range(n + 1):
        state[j, 0] = jnp.where(halo, from_strip(outer, half, -2 * j), pre_state[j])

    def sides(here, there, boundary_at):
        return lane_roll(jnp.where(near, here.astype(F32), there.astype(F32)), boundary_at)

    one = jnp.int32(1)
    heat = jnp.where(
        in_1,
        sides(one, f["beside_wet"], SEG),
        jnp.where(in_2, sides(f["beyond_wet"], one, 2 * SEG), sides(f["outer_own_wet"], f["outer_far_wet"], 0)),
    )
    outer_open = (f["outer_own_wet"] * f["outer_far_wet"]).astype(F32)
    face_open = jnp.where(
        lane == LANES - 1,
        outer_open,
        jnp.where(
            lane == SEG - 1,
            f["beside_wet"].astype(F32),
            jnp.where(lane == 2 * SEG - 1, f["beyond_wet"].astype(F32), 1.0),
        ),
    )
    copies = []

    def send(src, dst):
        copies.append(pltpu.make_async_copy(src, dst, sems.at[len(copies)]))
        copies[-1].start()

    def at(index):
        return pl.ds(pl.multiple_of(index * LANES, LANES), LANES)

    def edge(rows, at_left):
        here = lane_of(rows)
        return jnp.where(at_left, here, LANES - 1 - here) < FIX

    left, right = edge(16, jnp.logical_not(odd)), edge(16, odd)
    outer_fix = jnp.logical_and(left, f["outer_own_wet"] == 1)
    beside_fix = jnp.logical_and(right, f["beside_wet"] == 1)
    third = jnp.where(gives, 1, f["x_slot"])

    def emit(r, values):
        if r is None:
            for i, (patch, own, x, whole, out) in enumerate(
                ((values[0], own_u, x_u, whole_u, u_out), (values[1], own_b, x_b, whole_b, b_out))
            ):
                seg1, seg2 = lane_roll(patch, LANES - SEG), lane_roll(patch, LANES - 2 * SEG)
                left_w, right_w = edge(levels, jnp.logical_not(odd)), edge(levels, odd)
                for t in range(OCEAN_DEV):
                    whole[:, LANES * t : LANES * (t + 1)] = own[t]

                x = jnp.where(left_w, seg1, jnp.where(right_w, seg2, x[...]))
                x = jnp.where(gives, x, own[f["x_tile"]])
                whole[:, at(f["x_tile"])] = x
                whole[:, at(f["outer_tile"])] = jnp.where(left_w, patch, own[f["outer_tile"]])
                whole[:, at(f["beside_tile"])] = jnp.where(right_w, seg1, own[f["beside_tile"]])
                send(whole, out)
            return
        s = slice(r, r + 16)
        seg1, seg2 = lane_roll(values, LANES - SEG), lane_roll(values, LANES - 2 * SEG)
        merged[:, 0, s, :] = jnp.where(outer_fix, values, own_t[:, f["outer_slot"], s, :].astype(F32)).astype(BF16)
        merged[:, 1, s, :] = jnp.where(beside_fix, seg1, own_t[:, f["beside_slot"], s, :].astype(F32)).astype(BF16)
        x = jnp.where(left, seg1, jnp.where(right, seg2, x_t[:, s, :]))
        merged[:, 2, s, :] = jnp.where(gives, own_t[:, 1, s, :].astype(F32), x).astype(BF16)

    advance_alone(state, adv, u, b, heat, face_open, kron, n, levels, emit)
    for i, slot in enumerate((f["outer_slot"], f["beside_slot"], third)):
        send(merged.at[:, i], t_out.at[:, :, at(slot)])
    for c in copies:
        c.wait()


def call(kernel, outs, scratch, args, spaces, out_spaces=None, flops=0, name=None):
    where = {"s": pltpu.SMEM, "v": pltpu.VMEM, "h": pltpu.HBM}
    out_spaces = out_spaces or "v" * len(outs)
    return pl.pallas_call(
        kernel,
        out_shape=tuple(
            pltpu.SMEM(s, d) if c == "s" else jax.ShapeDtypeStruct(s, d) for (s, d), c in zip(outs, out_spaces)
        ),
        in_specs=[pl.BlockSpec(memory_space=where[c]) for c in spaces],
        out_specs=tuple(pl.BlockSpec(memory_space=where[c]) for c in out_spaces),
        scratch_shapes=[pltpu.VMEM(s, F32) if isinstance(s, tuple) else s for s in scratch],
        compiler_params=pltpu.CompilerParams(vmem_limit_bytes=48 * 2**20),
        cost_estimate=pl.CostEstimate(flops=flops, bytes_accessed=4_000_000, transcendentals=0),
        name=name,
    )(*(pltpu.with_memory_space_constraint(a, pltpu.HBM) if c == "h" else a for a, c in zip(args, spaces)))


def on_device(ocean_u, ocean_b, tracers, wet_tiles, kinetic):
    axes = ("sec", "tile")
    devices = lax.axis_size("sec") * lax.axis_size("tile")
    levels, n = ocean_u.shape[0], tracers.shape[0]
    dev = (lax.axis_index("sec") * lax.axis_size("tile") + lax.axis_index("tile")).astype(jnp.int32).reshape(1)
    strip = levels // 2
    fields = n + 1
    ocean, tile = ocean_u.shape, (levels, LANES)
    wet_smem, kin_smem = pltpu.SMEM(wet_tiles.shape, jnp.int32), pltpu.SMEM(kinetic.shape, F32)
    inner, outer, u0, b0, t0, kinetic_v, facts = call(
        pack_kernel,
        [
            ((strip + 2 * levels, LANES), F32),
            ((strip, LANES), F32),
            (ocean, F32),
            (ocean, F32),
            (tracers.shape, BF16),
            (kinetic.shape, F32),
            ((len(FACTS),), jnp.int32),
        ],
        [wet_smem, kin_smem, pltpu.SemaphoreType.DMA((6,))],
        (dev, wet_tiles, kinetic, ocean_u, ocean_b, tracers),
        "shhhhh",
        "vvvvvvs",
        flops=10_000_000,
        name="pack",
    )
    in_pairs = [(i, i ^ 1) for i in range(devices)]
    across = [(i, (i + 1) % devices if i % 2 else (i - 1) % devices) for i in range(devices)]
    inner = lax.ppermute(inner, axes, in_pairs)
    outer = lax.ppermute(outer, axes, across)
    own_u, own_b, own_t, kron, p_state, p_u, p_b = call(
        own_kernel,
        [
            ((OCEAN_DEV, *tile), F32),
            ((OCEAN_DEV, *tile), F32),
            ((n, WET_DEV, *tile), BF16),
            ((2, 2 * fields * 8, fields * 8), BF16),
            ((fields, *tile), F32),
            (tile, F32),
            (tile, F32),
        ],
        [
            (OCEAN_DEV, *tile),
            (OCEAN_DEV, *tile),
            (n, WET_DEV, *tile),
            (n, WET_DEV, levels + 2 * PAD, LANES),
        ],
        (facts, kinetic_v, u0, b0, t0),
        "svvvv",
        flops=2_000_000_000,
        name="own_tiles",
    )
    alone = [(fields, 1, *tile), (fields, 1, levels + 2 * PAD, LANES)]
    x_t, x_u, x_b, p_state, p_u, p_b = call(
        x_kernel,
        [((n, *tile), F32), (tile, F32), (tile, F32), ((fields, *tile), F32), (tile, F32), (tile, F32)],
        alone,
        (facts, kinetic_v, kron, u0, b0, t0, inner, p_state, p_u, p_b),
        "s" + "v" * 9,
        flops=1_000_000_000,
        name="x_tile",
    )
    return tuple(
        call(
            last_kernel,
            [(ocean, F32), (ocean, F32), (tracers.shape, BF16)],
            [*alone, ocean, ocean, pltpu.VMEM((n, WET_DEV, *tile), BF16), pltpu.SemaphoreType.DMA((5,))],
            (facts, kron, outer, p_state, p_u, p_b, own_u, own_b, own_t, x_u, x_b, x_t),
            "s" + "v" * 11,
            "hhh",
            flops=1_000_000_000,
            name="boundaries",
        )
    )


def solution(mesh):
    spread = P(None, ("sec", "tile"))
    tracer_spread = P(None, None, ("sec", "tile"))

    def program(ocean_u, ocean_b, tracers, wet_tiles, kinetic_matrix):
        u, b, t = jax.shard_map(
            on_device,
            mesh=mesh,
            in_specs=(spread, spread, tracer_spread, P(), P()),
            out_specs=(spread, spread, tracer_spread),
            check_vma=False,
        )(ocean_u, ocean_b, tracers, wet_tiles, kinetic_matrix)
        return t, u, b

    return program
```

```python
import functools

import jax
import jax.numpy as jnp
from jax import lax
from jax.experimental import pallas as pl
from jax.experimental.pallas import tpu as pltpu
from jax.sharding import PartitionSpec as P

LANES = 128
STEPS = 2
WET_DEV = 3
OCEAN_DEV = 4

DT_OCEAN = 0.25
PRESSURE = 1.0
HORIZ_VISC = 0.2
VERT_VISC = 0.2
HEATING = 0.2
KAPPA_BASE = 0.05
KAPPA_SPAN = 0.35
DT_TRACER = 0.3
DT_MIX = 1.0
KINETIC_DELTA = 0.5
SURFACE_LIGHT = 10.0
WATER_ATT = 0.04
PIGMENT_ATT = 0.08
GROWTH = 0.05
THERMAL_GAIN = 0.1

SEG = 40
HALF = SEG // 2
FIX = 8
PAD = 8
F32, BF16 = jnp.float32, jnp.bfloat16


FACTS = (
    "odd",
    "gives",
    "x_slot",
    "x_tile",
    "outer_slot",
    "outer_tile",
    "beside_slot",
    "beside_tile",
    "outer_own_wet",
    "outer_far_wet",
    "beside_wet",
    "beyond_wet",
    "tile0",
    "tile1",
    "tile2",
    "joined0",
    "joined1",
    "early",
)


def find_facts(share, dev_ref, wet_ref, out_ref):
    k = dev_ref[0]
    odd = lax.rem(k, 2)
    first, base = WET_DEV * k, OCEAN_DEV * k
    listed = wet_ref.shape[0]
    tiles = listed // WET_DEV * OCEAN_DEV
    is_odd = odd == 1
    w = [wet_ref[first + s] for s in range(WET_DEV)]
    probe = wet_ref[first + jnp.where(is_odd, -1, 3)]
    gives = jnp.logical_and(probe >= base, probe < base + OCEAN_DEV)
    before = jnp.where(k == 0, listed - 1, first - 1)
    after = jnp.where(first + WET_DEV == listed, 0, first + WET_DEV)
    outer_far = jnp.where(
        is_odd,
        jnp.where(base + OCEAN_DEV == tiles, 0, base + OCEAN_DEV),
        jnp.where(k == 0, tiles - 1, base - 1),
    )
    far_listed = wet_ref[first + jnp.where(is_odd, -2, 4)] == base + jnp.where(is_odd, -1, 4)
    f = {"odd": odd, "early": lax.rem(k, share) == 0, "gives": gives, "x_slot": 2 - 2 * odd, "x_tile": 3 - 3 * odd}
    f["outer_slot"], f["outer_tile"] = 2 * odd, 3 * odd
    f["beside_slot"] = jnp.where(gives, 2 - 2 * odd, 1)
    f["beside_tile"] = jnp.where(gives, 2 - odd, 3 - 3 * odd)
    f["outer_own_wet"] = jnp.where(is_odd, w[2] == base + 3, w[0] == base)
    f["outer_far_wet"] = wet_ref[jnp.where(is_odd, after, before)] == outer_far
    f["beside_wet"] = jnp.logical_or(gives, w[1] == base + 3 - 3 * odd)
    f["beyond_wet"] = jnp.logical_or(jnp.logical_not(gives), far_listed)
    for s in range(WET_DEV):
        f[f"tile{s}"] = jnp.clip(w[s] - base, 0, OCEAN_DEV - 1)
    for s in range(WET_DEV - 1):
        x_here = jnp.logical_or(f["x_slot"] == s, f["x_slot"] == s + 1)
        f[f"joined{s}"] = jnp.logical_and(w[s + 1] - w[s] == 1, jnp.logical_or(gives, jnp.logical_not(x_here)))
    for i, name in enumerate(FACTS):
        out_ref[i] = f[name].astype(jnp.int32)


def read_facts(ref):
    return {name: ref[i] for i, name in enumerate(FACTS)}


def lane_of(rows):
    return lax.broadcasted_iota(jnp.int32, (rows, LANES), 1)


def lane_roll(x, shift):
    return pltpu.roll(x, shift, x.ndim - 1)


def upper(x):
    row = lax.broadcasted_iota(jnp.int32, x.shape, 0)
    return jnp.where(row == 0, x, pltpu.roll(x, 1, 0))


def lower(x):
    n = x.shape[0]
    row = lax.broadcasted_iota(jnp.int32, x.shape, 0)
    return jnp.where(row == n - 1, x, pltpu.roll(x, n - 1, 0))


def absorbed_light(pigment):
    att = WATER_ATT + PIGMENT_ATT * pigment * pigment
    depth = att
    rows = att.shape[0]
    row = lax.broadcasted_iota(jnp.int32, att.shape, 0)
    step = 1
    while step < rows:
        depth = depth + jnp.where(row >= step, pltpu.roll(depth, step, 0), 0.0)
        step *= 2
    return SURFACE_LIGHT * (jnp.exp(att - depth) - jnp.exp(-depth))


def new_velocity(u, u_left, u_right, b, b_right):
    horiz = u_left + u_right - 2.0 * u
    vert = upper(u) + lower(u) - 2.0 * u
    return u + DT_OCEAN * (HORIZ_VISC * horiz + VERT_VISC * vert - PRESSURE * (b_right - b))


def diffusivity(u, b):
    rows = u.shape[0]
    row = lax.broadcasted_iota(jnp.int32, u.shape, 0)
    shear = u - lower(u)
    strat = b - lower(b)
    kappa = KAPPA_BASE + KAPPA_SPAN * (1.0 / (1.0 + jnp.exp(-4.0 * (shear * shear - strat))))
    return jnp.where(row == rows - 1, 0.0, kappa)


def face_parts(u, face_open):
    w = DT_TRACER * u * face_open
    return jnp.maximum(w, 0.0), jnp.minimum(w, 0.0)


def advect(state, adv, t, src, left, right, coeffs, fields, levels):
    centre, from_left, from_right = coeffs
    chunk = 16
    lane = lane_of(chunk)
    for r in range(0, levels, chunk):
        s = slice(r, r + chunk)
        for f in range(fields):
            here = to_left = to_right = state[f, src, s, :]
            if right is not None:
                to_left = jnp.where(lane == 0, state[f, right, s, :], here)
            if left is not None:
                to_right = jnp.where(lane == LANES - 1, state[f, left, s, :], here)
            adv[f, t, PAD + r : PAD + r + chunk, :] = (
                here * centre[s] + lane_roll(to_left, LANES - 1) * from_right[s] + lane_roll(to_right, 1) * from_left[s]
            )


def mix_and_react(adv, t, kappa, warmth, light, kron, fields, levels, emit):
    chunk = 16
    above = jnp.where(lax.broadcasted_iota(jnp.int32, kappa.shape, 0) == 0, 0.0, pltpu.roll(kappa, 1, 0))
    stay = 1.0 - DT_MIX * (kappa + above)
    rows = (fields + (18 - fields)) * 8
    k_hi = kron[:rows, :]
    k_both = kron[...]
    for r in range(0, levels, chunk):
        s = slice(r, r + chunk)
        at = PAD + r
        here = adv[:fields, t, at : at + chunk, :]
        up = adv[:fields, t, at - 1 : at - 1 + chunk, :]
        down = adv[:fields, t, at + 1 : at + 1 + chunk, :]
        mixed = here * stay[s] + (DT_MIX * kappa[s]) * down + (DT_MIX * above[s]) * up
        halves = []
        for h in range(2):
            part = mixed[:, 8 * h : 8 * h + 8, :].reshape(fields * 8, LANES)
            if fields < 18:
                part = jnp.concatenate([part, jnp.zeros(((18 - fields) * 8, LANES), F32)], axis=0)
            halves.append(part)
        wide = jnp.concatenate(halves, axis=1)
        hi = wide.astype(BF16)
        lo = (wide - hi.astype(F32)).astype(BF16)
        by_hi = jnp.dot(k_both, hi, preferred_element_type=F32)
        by_lo = jnp.dot(k_hi, lo, preferred_element_type=F32)
        drift = by_hi[:rows] + (by_hi[rows:] + by_lo)
        out = []
        for h in range(2):
            d = drift[:, LANES * h : LANES * h + LANES].reshape(18, 8, LANES)[:fields]
            sh = slice(r + 8 * h, r + 8 * h + 8)
            new = mixed[:, 8 * h : 8 * h + 8, :] + warmth[sh] * d
            first = new[:1] + GROWTH * light[sh][None]
            out.append(jnp.concatenate([first, new[1:]], axis=0))
        emit(r, jnp.concatenate(out, axis=1))


def tile_of(ref, index):
    return ref[:, pl.ds(pl.multiple_of(index * LANES, LANES), LANES)]


def slot_of(ref, j, index):
    return ref[j, :, pl.ds(pl.multiple_of(index * LANES, LANES), LANES)].astype(F32)


U_AT, B_AT, T0_AT, COMBO_AT, WIDE = 40, 44, 48, 50, 3


def pack_kernel(
    share, dev, wet_hbm, kin_hbm, u_hbm, b_hbm, t_hbm, inner, outer, u, b, tracers, kin_v, found, wet, kin, sems
):
    pairs = ((wet_hbm, wet), (kin_hbm, kin), (t_hbm, tracers), (u_hbm, u), (b_hbm, b), (kin_hbm, kin_v))
    copies = [pltpu.make_async_copy(src, dst, sems.at[i]) for i, (src, dst) in enumerate(pairs)]
    for c in copies:
        c.start()
    for c in copies:
        c.wait()
    find_facts(share, dev, wet, found)
    f = read_facts(found)
    levels = u.shape[0]
    half = levels // 2
    n = tracers.shape[0]
    lane = lane_of(half)

    def combo_of(index):
        total = None
        for j in range(n):
            term = kin[0, j] * slot_of(tracers, j, index)
            total = term if total is None else total + term
        return total

    def put(acc, value, at, width, right):
        for h in range(2):
            to = at + 64 * h
            here = jnp.bitwise_and(lane + right * width - to, LANES - 1) < width
            acc = jnp.where(here, lane_roll(value[half * h : half * (h + 1)], to), acc)
        return acc

    def strip(slot, tile, right):
        acc = jnp.zeros((half, LANES), F32)
        for j in range(n):
            acc = put(acc, slot_of(tracers, j, slot), 2 * j, 2, right)
        acc = put(acc, tile_of(u, tile), U_AT, WIDE, right)
        return put(acc, tile_of(b, tile), B_AT, WIDE, right)

    outer[...] = strip(f["outer_slot"], f["outer_tile"], f["odd"])
    x_combo = combo_of(f["x_slot"])
    acc = strip(f["x_slot"], f["beside_tile"], 1 - f["odd"])
    acc = put(acc, slot_of(tracers, 0, 1), T0_AT, 2, 1 - f["odd"])
    inner[:half] = put(acc, combo_of(1), COMBO_AT, 2, 1 - f["odd"])
    gives = f["gives"] == 1
    inner[half : half + levels] = jnp.where(gives, tile_of(u, f["x_tile"]), slot_of(tracers, 0, f["x_slot"]))
    inner[half + levels :] = jnp.where(gives, tile_of(b, f["x_tile"]), x_combo)


def patch_masks(f, rows):
    lane = lane_of(rows)
    near = jnp.where(f["odd"] == 1, LANES - 1 - lane, lane) < LANES // 2
    in_1 = jnp.logical_and(lane >= HALF, lane < HALF + SEG)
    in_2 = jnp.logical_and(lane >= HALF + SEG, lane < HALF + 2 * SEG)
    return near, in_1, in_2


def expand_kinetics(kin, kron):
    n = kin.shape[0]
    rows = (n + 1) * 8
    to_rows = lax.broadcasted_iota(jnp.int32, (rows, n), 0) // 8 == lax.broadcasted_iota(jnp.int32, (rows, n), 1)
    to_cols = lax.broadcasted_iota(jnp.int32, (n, rows), 1) // 8 == lax.broadcasted_iota(jnp.int32, (n, rows), 0)
    tall = jnp.dot(to_rows.astype(F32), kin[...], precision=lax.Precision.HIGHEST, preferred_element_type=F32)
    full = jnp.dot(tall, to_cols.astype(F32), precision=lax.Precision.HIGHEST, preferred_element_type=F32)
    row = lax.broadcasted_iota(jnp.int32, (rows, rows), 0)
    col = lax.broadcasted_iota(jnp.int32, (rows, rows), 1)
    full = jnp.where(lax.rem(row, 8) == lax.rem(col, 8), full, 0.0)
    with_combo = jnp.where(row < 8, jnp.where(col - 8 * n == row, 1.0, 0.0), full)
    for i, m in enumerate((with_combo, full)):
        hi = m.astype(BF16)
        kron[i, :rows, :] = hi
        kron[i, rows:, :] = (m - hi.astype(F32)).astype(BF16)


def start_tile(state, adv, t, fields, levels):
    for row in (0, PAD + levels):
        adv[:, t, row : row + 8, :] = jnp.zeros((fields, 8, LANES), F32)


def own_kernel(part, facts, kin, u0, b0, tracers, *refs):
    u, b, state, kron, p_state, p_u, p_b = refs[-9:-2] if part == 0 else refs[-8:-1]
    adv = refs[-1]
    if part == 0:
        refs[-2][...] = refs[0][...]
    f = read_facts(facts)
    levels = u0.shape[0]
    n = tracers.shape[0]
    lane = lane_of(levels)
    gives = f["gives"] == 1
    tile = [f[f"tile{s}"] for s in range(WET_DEV)]
    joined = [f["joined0"], f["joined1"]]

    def start():
        expand_kinetics(kin, kron)
        for t in range(OCEAN_DEV):
            u[t] = u0[:, LANES * t : LANES * (t + 1)]
            b[t] = b0[:, LANES * t : LANES * (t + 1)]
        for s in range(WET_DEV):
            state[:, s] = tracers[:, :, LANES * s : LANES * (s + 1)].astype(F32)

        near, in_1, in_2 = patch_masks(f, levels)

        def lay(own, beside, x):
            seg1 = lane_roll(jnp.where(near, x, beside), SEG)
            return jnp.where(in_1, seg1, jnp.where(in_2, lane_roll(x, 2 * SEG), own))

        for p, field in ((p_u, u), (p_b, b)):
            p[...] = lay(field[f["outer_tile"]], field[f["beside_tile"]], field[f["x_tile"]])
        for j in range(n):
            p_state[j] = lay(*[state[j, f[name]] for name in ("outer_slot", "beside_slot", "x_slot")])

    def one_step(count, first, tile, joined):
        light = []
        for s in range(count):
            start_tile(state, adv, s, n, levels)
            light.append(absorbed_light(state[0, first + s]))
            b[tile[s]] = b[tile[s]] + HEATING * light[s]
        us = [u[t] for t in range(OCEAN_DEV)]
        bs = [b[t] for t in range(OCEAN_DEV)]
        for t in range(OCEAN_DEV):
            nxt, prv = (t + 1) % OCEAN_DEV, (t - 1) % OCEAN_DEV
            u_right = lane_roll(jnp.where(lane == 0, us[nxt], us[t]), LANES - 1)
            u_left = lane_roll(jnp.where(lane == LANES - 1, us[prv], us[t]), 1)
            b_right = lane_roll(jnp.where(lane == 0, bs[nxt], bs[t]), LANES - 1)
            u[t] = new_velocity(us[t], u_left, u_right, bs[t], b_right)
        parts = []
        for s in range(count):
            shut = lane == LANES - 1
            if s < count - 1:
                shut = jnp.logical_and(shut, joined[s] == 0)
            parts.append(face_parts(u[tile[s]], jnp.where(shut, 0.0, 1.0)))
        for s in range(count):
            pos, neg = parts[s]
            before = parts[s - 1] if s else (jnp.zeros_like(pos), jnp.zeros_like(neg))
            pos_left = lane_roll(jnp.where(lane == LANES - 1, before[0], pos), 1)
            neg_left = lane_roll(jnp.where(lane == LANES - 1, before[1], neg), 1)
            coeffs = (1.0 - pos + neg_left, pos_left, -neg)
            left = first + s - 1 if s else None
            right = first + s + 1 if s < count - 1 else None
            advect(state, adv, s, first + s, left, right, coeffs, n, levels)
        for s in range(count):
            ub, bb = u[tile[s]], b[tile[s]]
            kappa = diffusivity(ub, bb)
            warmth = KINETIC_DELTA * jnp.exp(THERMAL_GAIN * bb)

            def emit(r, values, s=s):
                state[:, first + s, r : r + 16, :] = values

            mix_and_react(adv, s, kappa, warmth, light[s], kron.at[1], n, levels, emit)

    early = f["early"] == 1
    if part == 0:
        pl.when(early)(start)
    else:
        pl.when(jnp.logical_not(early))(start)

        @pl.when(gives)
        def _():
            pl.loop(0, STEPS)(lambda _: one_step(WET_DEV, 0, tile, joined))

        @pl.when(jnp.logical_not(gives))
        def _():
            odd = f["odd"]
            tiles = [jnp.where(odd == 1, tile[s + 1], tile[s]) for s in range(WET_DEV - 1)]
            pairs = [jnp.where(odd == 1, joined[1], joined[0])]
            pl.loop(0, STEPS)(lambda _: one_step(WET_DEV - 1, odd, tiles, pairs))


def advance_alone(state, adv, u, b, heat, face_open, kron, n, levels, emit, combined):
    for step in range(STEPS):
        last = step == STEPS - 1
        light = absorbed_light(state[0, 0])
        b = b + HEATING * heat * light
        u = new_velocity(u, lane_roll(u, 1), lane_roll(u, LANES - 1), b, lane_roll(b, LANES - 1))
        if last:
            emit(None, (u, b))
        by_field = combined and not last
        count = n + 1 if by_field else n
        pos, neg = face_parts(u, face_open)
        pos_left, neg_left = lane_roll(pos, 1), lane_roll(neg, 1)
        advect(state, adv, 0, 0, None, None, (1.0 - pos + neg_left, pos_left, -neg), count, levels)
        kappa = diffusivity(u, b)
        warmth = KINETIC_DELTA * jnp.exp(THERMAL_GAIN * b)

        def put(r, values):
            state[:n, 0, r : r + 16, :] = values[:n]

        mix_and_react(adv, 0, kappa, warmth, light, kron.at[0 if by_field else 1], count, levels, emit if last else put)


def from_strip(ref, half, shift):
    return jnp.concatenate(
        [lane_roll(ref[:half], lax.rem(shift + 3 * LANES - 64 * h, LANES)) for h in range(2)], axis=0
    )


def x_kernel(
    facts, kron, u0, b0, tracers, inner, pre_state, pre_u, pre_b,
    x_t, x_u, x_b, p_state, p_combo, p_u, p_b, state, adv,
):
    f = read_facts(facts)
    levels = u0.shape[0]
    half = levels // 2
    n = tracers.shape[0]
    gives = f["gives"] == 1
    lane = lane_of(levels)
    tile1 = inner[half : half + levels]
    tile2 = inner[half + levels :]
    start_tile(state, adv, 0, n, levels)

    near, in_1, in_2 = patch_masks(f, levels)
    x_in_1 = jnp.logical_and(in_1, lane_roll(jnp.where(near, 1, 0), SEG) == 1)
    beyond = jnp.logical_and(in_2, lane_roll(jnp.where(near, 1, 0), 2 * SEG) == 1)
    face_open = jnp.where(lane == LANES - 1, 0.0, 1.0)

    def x_whole(patch, x):
        patch = jnp.where(x_in_1, lane_roll(x, SEG), patch)
        return jnp.where(in_2, lane_roll(x, 2 * SEG), patch)

    def with_far(patch, at):
        return jnp.where(beyond, from_strip(inner, half, 2 * SEG - at), patch)

    @pl.when(gives)
    def _():
        p_u[...] = with_far(pre_u[...], U_AT)
        p_b[...] = with_far(pre_b[...], B_AT)
        for j in range(1, n):
            p_state[j] = jnp.where(x_in_1, from_strip(inner, half, SEG - 2 * j), pre_state[j])
        p_state[0] = with_far(x_whole(pre_state[0], tile1), T0_AT)
        p_combo[...] = with_far(x_whole(pre_state[0], tile2), COMBO_AT)
        state[0, 0], state[1, 0] = tile1, tile2
        u, b = tile_of(u0, f["x_tile"]), tile_of(b0, f["x_tile"])
        for step in range(STEPS):
            light = absorbed_light(state[0, 0])
            b = b + HEATING * light
            u = new_velocity(u, lane_roll(u, 1), lane_roll(u, LANES - 1), b, lane_roll(b, LANES - 1))
            if step < STEPS - 1:
                pos, neg = face_parts(u, face_open)
                pos_left, neg_left = lane_roll(pos, 1), lane_roll(neg, 1)
                advect(state, adv, 0, 0, None, None, (1.0 - pos + neg_left, pos_left, -neg), 2, levels)
                kappa = diffusivity(u, b)
                mixed = []
                for i in range(2):
                    field = adv[i, 0, PAD : PAD + levels, :]
                    flux = kappa * (lower(field) - field)
                    row = lax.broadcasted_iota(jnp.int32, flux.shape, 0)
                    mixed.append(field + DT_MIX * (flux - jnp.where(row == 0, 0.0, pltpu.roll(flux, 1, 0))))
                warmth = KINETIC_DELTA * jnp.exp(THERMAL_GAIN * b)
                state[0, 0] = mixed[0] + warmth * mixed[1] + GROWTH * light
        x_u[...], x_b[...] = u, b

    @pl.when(jnp.logical_not(gives))
    def _():
        p_u[...] = with_far(x_whole(pre_u[...], tile1), U_AT)
        p_b[...] = with_far(x_whole(pre_b[...], tile2), B_AT)
        for j in range(n):
            p_state[j] = with_far(pre_state[j], 2 * j)
            state[j, 0] = slot_of(tracers, j, f["x_slot"])
        p_combo[...] = pre_state[0]

        def emit(r, values):
            if r is None:
                x_u[...], x_b[...] = values
            else:
                x_t[:, r : r + 16, :] = values

        advance_alone(state, adv, tile1, tile2, 1.0, face_open, kron, n, levels, emit, False)


def last_kernel(
    facts, kin, kron, outer, pre_state, p_combo, p_u, p_b, own_u, own_b, own_t, x_u, x_b, x_t,
    u_out, b_out, t_out, state, adv, whole_u, whole_b, merged, sems,
):
    f = read_facts(facts)
    levels = p_u.shape[0]
    half = levels // 2
    n = own_t.shape[0]
    gives, odd = f["gives"] == 1, f["odd"] == 1
    lane = lane_of(levels)
    near, in_1, in_2 = patch_masks(f, levels)
    halo = jnp.logical_not(jnp.logical_or(near, jnp.logical_or(in_1, in_2)))
    start_tile(state, adv, 0, n + 1, levels)
    u = jnp.where(halo, from_strip(outer, half, -U_AT), p_u[...])
    b = jnp.where(halo, from_strip(outer, half, -B_AT), p_b[...])
    combo = None
    for j in range(n):
        x = jnp.where(halo, from_strip(outer, half, -2 * j), pre_state[j])
        state[j, 0] = x
        combo = kin[0:1, j : j + 1] * x if combo is None else combo + kin[0:1, j : j + 1] * x
    x_in_1 = jnp.logical_and(in_1, lane_roll(jnp.where(near, 1, 0), SEG) == 1)
    handed = jnp.logical_and(gives, jnp.logical_or(x_in_1, in_2))
    state[n, 0] = jnp.where(handed, p_combo[...], combo)

    def sides(here, there, boundary_at):
        return lane_roll(jnp.where(near, here.astype(F32), there.astype(F32)), boundary_at)

    one = jnp.int32(1)
    heat = jnp.where(
        in_1,
        sides(one, f["beside_wet"], SEG),
        jnp.where(in_2, sides(f["beyond_wet"], one, 2 * SEG), sides(f["outer_own_wet"], f["outer_far_wet"], 0)),
    )
    outer_open = (f["outer_own_wet"] * f["outer_far_wet"]).astype(F32)
    face_open = jnp.where(
        lane == LANES - 1,
        outer_open,
        jnp.where(
            lane == SEG - 1,
            f["beside_wet"].astype(F32),
            jnp.where(lane == 2 * SEG - 1, f["beyond_wet"].astype(F32), 1.0),
        ),
    )
    copies = []

    def send(src, dst):
        copies.append(pltpu.make_async_copy(src, dst, sems.at[len(copies)]))
        copies[-1].start()

    def at(index):
        return pl.ds(pl.multiple_of(index * LANES, LANES), LANES)

    def edge(rows, at_left):
        here = lane_of(rows)
        return jnp.where(at_left, here, LANES - 1 - here) < FIX

    left, right = edge(16, jnp.logical_not(odd)), edge(16, odd)
    outer_fix = jnp.logical_and(left, f["outer_own_wet"] == 1)
    beside_fix = jnp.logical_and(right, f["beside_wet"] == 1)
    third = jnp.where(gives, 1, f["x_slot"])

    def emit(r, values):
        if r is None:
            for i, (patch, own, x, whole, out) in enumerate(
                ((values[0], own_u, x_u, whole_u, u_out), (values[1], own_b, x_b, whole_b, b_out))
            ):
                seg1, seg2 = lane_roll(patch, LANES - SEG), lane_roll(patch, LANES - 2 * SEG)
                left_w, right_w = edge(levels, jnp.logical_not(odd)), edge(levels, odd)
                for t in range(OCEAN_DEV):
                    whole[:, LANES * t : LANES * (t + 1)] = own[t]

                x = jnp.where(left_w, seg1, jnp.where(right_w, seg2, x[...]))
                x = jnp.where(gives, x, own[f["x_tile"]])
                whole[:, at(f["x_tile"])] = x
                whole[:, at(f["outer_tile"])] = jnp.where(left_w, patch, own[f["outer_tile"]])
                whole[:, at(f["beside_tile"])] = jnp.where(right_w, seg1, own[f["beside_tile"]])
                send(whole, out)
            return
        s = slice(r, r + 16)
        seg1, seg2 = lane_roll(values, LANES - SEG), lane_roll(values, LANES - 2 * SEG)
        merged[:, 0, s, :] = jnp.where(outer_fix, values, own_t[:, f["outer_slot"], s, :]).astype(BF16)
        merged[:, 1, s, :] = jnp.where(beside_fix, seg1, own_t[:, f["beside_slot"], s, :]).astype(BF16)
        x = jnp.where(left, seg1, jnp.where(right, seg2, x_t[:, s, :]))
        merged[:, 2, s, :] = jnp.where(gives, own_t[:, 1, s, :], x).astype(BF16)

    advance_alone(state, adv, u, b, heat, face_open, kron, n, levels, emit, True)
    for i, slot in enumerate((f["outer_slot"], f["beside_slot"], third)):
        send(merged.at[:, i], t_out.at[:, :, at(slot)])
    for c in copies:
        c.wait()


def call(kernel, outs, scratch, args, spaces, out_spaces=None, aliases=None, flops=0, name=None):
    where = {"s": pltpu.SMEM, "v": pltpu.VMEM, "h": pltpu.HBM}
    out_spaces = out_spaces or "v" * len(outs)
    return pl.pallas_call(
        kernel,
        out_shape=tuple(
            pltpu.SMEM(s, d) if c == "s" else jax.ShapeDtypeStruct(s, d) for (s, d), c in zip(outs, out_spaces)
        ),
        in_specs=[pl.BlockSpec(memory_space=where[c]) for c in spaces],
        out_specs=tuple(pl.BlockSpec(memory_space=where[c]) for c in out_spaces),
        scratch_shapes=[pltpu.VMEM(s, F32) if isinstance(s, tuple) else s for s in scratch],
        input_output_aliases=aliases or {},
        compiler_params=pltpu.CompilerParams(vmem_limit_bytes=48 * 2**20),
        cost_estimate=pl.CostEstimate(flops=flops, bytes_accessed=4_000_000, transcendentals=0),
        name=name,
    )(*(pltpu.with_memory_space_constraint(a, pltpu.HBM) if c == "h" else a for a, c in zip(args, spaces)))


def on_device(ocean_u, ocean_b, tracers, wet_tiles, kinetic):
    axes = ("sec", "tile")
    devices = lax.axis_size("sec") * lax.axis_size("tile")
    levels, n = ocean_u.shape[0], tracers.shape[0]
    share = lax.axis_size("tile")
    dev = (lax.axis_index("sec") * share + lax.axis_index("tile")).astype(jnp.int32).reshape(1)
    strip = levels // 2
    fields = n + 1
    ocean, tile = ocean_u.shape, (levels, LANES)
    wet_smem, kin_smem = pltpu.SMEM(wet_tiles.shape, jnp.int32), pltpu.SMEM(kinetic.shape, F32)
    inner, outer, u0, b0, t0, kinetic_v, facts = call(
        functools.partial(pack_kernel, share),
        [
            ((strip + 2 * levels, LANES), F32),
            ((strip, LANES), F32),
            (ocean, F32),
            (ocean, F32),
            (tracers.shape, BF16),
            (kinetic.shape, F32),
            ((len(FACTS),), jnp.int32),
        ],
        [wet_smem, kin_smem, pltpu.SemaphoreType.DMA((6,))],
        (dev, wet_tiles, kinetic, ocean_u, ocean_b, tracers),
        "shhhhh",
        "vvvvvvs",
        flops=10_000_000,
        name="pack",
    )
    in_pairs = [(i, i ^ 1) for i in range(devices)]
    across = [(i, (i + 1) % devices if i % 2 else (i - 1) % devices) for i in range(devices)]
    inner = lax.ppermute(inner, axes, in_pairs)
    shapes = [
        ((OCEAN_DEV, *tile), F32),
        ((OCEAN_DEV, *tile), F32),
        ((n, WET_DEV, *tile), F32),
        ((2, 2 * fields * 8, fields * 8), BF16),
        ((n, *tile), F32),
        (tile, F32),
        (tile, F32),
    ]
    adv = [(n, WET_DEV, levels + 2 * PAD, LANES)]
    *carried, outer = call(
        functools.partial(own_kernel, 0),
        [*shapes, (outer.shape, F32)],
        adv,
        (facts, kinetic_v, u0, b0, t0, outer),
        "svvvvv",
        flops=1_000_000_000,
        name="own_tiles_early",
    )
    outer = lax.ppermute(outer, axes, across)
    carried = call(
        functools.partial(own_kernel, 1),
        shapes,
        adv,
        (facts, kinetic_v, u0, b0, t0, *carried),
        "svvvv" + "v" * len(carried),
        aliases={5 + i: i for i in range(len(carried))},
        flops=2_000_000_000,
        name="own_tiles",
    )
    own_u, own_b, own_t, kron, p_state, p_u, p_b = carried
    x_t, x_u, x_b, p_state, p_combo, p_u, p_b = call(
        x_kernel,
        [((n, *tile), F32), (tile, F32), (tile, F32), ((n, *tile), F32), (tile, F32), (tile, F32), (tile, F32)],
        [(n, 1, *tile), (n, 1, levels + 2 * PAD, LANES)],
        (facts, kron, u0, b0, t0, inner, p_state, p_u, p_b),
        "s" + "v" * 8,
        flops=1_000_000_000,
        name="x_tile",
    )
    return tuple(
        call(
            last_kernel,
            [(ocean, F32), (ocean, F32), (tracers.shape, BF16)],
            [
                (fields, 1, *tile),
                (fields, 1, levels + 2 * PAD, LANES),
                ocean,
                ocean,
                pltpu.VMEM((n, WET_DEV, *tile), BF16),
                pltpu.SemaphoreType.DMA((2 + WET_DEV * (levels // 16),)),
            ],
            (facts, kinetic_v, kron, outer, p_state, p_combo, p_u, p_b, own_u, own_b, own_t, x_u, x_b, x_t),
            "s" + "v" * 13,
            "hhh",
            flops=1_000_000_000,
            name="boundaries",
        )
    )


def solution(mesh):
    spread = P(None, ("sec", "tile"))
    tracer_spread = P(None, None, ("sec", "tile"))

    def program(ocean_u, ocean_b, tracers, wet_tiles, kinetic_matrix):
        u, b, t = jax.shard_map(
            on_device,
            mesh=mesh,
            in_specs=(spread, spread, tracer_spread, P(), P()),
            out_specs=(spread, spread, tracer_spread),
            check_vma=False,
        )(ocean_u, ocean_b, tracers, wet_tiles, kinetic_matrix)
        return t, u, b

    return program
```

```python
import functools

import jax
import jax.numpy as jnp
from jax import lax
from jax.experimental import pallas as pl
from jax.experimental.pallas import tpu as pltpu
from jax.sharding import PartitionSpec as P

LANES = 128
STEPS = 2
WET_DEV = 3
OCEAN_DEV = 4

DT_OCEAN = 0.25
PRESSURE = 1.0
HORIZ_VISC = 0.2
VERT_VISC = 0.2
HEATING = 0.2
KAPPA_BASE = 0.05
KAPPA_SPAN = 0.35
DT_TRACER = 0.3
DT_MIX = 1.0
KINETIC_DELTA = 0.5
SURFACE_LIGHT = 10.0
WATER_ATT = 0.04
PIGMENT_ATT = 0.08
GROWTH = 0.05
THERMAL_GAIN = 0.1

EARLY_STEPS = 1
SEG = 40
HALF = SEG // 2
FIX = 8
PAD = 8
F32, BF16 = jnp.float32, jnp.bfloat16


FACTS = (
    "odd",
    "gives",
    "x_slot",
    "x_tile",
    "outer_slot",
    "outer_tile",
    "beside_slot",
    "beside_tile",
    "outer_own_wet",
    "outer_far_wet",
    "beside_wet",
    "beyond_wet",
    "tile0",
    "tile1",
    "tile2",
    "joined0",
    "joined1",
    "early",
)


def find_facts(share, dev_ref, wet_ref, out_ref):
    k = dev_ref[0]
    odd = lax.rem(k, 2)
    first, base = WET_DEV * k, OCEAN_DEV * k
    listed = wet_ref.shape[0]
    tiles = listed // WET_DEV * OCEAN_DEV
    is_odd = odd == 1
    w = [wet_ref[first + s] for s in range(WET_DEV)]
    probe = wet_ref[first + jnp.where(is_odd, -1, 3)]
    gives = jnp.logical_and(probe >= base, probe < base + OCEAN_DEV)
    before = jnp.where(k == 0, listed - 1, first - 1)
    after = jnp.where(first + WET_DEV == listed, 0, first + WET_DEV)
    outer_far = jnp.where(
        is_odd,
        jnp.where(base + OCEAN_DEV == tiles, 0, base + OCEAN_DEV),
        jnp.where(k == 0, tiles - 1, base - 1),
    )
    far_listed = wet_ref[first + jnp.where(is_odd, -2, 4)] == base + jnp.where(is_odd, -1, 4)
    f = {"odd": odd, "early": lax.rem(k, share) == 0, "gives": gives, "x_slot": 2 - 2 * odd, "x_tile": 3 - 3 * odd}
    f["outer_slot"], f["outer_tile"] = 2 * odd, 3 * odd
    f["beside_slot"] = jnp.where(gives, 2 - 2 * odd, 1)
    f["beside_tile"] = jnp.where(gives, 2 - odd, 3 - 3 * odd)
    f["outer_own_wet"] = jnp.where(is_odd, w[2] == base + 3, w[0] == base)
    f["outer_far_wet"] = wet_ref[jnp.where(is_odd, after, before)] == outer_far
    f["beside_wet"] = jnp.logical_or(gives, w[1] == base + 3 - 3 * odd)
    f["beyond_wet"] = jnp.logical_or(jnp.logical_not(gives), far_listed)
    for s in range(WET_DEV):
        f[f"tile{s}"] = jnp.clip(w[s] - base, 0, OCEAN_DEV - 1)
    for s in range(WET_DEV - 1):
        x_here = jnp.logical_or(f["x_slot"] == s, f["x_slot"] == s + 1)
        f[f"joined{s}"] = jnp.logical_and(w[s + 1] - w[s] == 1, jnp.logical_or(gives, jnp.logical_not(x_here)))
    for i, name in enumerate(FACTS):
        out_ref[i] = f[name].astype(jnp.int32)


def read_facts(ref):
    return {name: ref[i] for i, name in enumerate(FACTS)}


def lane_of(rows):
    return lax.broadcasted_iota(jnp.int32, (rows, LANES), 1)


def lane_roll(x, shift):
    return pltpu.roll(x, shift, x.ndim - 1)


def upper(x):
    row = lax.broadcasted_iota(jnp.int32, x.shape, 0)
    return jnp.where(row == 0, x, pltpu.roll(x, 1, 0))


def lower(x):
    n = x.shape[0]
    row = lax.broadcasted_iota(jnp.int32, x.shape, 0)
    return jnp.where(row == n - 1, x, pltpu.roll(x, n - 1, 0))


def absorbed_light(pigment):
    att = WATER_ATT + PIGMENT_ATT * pigment * pigment
    depth = att
    rows = att.shape[0]
    row = lax.broadcasted_iota(jnp.int32, att.shape, 0)
    step = 1
    while step < rows:
        depth = depth + jnp.where(row >= step, pltpu.roll(depth, step, 0), 0.0)
        step *= 2
    return SURFACE_LIGHT * (jnp.exp(att - depth) - jnp.exp(-depth))


def new_velocity(u, u_left, u_right, b, b_right):
    horiz = u_left + u_right - 2.0 * u
    vert = upper(u) + lower(u) - 2.0 * u
    return u + DT_OCEAN * (HORIZ_VISC * horiz + VERT_VISC * vert - PRESSURE * (b_right - b))


def diffusivity(u, b):
    rows = u.shape[0]
    row = lax.broadcasted_iota(jnp.int32, u.shape, 0)
    shear = u - lower(u)
    strat = b - lower(b)
    kappa = KAPPA_BASE + KAPPA_SPAN * (1.0 / (1.0 + jnp.exp(-4.0 * (shear * shear - strat))))
    return jnp.where(row == rows - 1, 0.0, kappa)


def face_parts(u, face_open):
    w = DT_TRACER * u * face_open
    return jnp.maximum(w, 0.0), jnp.minimum(w, 0.0)


def advect(state, adv, t, src, left, right, coeffs, fields, levels):
    centre, from_left, from_right = coeffs
    chunk = 16
    lane = lane_of(chunk)
    for r in range(0, levels, chunk):
        s = slice(r, r + chunk)
        for f in range(fields):
            here = to_left = to_right = state[f, src, s, :]
            if right is not None:
                to_left = jnp.where(lane == 0, state[f, right, s, :], here)
            if left is not None:
                to_right = jnp.where(lane == LANES - 1, state[f, left, s, :], here)
            adv[f, t, PAD + r : PAD + r + chunk, :] = (
                here * centre[s] + lane_roll(to_left, LANES - 1) * from_right[s] + lane_roll(to_right, 1) * from_left[s]
            )


def mix_and_react(adv, t, kappa, warmth, light, kron, fields, levels, emit):
    chunk = 16
    above = jnp.where(lax.broadcasted_iota(jnp.int32, kappa.shape, 0) == 0, 0.0, pltpu.roll(kappa, 1, 0))
    stay = 1.0 - DT_MIX * (kappa + above)
    rows = (fields + (18 - fields)) * 8
    k_hi = kron[:rows, :]
    k_both = kron[...]
    for r in range(0, levels, chunk):
        s = slice(r, r + chunk)
        at = PAD + r
        here = adv[:fields, t, at : at + chunk, :]
        up = adv[:fields, t, at - 1 : at - 1 + chunk, :]
        down = adv[:fields, t, at + 1 : at + 1 + chunk, :]
        mixed = here * stay[s] + (DT_MIX * kappa[s]) * down + (DT_MIX * above[s]) * up
        halves = []
        for h in range(2):
            part = mixed[:, 8 * h : 8 * h + 8, :].reshape(fields * 8, LANES)
            if fields < 18:
                part = jnp.concatenate([part, jnp.zeros(((18 - fields) * 8, LANES), F32)], axis=0)
            halves.append(part)
        wide = jnp.concatenate(halves, axis=1)
        hi = wide.astype(BF16)
        lo = (wide - hi.astype(F32)).astype(BF16)
        by_hi = jnp.dot(k_both, hi, preferred_element_type=F32)
        by_lo = jnp.dot(k_hi, lo, preferred_element_type=F32)
        drift = by_hi[:rows] + (by_hi[rows:] + by_lo)
        out = []
        for h in range(2):
            d = drift[:, LANES * h : LANES * h + LANES].reshape(18, 8, LANES)[:fields]
            sh = slice(r + 8 * h, r + 8 * h + 8)
            new = mixed[:, 8 * h : 8 * h + 8, :] + warmth[sh] * d
            first = new[:1] + GROWTH * light[sh][None]
            out.append(jnp.concatenate([first, new[1:]], axis=0))
        emit(r, jnp.concatenate(out, axis=1))


def tile_of(ref, index):
    return ref[:, pl.ds(pl.multiple_of(index * LANES, LANES), LANES)]


def slot_of(ref, j, index):
    return ref[j, :, pl.ds(pl.multiple_of(index * LANES, LANES), LANES)].astype(F32)


U_AT, B_AT, T0_AT, COMBO_AT, WIDE = 40, 44, 48, 50, 3


def pack_kernel(
    share, dev, wet_hbm, kin_hbm, u_hbm, b_hbm, t_hbm, inner, outer, u, b, tracers, kin_v, found, wet, kin, sems
):
    pairs = ((wet_hbm, wet), (kin_hbm, kin), (t_hbm, tracers), (u_hbm, u), (b_hbm, b), (kin_hbm, kin_v))
    copies = [pltpu.make_async_copy(src, dst, sems.at[i]) for i, (src, dst) in enumerate(pairs)]
    for c in copies:
        c.start()
    for c in copies:
        c.wait()
    find_facts(share, dev, wet, found)
    f = read_facts(found)
    levels = u.shape[0]
    half = levels // 2
    n = tracers.shape[0]
    lane = lane_of(half)

    def combo_of(index):
        total = None
        for j in range(n):
            term = kin[0, j] * slot_of(tracers, j, index)
            total = term if total is None else total + term
        return total

    def put(acc, value, at, width, right):
        for h in range(2):
            to = at + 64 * h
            here = jnp.bitwise_and(lane + right * width - to, LANES - 1) < width
            acc = jnp.where(here, lane_roll(value[half * h : half * (h + 1)], to), acc)
        return acc

    def strip(slot, tile, right):
        acc = jnp.zeros((half, LANES), F32)
        for j in range(n):
            acc = put(acc, slot_of(tracers, j, slot), 2 * j, 2, right)
        acc = put(acc, tile_of(u, tile), U_AT, WIDE, right)
        return put(acc, tile_of(b, tile), B_AT, WIDE, right)

    outer[...] = strip(f["outer_slot"], f["outer_tile"], f["odd"])
    x_combo = combo_of(f["x_slot"])
    acc = strip(f["x_slot"], f["beside_tile"], 1 - f["odd"])
    acc = put(acc, slot_of(tracers, 0, 1), T0_AT, 2, 1 - f["odd"])
    inner[:half] = put(acc, combo_of(1), COMBO_AT, 2, 1 - f["odd"])
    gives = f["gives"] == 1
    inner[half : half + levels] = jnp.where(gives, tile_of(u, f["x_tile"]), slot_of(tracers, 0, f["x_slot"]))
    inner[half + levels :] = jnp.where(gives, tile_of(b, f["x_tile"]), x_combo)


def patch_masks(f, rows):
    lane = lane_of(rows)
    near = jnp.where(f["odd"] == 1, LANES - 1 - lane, lane) < LANES // 2
    in_1 = jnp.logical_and(lane >= HALF, lane < HALF + SEG)
    in_2 = jnp.logical_and(lane >= HALF + SEG, lane < HALF + 2 * SEG)
    return near, in_1, in_2


def expand_kinetics(kin, kron):
    n = kin.shape[0]
    rows = (n + 1) * 8
    to_rows = lax.broadcasted_iota(jnp.int32, (rows, n), 0) // 8 == lax.broadcasted_iota(jnp.int32, (rows, n), 1)
    to_cols = lax.broadcasted_iota(jnp.int32, (n, rows), 1) // 8 == lax.broadcasted_iota(jnp.int32, (n, rows), 0)
    tall = jnp.dot(to_rows.astype(F32), kin[...], precision=lax.Precision.HIGHEST, preferred_element_type=F32)
    full = jnp.dot(tall, to_cols.astype(F32), precision=lax.Precision.HIGHEST, preferred_element_type=F32)
    row = lax.broadcasted_iota(jnp.int32, (rows, rows), 0)
    col = lax.broadcasted_iota(jnp.int32, (rows, rows), 1)
    full = jnp.where(lax.rem(row, 8) == lax.rem(col, 8), full, 0.0)
    with_combo = jnp.where(row < 8, jnp.where(col - 8 * n == row, 1.0, 0.0), full)
    for i, m in enumerate((with_combo, full)):
        hi = m.astype(BF16)
        kron[i, :rows, :] = hi
        kron[i, rows:, :] = (m - hi.astype(F32)).astype(BF16)


def start_tile(state, adv, t, fields, levels):
    for row in (0, PAD + levels):
        adv[:, t, row : row + 8, :] = jnp.zeros((fields, 8, LANES), F32)


def own_kernel(part, facts, kin, u0, b0, tracers, *refs):
    u, b, state, kron, p_state, p_u, p_b = refs[-10:-3] if part == 0 else refs[-8:-1]
    adv = refs[-1]
    if part == 0:
        refs[-3][...] = refs[0][...]
        refs[-2][...] = refs[1][...]
    f = read_facts(facts)
    levels = u0.shape[0]
    n = tracers.shape[0]
    lane = lane_of(levels)
    gives = f["gives"] == 1
    tile = [f[f"tile{s}"] for s in range(WET_DEV)]
    joined = [f["joined0"], f["joined1"]]

    def start():
        expand_kinetics(kin, kron)
        for t in range(OCEAN_DEV):
            u[t] = u0[:, LANES * t : LANES * (t + 1)]
            b[t] = b0[:, LANES * t : LANES * (t + 1)]
        for s in range(WET_DEV):
            state[:, s] = tracers[:, :, LANES * s : LANES * (s + 1)].astype(F32)

        near, in_1, in_2 = patch_masks(f, levels)

        def lay(own, beside, x):
            seg1 = lane_roll(jnp.where(near, x, beside), SEG)
            return jnp.where(in_1, seg1, jnp.where(in_2, lane_roll(x, 2 * SEG), own))

        for p, field in ((p_u, u), (p_b, b)):
            p[...] = lay(field[f["outer_tile"]], field[f["beside_tile"]], field[f["x_tile"]])
        for j in range(n):
            p_state[j] = lay(*[state[j, f[name]] for name in ("outer_slot", "beside_slot", "x_slot")])

    def one_step(count, first, tile, joined):
        light = []
        for s in range(count):
            start_tile(state, adv, s, n, levels)
            light.append(absorbed_light(state[0, first + s]))
            b[tile[s]] = b[tile[s]] + HEATING * light[s]
        us = [u[t] for t in range(OCEAN_DEV)]
        bs = [b[t] for t in range(OCEAN_DEV)]
        for t in range(OCEAN_DEV):
            nxt, prv = (t + 1) % OCEAN_DEV, (t - 1) % OCEAN_DEV
            u_right = lane_roll(jnp.where(lane == 0, us[nxt], us[t]), LANES - 1)
            u_left = lane_roll(jnp.where(lane == LANES - 1, us[prv], us[t]), 1)
            b_right = lane_roll(jnp.where(lane == 0, bs[nxt], bs[t]), LANES - 1)
            u[t] = new_velocity(us[t], u_left, u_right, bs[t], b_right)
        parts = []
        for s in range(count):
            shut = lane == LANES - 1
            if s < count - 1:
                shut = jnp.logical_and(shut, joined[s] == 0)
            parts.append(face_parts(u[tile[s]], jnp.where(shut, 0.0, 1.0)))
        for s in range(count):
            pos, neg = parts[s]
            before = parts[s - 1] if s else (jnp.zeros_like(pos), jnp.zeros_like(neg))
            pos_left = lane_roll(jnp.where(lane == LANES - 1, before[0], pos), 1)
            neg_left = lane_roll(jnp.where(lane == LANES - 1, before[1], neg), 1)
            coeffs = (1.0 - pos + neg_left, pos_left, -neg)
            left = first + s - 1 if s else None
            right = first + s + 1 if s < count - 1 else None
            advect(state, adv, s, first + s, left, right, coeffs, n, levels)
        for s in range(count):
            ub, bb = u[tile[s]], b[tile[s]]
            kappa = diffusivity(ub, bb)
            warmth = KINETIC_DELTA * jnp.exp(THERMAL_GAIN * bb)

            def emit(r, values, s=s):
                state[:, first + s, r : r + 16, :] = values

            mix_and_react(adv, s, kappa, warmth, light[s], kron.at[1], n, levels, emit)

    def steps(begin, end):
        @pl.when(gives)
        def _():
            pl.loop(begin, end)(lambda _: one_step(WET_DEV, 0, tile, joined))

        @pl.when(jnp.logical_not(gives))
        def _():
            odd = f["odd"]
            tiles = [jnp.where(odd == 1, tile[s + 1], tile[s]) for s in range(WET_DEV - 1)]
            pairs = [jnp.where(odd == 1, joined[1], joined[0])]
            pl.loop(begin, end)(lambda _: one_step(WET_DEV - 1, odd, tiles, pairs))

    if part == 0:

        @pl.when(f["early"] == 1)
        def _():
            start()
            steps(0, EARLY_STEPS)

    else:
        pl.when(f["early"] == 0)(start)
        steps(f["early"] * EARLY_STEPS, STEPS)


def gate_kernel(strip, out, passed):
    out[...] = strip[...]
    passed[...] = strip[:8]


def advance_alone(state, adv, u, b, heat, face_open, kron, n, levels, emit, combined):
    for step in range(STEPS):
        last = step == STEPS - 1
        light = absorbed_light(state[0, 0])
        b = b + HEATING * heat * light
        u = new_velocity(u, lane_roll(u, 1), lane_roll(u, LANES - 1), b, lane_roll(b, LANES - 1))
        if last:
            emit(None, (u, b))
        by_field = combined and not last
        count = n + 1 if by_field else n
        pos, neg = face_parts(u, face_open)
        pos_left, neg_left = lane_roll(pos, 1), lane_roll(neg, 1)
        advect(state, adv, 0, 0, None, None, (1.0 - pos + neg_left, pos_left, -neg), count, levels)
        kappa = diffusivity(u, b)
        warmth = KINETIC_DELTA * jnp.exp(THERMAL_GAIN * b)

        def put(r, values):
            state[:n, 0, r : r + 16, :] = values[:n]

        mix_and_react(adv, 0, kappa, warmth, light, kron.at[0 if by_field else 1], count, levels, emit if last else put)


def from_strip(ref, half, shift):
    return jnp.concatenate(
        [lane_roll(ref[:half], lax.rem(shift + 3 * LANES - 64 * h, LANES)) for h in range(2)], axis=0
    )


def x_kernel(
    facts, kron, u0, b0, tracers, inner, pre_state, pre_u, pre_b,
    x_t, x_u, x_b, p_state, p_combo, p_u, p_b, state, adv,
):
    f = read_facts(facts)
    levels = u0.shape[0]
    half = levels // 2
    n = tracers.shape[0]
    gives = f["gives"] == 1
    lane = lane_of(levels)
    tile1 = inner[half : half + levels]
    tile2 = inner[half + levels :]
    start_tile(state, adv, 0, n, levels)

    near, in_1, in_2 = patch_masks(f, levels)
    x_in_1 = jnp.logical_and(in_1, lane_roll(jnp.where(near, 1, 0), SEG) == 1)
    beyond = jnp.logical_and(in_2, lane_roll(jnp.where(near, 1, 0), 2 * SEG) == 1)
    face_open = jnp.where(lane == LANES - 1, 0.0, 1.0)

    def x_whole(patch, x):
        patch = jnp.where(x_in_1, lane_roll(x, SEG), patch)
        return jnp.where(in_2, lane_roll(x, 2 * SEG), patch)

    def with_far(patch, at):
        return jnp.where(beyond, from_strip(inner, half, 2 * SEG - at), patch)

    @pl.when(gives)
    def _():
        p_u[...] = with_far(pre_u[...], U_AT)
        p_b[...] = with_far(pre_b[...], B_AT)
        for j in range(1, n):
            p_state[j] = jnp.where(x_in_1, from_strip(inner, half, SEG - 2 * j), pre_state[j])
        p_state[0] = with_far(x_whole(pre_state[0], tile1), T0_AT)
        p_combo[...] = with_far(x_whole(pre_state[0], tile2), COMBO_AT)
        state[0, 0], state[1, 0] = tile1, tile2
        u, b = tile_of(u0, f["x_tile"]), tile_of(b0, f["x_tile"])
        for step in range(STEPS):
            light = absorbed_light(state[0, 0])
            b = b + HEATING * light
            u = new_velocity(u, lane_roll(u, 1), lane_roll(u, LANES - 1), b, lane_roll(b, LANES - 1))
            if step < STEPS - 1:
                pos, neg = face_parts(u, face_open)
                pos_left, neg_left = lane_roll(pos, 1), lane_roll(neg, 1)
                advect(state, adv, 0, 0, None, None, (1.0 - pos + neg_left, pos_left, -neg), 2, levels)
                kappa = diffusivity(u, b)
                mixed = []
                for i in range(2):
                    field = adv[i, 0, PAD : PAD + levels, :]
                    flux = kappa * (lower(field) - field)
                    row = lax.broadcasted_iota(jnp.int32, flux.shape, 0)
                    mixed.append(field + DT_MIX * (flux - jnp.where(row == 0, 0.0, pltpu.roll(flux, 1, 0))))
                warmth = KINETIC_DELTA * jnp.exp(THERMAL_GAIN * b)
                state[0, 0] = mixed[0] + warmth * mixed[1] + GROWTH * light
        x_u[...], x_b[...] = u, b

    @pl.when(jnp.logical_not(gives))
    def _():
        p_u[...] = with_far(x_whole(pre_u[...], tile1), U_AT)
        p_b[...] = with_far(x_whole(pre_b[...], tile2), B_AT)
        for j in range(n):
            p_state[j] = with_far(pre_state[j], 2 * j)
            state[j, 0] = slot_of(tracers, j, f["x_slot"])
        p_combo[...] = pre_state[0]

        def emit(r, values):
            if r is None:
                x_u[...], x_b[...] = values
            else:
                x_t[:, r : r + 16, :] = values

        advance_alone(state, adv, tile1, tile2, 1.0, face_open, kron, n, levels, emit, False)


def last_kernel(
    facts, kin, kron, outer, pre_state, p_combo, p_u, p_b, own_u, own_b, own_t, x_u, x_b, x_t,
    u_out, b_out, t_out, state, adv, whole_u, whole_b, merged, sems,
):
    f = read_facts(facts)
    levels = p_u.shape[0]
    half = levels // 2
    n = own_t.shape[0]
    gives, odd = f["gives"] == 1, f["odd"] == 1
    lane = lane_of(levels)
    near, in_1, in_2 = patch_masks(f, levels)
    halo = jnp.logical_not(jnp.logical_or(near, jnp.logical_or(in_1, in_2)))
    start_tile(state, adv, 0, n + 1, levels)
    u = jnp.where(halo, from_strip(outer, half, -U_AT), p_u[...])
    b = jnp.where(halo, from_strip(outer, half, -B_AT), p_b[...])
    combo = None
    for j in range(n):
        x = jnp.where(halo, from_strip(outer, half, -2 * j), pre_state[j])
        state[j, 0] = x
        combo = kin[0:1, j : j + 1] * x if combo is None else combo + kin[0:1, j : j + 1] * x
    x_in_1 = jnp.logical_and(in_1, lane_roll(jnp.where(near, 1, 0), SEG) == 1)
    handed = jnp.logical_and(gives, jnp.logical_or(x_in_1, in_2))
    state[n, 0] = jnp.where(handed, p_combo[...], combo)

    def sides(here, there, boundary_at):
        return lane_roll(jnp.where(near, here.astype(F32), there.astype(F32)), boundary_at)

    one = jnp.int32(1)
    heat = jnp.where(
        in_1,
        sides(one, f["beside_wet"], SEG),
        jnp.where(in_2, sides(f["beyond_wet"], one, 2 * SEG), sides(f["outer_own_wet"], f["outer_far_wet"], 0)),
    )
    outer_open = (f["outer_own_wet"] * f["outer_far_wet"]).astype(F32)
    face_open = jnp.where(
        lane == LANES - 1,
        outer_open,
        jnp.where(
            lane == SEG - 1,
            f["beside_wet"].astype(F32),
            jnp.where(lane == 2 * SEG - 1, f["beyond_wet"].astype(F32), 1.0),
        ),
    )
    copies = []

    def send(src, dst):
        copies.append(pltpu.make_async_copy(src, dst, sems.at[len(copies)]))
        copies[-1].start()

    def at(index):
        return pl.ds(pl.multiple_of(index * LANES, LANES), LANES)

    def edge(rows, at_left):
        here = lane_of(rows)
        return jnp.where(at_left, here, LANES - 1 - here) < FIX

    left, right = edge(16, jnp.logical_not(odd)), edge(16, odd)
    outer_fix = jnp.logical_and(left, f["outer_own_wet"] == 1)
    beside_fix = jnp.logical_and(right, f["beside_wet"] == 1)
    third = jnp.where(gives, 1, f["x_slot"])

    def emit(r, values):
        if r is None:
            for i, (patch, own, x, whole, out) in enumerate(
                ((values[0], own_u, x_u, whole_u, u_out), (values[1], own_b, x_b, whole_b, b_out))
            ):
                seg1, seg2 = lane_roll(patch, LANES - SEG), lane_roll(patch, LANES - 2 * SEG)
                left_w, right_w = edge(levels, jnp.logical_not(odd)), edge(levels, odd)
                for t in range(OCEAN_DEV):
                    whole[:, LANES * t : LANES * (t + 1)] = own[t]

                x = jnp.where(left_w, seg1, jnp.where(right_w, seg2, x[...]))
                x = jnp.where(gives, x, own[f["x_tile"]])
                whole[:, at(f["x_tile"])] = x
                whole[:, at(f["outer_tile"])] = jnp.where(left_w, patch, own[f["outer_tile"]])
                whole[:, at(f["beside_tile"])] = jnp.where(right_w, seg1, own[f["beside_tile"]])
                send(whole, out)
            return
        s = slice(r, r + 16)
        seg1, seg2 = lane_roll(values, LANES - SEG), lane_roll(values, LANES - 2 * SEG)
        merged[:, 0, s, :] = jnp.where(outer_fix, values, own_t[:, f["outer_slot"], s, :]).astype(BF16)
        merged[:, 1, s, :] = jnp.where(beside_fix, seg1, own_t[:, f["beside_slot"], s, :]).astype(BF16)
        x = jnp.where(left, seg1, jnp.where(right, seg2, x_t[:, s, :]))
        merged[:, 2, s, :] = jnp.where(gives, own_t[:, 1, s, :], x).astype(BF16)

    advance_alone(state, adv, u, b, heat, face_open, kron, n, levels, emit, True)
    for i, slot in enumerate((f["outer_slot"], f["beside_slot"], third)):
        send(merged.at[:, i], t_out.at[:, :, at(slot)])
    for c in copies:
        c.wait()


def call(kernel, outs, scratch, args, spaces, out_spaces=None, aliases=None, flops=0, name=None):
    where = {"s": pltpu.SMEM, "v": pltpu.VMEM, "h": pltpu.HBM}
    out_spaces = out_spaces or "v" * len(outs)
    return pl.pallas_call(
        kernel,
        out_shape=tuple(
            pltpu.SMEM(s, d) if c == "s" else jax.ShapeDtypeStruct(s, d) for (s, d), c in zip(outs, out_spaces)
        ),
        in_specs=[pl.BlockSpec(memory_space=where[c]) for c in spaces],
        out_specs=tuple(pl.BlockSpec(memory_space=where[c]) for c in out_spaces),
        scratch_shapes=[pltpu.VMEM(s, F32) if isinstance(s, tuple) else s for s in scratch],
        input_output_aliases=aliases or {},
        compiler_params=pltpu.CompilerParams(vmem_limit_bytes=48 * 2**20),
        cost_estimate=pl.CostEstimate(flops=flops, bytes_accessed=0, transcendentals=0),
        name=name,
    )(*(pltpu.with_memory_space_constraint(a, pltpu.HBM) if c == "h" else a for a, c in zip(args, spaces)))


def on_device(ocean_u, ocean_b, tracers, wet_tiles, kinetic):
    axes = ("sec", "tile")
    devices = lax.axis_size("sec") * lax.axis_size("tile")
    levels, n = ocean_u.shape[0], tracers.shape[0]
    share = lax.axis_size("tile")
    dev = (lax.axis_index("sec") * share + lax.axis_index("tile")).astype(jnp.int32).reshape(1)
    strip = levels // 2
    fields = n + 1
    ocean, tile = ocean_u.shape, (levels, LANES)
    wet_smem, kin_smem = pltpu.SMEM(wet_tiles.shape, jnp.int32), pltpu.SMEM(kinetic.shape, F32)
    inner, outer, u0, b0, t0, kinetic_v, facts = call(
        functools.partial(pack_kernel, share),
        [
            ((strip + 2 * levels, LANES), F32),
            ((strip, LANES), F32),
            (ocean, F32),
            (ocean, F32),
            (tracers.shape, BF16),
            (kinetic.shape, F32),
            ((len(FACTS),), jnp.int32),
        ],
        [wet_smem, kin_smem, pltpu.SemaphoreType.DMA((6,))],
        (dev, wet_tiles, kinetic, ocean_u, ocean_b, tracers),
        "shhhhh",
        "vvvvvvs",
        flops=10_000_000,
        name="pack",
    )
    in_pairs = [(i, i ^ 1) for i in range(devices)]
    across = [(i, (i + 1) % devices if i % 2 else (i - 1) % devices) for i in range(devices)]
    shapes = [
        ((OCEAN_DEV, *tile), F32),
        ((OCEAN_DEV, *tile), F32),
        ((n, WET_DEV, *tile), F32),
        ((2, 2 * fields * 8, fields * 8), BF16),
        ((n, *tile), F32),
        (tile, F32),
        (tile, F32),
    ]
    adv = [(n, WET_DEV, levels + 2 * PAD, LANES)]
    *carried, inner, outer = call(
        functools.partial(own_kernel, 0),
        [*shapes, (inner.shape, F32), (outer.shape, F32)],
        adv,
        (facts, kinetic_v, u0, b0, t0, inner, outer),
        "svvvvvv",
        flops=1_000_000_000,
        name="own_tiles_early",
    )
    inner = lax.ppermute(inner, axes, in_pairs)
    outer, passed = call(
        gate_kernel,
        [(outer.shape, F32), ((8, LANES), F32)],
        [],
        (outer,),
        "v",
        flops=8_000_000_000,
        name="outer_strip",
    )
    outer = lax.ppermute(outer, axes, across)
    carried = call(
        functools.partial(own_kernel, 1),
        shapes,
        adv,
        (facts, kinetic_v, u0, b0, t0, *carried, passed),
        "svvvv" + "v" * len(carried) + "v",
        aliases={5 + i: i for i in range(len(carried))},
        flops=0,
        name="own_tiles",
    )
    own_u, own_b, own_t, kron, p_state, p_u, p_b = carried
    x_t, x_u, x_b, p_state, p_combo, p_u, p_b = call(
        x_kernel,
        [((n, *tile), F32), (tile, F32), (tile, F32), ((n, *tile), F32), (tile, F32), (tile, F32), (tile, F32)],
        [(n, 1, *tile), (n, 1, levels + 2 * PAD, LANES)],
        (facts, kron, u0, b0, t0, inner, p_state, p_u, p_b),
        "s" + "v" * 8,
        flops=0,
        name="x_tile",
    )
    return tuple(
        call(
            last_kernel,
            [(ocean, F32), (ocean, F32), (tracers.shape, BF16)],
            [
                (fields, 1, *tile),
                (fields, 1, levels + 2 * PAD, LANES),
                ocean,
                ocean,
                pltpu.VMEM((n, WET_DEV, *tile), BF16),
                pltpu.SemaphoreType.DMA((2 + WET_DEV * (levels // 16),)),
            ],
            (facts, kinetic_v, kron, outer, p_state, p_combo, p_u, p_b, own_u, own_b, own_t, x_u, x_b, x_t),
            "s" + "v" * 13,
            "hhh",
            flops=1_000_000_000,
            name="boundaries",
        )
    )


def solution(mesh):
    spread = P(None, ("sec", "tile"))
    tracer_spread = P(None, None, ("sec", "tile"))

    def program(ocean_u, ocean_b, tracers, wet_tiles, kinetic_matrix):
        u, b, t = jax.shard_map(
            on_device,
            mesh=mesh,
            in_specs=(spread, spread, tracer_spread, P(), P()),
            out_specs=(spread, spread, tracer_spread),
            check_vma=False,
        )(ocean_u, ocean_b, tracers, wet_tiles, kinetic_matrix)
        return t, u, b

    return program
```

```python
import functools

import jax
import jax.numpy as jnp
from jax import lax
from jax.experimental import pallas as pl
from jax.experimental.pallas import tpu as pltpu
from jax.sharding import PartitionSpec as P

LANES = 128
STEPS = 2
WET_DEV = 3
OCEAN_DEV = 4

DT_OCEAN = 0.25
PRESSURE = 1.0
HORIZ_VISC = 0.2
VERT_VISC = 0.2
HEATING = 0.2
KAPPA_BASE = 0.05
KAPPA_SPAN = 0.35
DT_TRACER = 0.3
DT_MIX = 1.0
KINETIC_DELTA = 0.5
SURFACE_LIGHT = 10.0
WATER_ATT = 0.04
PIGMENT_ATT = 0.08
GROWTH = 0.05
THERMAL_GAIN = 0.1

EARLY_STEPS = 1
GROUPS = 4
GROUP = LANES // GROUPS
SEG = 10
HALF = SEG // 2
FIX_FIRST, FIX_LAST = 3, 2
PAD = 8
F32, BF16 = jnp.float32, jnp.bfloat16


FACTS = (
    "odd",
    "gives",
    "x_slot",
    "x_tile",
    "outer_slot",
    "outer_tile",
    "beside_slot",
    "beside_tile",
    "outer_own_wet",
    "outer_far_wet",
    "beside_wet",
    "beyond_wet",
    "tile0",
    "tile1",
    "tile2",
    "joined0",
    "joined1",
    "early",
)


def find_facts(share, dev_ref, wet_ref, out_ref):
    k = dev_ref[0]
    odd = lax.rem(k, 2)
    first, base = WET_DEV * k, OCEAN_DEV * k
    listed = wet_ref.shape[0]
    tiles = listed // WET_DEV * OCEAN_DEV
    is_odd = odd == 1
    w = [wet_ref[first + s] for s in range(WET_DEV)]
    probe = wet_ref[first + jnp.where(is_odd, -1, 3)]
    gives = jnp.logical_and(probe >= base, probe < base + OCEAN_DEV)
    before = jnp.where(k == 0, listed - 1, first - 1)
    after = jnp.where(first + WET_DEV == listed, 0, first + WET_DEV)
    outer_far = jnp.where(
        is_odd,
        jnp.where(base + OCEAN_DEV == tiles, 0, base + OCEAN_DEV),
        jnp.where(k == 0, tiles - 1, base - 1),
    )
    far_listed = wet_ref[first + jnp.where(is_odd, -2, 4)] == base + jnp.where(is_odd, -1, 4)
    f = {"odd": odd, "early": lax.rem(k, share) == 0, "gives": gives, "x_slot": 2 - 2 * odd, "x_tile": 3 - 3 * odd}
    f["outer_slot"], f["outer_tile"] = 2 * odd, 3 * odd
    f["beside_slot"] = jnp.where(gives, 2 - 2 * odd, 1)
    f["beside_tile"] = jnp.where(gives, 2 - odd, 3 - 3 * odd)
    f["outer_own_wet"] = jnp.where(is_odd, w[2] == base + 3, w[0] == base)
    f["outer_far_wet"] = wet_ref[jnp.where(is_odd, after, before)] == outer_far
    f["beside_wet"] = jnp.logical_or(gives, w[1] == base + 3 - 3 * odd)
    f["beyond_wet"] = jnp.logical_or(jnp.logical_not(gives), far_listed)
    for s in range(WET_DEV):
        f[f"tile{s}"] = jnp.clip(w[s] - base, 0, OCEAN_DEV - 1)
    for s in range(WET_DEV - 1):
        x_here = jnp.logical_or(f["x_slot"] == s, f["x_slot"] == s + 1)
        f[f"joined{s}"] = jnp.logical_and(w[s + 1] - w[s] == 1, jnp.logical_or(gives, jnp.logical_not(x_here)))
    for i, name in enumerate(FACTS):
        out_ref[i] = f[name].astype(jnp.int32)


def read_facts(ref):
    return {name: ref[i] for i, name in enumerate(FACTS)}


def lane_of(rows):
    return lax.broadcasted_iota(jnp.int32, (rows, LANES), 1)


def lane_roll(x, shift):
    return pltpu.roll(x, shift, x.ndim - 1)


def row_of(x):
    return lax.broadcasted_iota(jnp.int32, x.shape, 0)


def upper(x, groups=1):
    row, rolled = row_of(x), pltpu.roll(x, 1, 0)
    if groups == 1:
        return jnp.where(row == 0, x, rolled)
    other = jnp.where(lane_of(x.shape[0]) < GROUP, x, lane_roll(rolled, GROUP))
    return jnp.where(row == 0, other, rolled)


def lower(x, groups=1):
    n = x.shape[0]
    row, rolled = row_of(x), pltpu.roll(x, n - 1, 0)
    if groups == 1:
        return jnp.where(row == n - 1, x, rolled)
    other = jnp.where(lane_of(n) >= LANES - GROUP, x, lane_roll(rolled, LANES - GROUP))
    return jnp.where(row == n - 1, other, rolled)


def at_top(x, groups):
    top = row_of(x) == 0
    return top if groups == 1 else jnp.logical_and(top, lane_of(x.shape[0]) < GROUP)


def at_bottom(x, groups):
    bottom = row_of(x) == x.shape[0] - 1
    return bottom if groups == 1 else jnp.logical_and(bottom, lane_of(x.shape[0]) >= LANES - GROUP)


def absorbed_light(pigment, groups=1):
    att = WATER_ATT + PIGMENT_ATT * pigment * pigment
    depth = att
    rows = att.shape[0]
    row = row_of(att)
    step = 1
    while step < rows:
        depth = depth + jnp.where(row >= step, pltpu.roll(depth, step, 0), 0.0)
        step *= 2
    if groups > 1:
        total = jnp.broadcast_to(depth[rows - 1 :], depth.shape)
        lane = lane_of(rows)
        for g in range(1, groups):
            depth = depth + jnp.where(lane >= GROUP * g, lane_roll(total, GROUP * g), 0.0)
    return SURFACE_LIGHT * (jnp.exp(att - depth) - jnp.exp(-depth))


def new_velocity(u, u_left, u_right, b, b_right, groups=1):
    horiz = u_left + u_right - 2.0 * u
    vert = upper(u, groups) + lower(u, groups) - 2.0 * u
    return u + DT_OCEAN * (HORIZ_VISC * horiz + VERT_VISC * vert - PRESSURE * (b_right - b))


def diffusivity(u, b, groups=1):
    shear = u - lower(u, groups)
    strat = b - lower(b, groups)
    kappa = KAPPA_BASE + KAPPA_SPAN * (1.0 / (1.0 + jnp.exp(-4.0 * (shear * shear - strat))))
    return jnp.where(at_bottom(kappa, groups), 0.0, kappa)


def face_parts(u, face_open):
    w = DT_TRACER * u * face_open
    return jnp.maximum(w, 0.0), jnp.minimum(w, 0.0)


def advect(state, adv, t, src, left, right, coeffs, fields, levels, groups=1):
    centre, from_left, from_right = coeffs
    chunk = 16
    lane = lane_of(chunk)
    for r in range(0, levels, chunk):
        s = slice(r, r + chunk)
        for f in range(fields):
            here = to_left = to_right = state[f, src, s, :]
            if right is not None:
                to_left = jnp.where(lane == 0, state[f, right, s, :], here)
            if left is not None:
                to_right = jnp.where(lane == LANES - 1, state[f, left, s, :], here)
            new = (
                here * centre[s] + lane_roll(to_left, LANES - 1) * from_right[s] + lane_roll(to_right, 1) * from_left[s]
            )
            adv[f, t, PAD + r : PAD + r + chunk, :] = new
            if groups > 1:
                assert levels == chunk
                adv[f, t, :PAD, :] = lane_roll(new[chunk - PAD :], GROUP)
                adv[f, t, PAD + chunk :, :] = lane_roll(new[:PAD], LANES - GROUP)


def mix_and_react(adv, t, kappa, warmth, light, kron, fields, levels, emit, groups=1):
    chunk = 16
    above = jnp.where(at_top(kappa, groups), 0.0, upper(kappa, groups))
    stay = 1.0 - DT_MIX * (kappa + above)
    rows = kron.shape[1]
    n = rows // 8 - 1
    k_hi, k_both = kron[:rows, :], kron[...]
    for r in range(0, levels, chunk):
        s = slice(r, r + chunk)
        at = PAD + r
        here = adv[:fields, t, at : at + chunk, :]
        up = adv[:fields, t, at - 1 : at - 1 + chunk, :]
        down = adv[:fields, t, at + 1 : at + 1 + chunk, :]
        mixed = here * stay[s] + (DT_MIX * kappa[s]) * down + (DT_MIX * above[s]) * up
        halves = []
        for h in range(2):
            part = mixed[:n, 8 * h : 8 * h + 8, :].reshape(n * 8, LANES)
            halves.append(jnp.concatenate([part, jnp.zeros((8, LANES), F32)], axis=0))
        wide = jnp.concatenate(halves, axis=1)
        hi = wide.astype(BF16)
        lo = (wide - hi.astype(F32)).astype(BF16)
        by_hi = jnp.dot(k_both, hi, preferred_element_type=F32)
        by_lo = jnp.dot(k_hi, lo, preferred_element_type=F32)
        drift = by_hi[:rows] + (by_hi[rows:] + by_lo)
        out = []
        for h in range(2):
            d = drift[:, LANES * h : LANES * h + LANES].reshape(n + 1, 8, LANES)
            part = mixed[:, 8 * h : 8 * h + 8, :]
            sh = slice(r + 8 * h, r + 8 * h + 8)
            first = part[:1] + warmth[sh] * (d[:1] if fields == n else part[n:]) + GROWTH * light[sh][None]
            out.append(jnp.concatenate([first, part[1:n] + warmth[sh] * d[1:n]], axis=0))
        emit(r, jnp.concatenate(out, axis=1))


def tile_of(ref, index):
    return ref[:, pl.ds(pl.multiple_of(index * LANES, LANES), LANES)]


def slot_of(ref, j, index):
    return ref[j, :, pl.ds(pl.multiple_of(index * LANES, LANES), LANES)].astype(F32)


U_AT, B_AT, T0_AT, COMBO_AT, WIDE = 40, 44, 48, 50, 3


def pack_kernel(
    share, dev, wet_hbm, kin_hbm, u_hbm, b_hbm, t_hbm, inner, outer, u, b, tracers, kin_v, found, wet, kin, sems
):
    pairs = ((wet_hbm, wet), (kin_hbm, kin), (t_hbm, tracers), (u_hbm, u), (b_hbm, b), (kin_hbm, kin_v))
    copies = [pltpu.make_async_copy(src, dst, sems.at[i]) for i, (src, dst) in enumerate(pairs)]
    for c in copies:
        c.start()
    for c in copies:
        c.wait()
    find_facts(share, dev, wet, found)
    f = read_facts(found)
    levels = u.shape[0]
    half = levels // 2
    n = tracers.shape[0]
    lane = lane_of(half)

    def combo_of(index):
        total = None
        for j in range(n):
            term = kin[0, j] * slot_of(tracers, j, index)
            total = term if total is None else total + term
        return total

    def put(acc, value, at, width, right):
        for h in range(2):
            to = at + 64 * h
            here = jnp.bitwise_and(lane + right * width - to, LANES - 1) < width
            acc = jnp.where(here, lane_roll(value[half * h : half * (h + 1)], to), acc)
        return acc

    def strip(slot, tile, right):
        acc = jnp.zeros((half, LANES), F32)
        for j in range(n):
            acc = put(acc, slot_of(tracers, j, slot), 2 * j, 2, right)
        acc = put(acc, tile_of(u, tile), U_AT, WIDE, right)
        return put(acc, tile_of(b, tile), B_AT, WIDE, right)

    outer[...] = strip(f["outer_slot"], f["outer_tile"], f["odd"])
    x_combo = combo_of(f["x_slot"])
    acc = strip(f["x_slot"], f["beside_tile"], 1 - f["odd"])
    acc = put(acc, slot_of(tracers, 0, 1), T0_AT, 2, 1 - f["odd"])
    inner[:half] = put(acc, combo_of(1), COMBO_AT, 2, 1 - f["odd"])
    gives = f["gives"] == 1
    inner[half : half + levels] = jnp.where(gives, tile_of(u, f["x_tile"]), slot_of(tracers, 0, f["x_slot"]))
    inner[half + levels :] = jnp.where(gives, tile_of(b, f["x_tile"]), x_combo)


def near_half(f, rows):
    lane = lane_of(rows)
    return jnp.where(f["odd"] == 1, LANES - 1 - lane, lane) < LANES // 2


def patch_masks(f, rows):
    lane = jnp.bitwise_and(lane_of(rows), GROUP - 1)
    in_1 = jnp.logical_and(lane >= SEG, lane < 2 * SEG)
    in_2 = lane >= 2 * SEG
    within = lane - jnp.where(in_2, 2 * SEG, jnp.where(in_1, SEG, 0))
    near = jnp.where(f["odd"] == 1, SEG - 1 - within, within) >= HALF
    return near, in_1, in_2, within


def fold(x, seg):
    rows = x.shape[0] // GROUPS
    group = lane_of(rows) // GROUP
    out = None
    for g in range(GROUPS):
        part = lane_roll(x[rows * g : rows * (g + 1)], GROUP * g + SEG * seg + HALF)
        out = part if out is None else jnp.where(group == g, part, out)
    return out


def unfold(patch, seg, g):
    return lane_roll(patch, LANES - (GROUP * g + SEG * seg + HALF))


def expand_kinetics(kin, kron):
    n = kin.shape[0]
    rows = kron.shape[1]
    to_rows = lax.broadcasted_iota(jnp.int32, (rows, n), 0) // 8 == lax.broadcasted_iota(jnp.int32, (rows, n), 1)
    to_cols = lax.broadcasted_iota(jnp.int32, (n, rows), 1) // 8 == lax.broadcasted_iota(jnp.int32, (n, rows), 0)
    to_rows, to_cols = (jnp.where(m, 1.0, 0.0).astype(BF16) for m in (to_rows, to_cols))
    row = lax.broadcasted_iota(jnp.int32, (rows, rows), 0)
    col = lax.broadcasted_iota(jnp.int32, (rows, rows), 1)
    same = jnp.bitwise_and(row, 7) == jnp.bitwise_and(col, 7)
    hi = kin[...].astype(BF16)
    lo = (kin[...] - hi.astype(F32)).astype(BF16)
    for i, part in enumerate((hi, lo)):
        tall = jnp.dot(to_rows, part, preferred_element_type=F32).astype(BF16)
        full = jnp.dot(tall, to_cols, preferred_element_type=F32)
        kron[rows * i : rows * (i + 1), :] = jnp.where(same, full, 0.0).astype(BF16)


def start_tile(state, adv, t, fields, levels):
    for row in (0, PAD + levels):
        adv[:, t, row : row + 8, :] = jnp.zeros((fields, 8, LANES), F32)


def own_kernel(part, facts, kin, u0, b0, tracers, *refs):
    u, b, state, kron, p_state, p_u, p_b = refs[-10:-3] if part == 0 else refs[-8:-1]
    adv = refs[-1]
    if part == 0:
        refs[-3][...] = refs[0][...]
        refs[-2][...] = refs[1][...]
    f = read_facts(facts)
    levels = u0.shape[0]
    n = tracers.shape[0]
    lane = lane_of(levels)
    gives = f["gives"] == 1
    tile = [f[f"tile{s}"] for s in range(WET_DEV)]
    joined = [f["joined0"], f["joined1"]]

    def start():
        expand_kinetics(kin, kron)
        for t in range(OCEAN_DEV):
            u[t] = u0[:, LANES * t : LANES * (t + 1)]
            b[t] = b0[:, LANES * t : LANES * (t + 1)]
        for s in range(WET_DEV):
            state[:, s] = tracers[:, :, LANES * s : LANES * (s + 1)].astype(F32)

        _, in_1, in_2, _ = patch_masks(f, levels // GROUPS)
        near = near_half(f, levels)

        def lay(own, beside, x):
            seg1 = fold(jnp.where(near, x, beside), 1)
            return jnp.where(in_1, seg1, jnp.where(in_2, fold(x, 2), fold(own, 0)))

        for p, field in ((p_u, u), (p_b, b)):
            p[...] = lay(field[f["outer_tile"]], field[f["beside_tile"]], field[f["x_tile"]])
        for j in range(n):
            p_state[j] = lay(*[state[j, f[name]] for name in ("outer_slot", "beside_slot", "x_slot")])

    def one_step(count, first, tile, joined):
        light = []
        for s in range(count):
            start_tile(state, adv, s, n, levels)
            light.append(absorbed_light(state[0, first + s]))
            b[tile[s]] = b[tile[s]] + HEATING * light[s]
        us = [u[t] for t in range(OCEAN_DEV)]
        bs = [b[t] for t in range(OCEAN_DEV)]
        for t in range(OCEAN_DEV):
            nxt, prv = (t + 1) % OCEAN_DEV, (t - 1) % OCEAN_DEV
            u_right = lane_roll(jnp.where(lane == 0, us[nxt], us[t]), LANES - 1)
            u_left = lane_roll(jnp.where(lane == LANES - 1, us[prv], us[t]), 1)
            b_right = lane_roll(jnp.where(lane == 0, bs[nxt], bs[t]), LANES - 1)
            u[t] = new_velocity(us[t], u_left, u_right, bs[t], b_right)
        parts = []
        for s in range(count):
            shut = lane == LANES - 1
            if s < count - 1:
                shut = jnp.logical_and(shut, joined[s] == 0)
            parts.append(face_parts(u[tile[s]], jnp.where(shut, 0.0, 1.0)))
        for s in range(count):
            pos, neg = parts[s]
            before = parts[s - 1] if s else (jnp.zeros_like(pos), jnp.zeros_like(neg))
            pos_left = lane_roll(jnp.where(lane == LANES - 1, before[0], pos), 1)
            neg_left = lane_roll(jnp.where(lane == LANES - 1, before[1], neg), 1)
            coeffs = (1.0 - pos + neg_left, pos_left, -neg)
            left = first + s - 1 if s else None
            right = first + s + 1 if s < count - 1 else None
            advect(state, adv, s, first + s, left, right, coeffs, n, levels)
        for s in range(count):
            ub, bb = u[tile[s]], b[tile[s]]
            kappa = diffusivity(ub, bb)
            warmth = KINETIC_DELTA * jnp.exp(THERMAL_GAIN * bb)

            def emit(r, values, s=s):
                state[:, first + s, r : r + 16, :] = values

            mix_and_react(adv, s, kappa, warmth, light[s], kron, n, levels, emit)

    def steps(begin, end):
        @pl.when(gives)
        def _():
            pl.loop(begin, end)(lambda _: one_step(WET_DEV, 0, tile, joined))

        @pl.when(jnp.logical_not(gives))
        def _():
            odd = f["odd"]
            tiles = [jnp.where(odd == 1, tile[s + 1], tile[s]) for s in range(WET_DEV - 1)]
            pairs = [jnp.where(odd == 1, joined[1], joined[0])]
            pl.loop(begin, end)(lambda _: one_step(WET_DEV - 1, odd, tiles, pairs))

    if part == 0:

        @pl.when(f["early"] == 1)
        def _():
            start()
            steps(0, EARLY_STEPS)

    else:
        pl.when(f["early"] == 0)(start)
        steps(f["early"] * EARLY_STEPS, STEPS)


def gate_kernel(strip, out, passed):
    out[...] = strip[...]
    passed[...] = strip[:8]


def advance_alone(state, adv, u, b, heat, face_open, kron, n, levels, emit, combined, groups=1):
    for step in range(STEPS):
        last = step == STEPS - 1
        light = absorbed_light(state[0, 0], groups)
        b = b + HEATING * heat * light
        u = new_velocity(u, lane_roll(u, 1), lane_roll(u, LANES - 1), b, lane_roll(b, LANES - 1), groups)
        if last:
            emit(None, (u, b))
        by_field = combined and not last
        count = n + 1 if by_field else n
        pos, neg = face_parts(u, face_open)
        pos_left, neg_left = lane_roll(pos, 1), lane_roll(neg, 1)
        advect(state, adv, 0, 0, None, None, (1.0 - pos + neg_left, pos_left, -neg), count, levels, groups)
        kappa = diffusivity(u, b, groups)
        warmth = KINETIC_DELTA * jnp.exp(THERMAL_GAIN * b)

        def put(r, values):
            state[:n, 0, r : r + 16, :] = values

        mix_and_react(adv, 0, kappa, warmth, light, kron, count, levels, emit if last else put, groups)


def from_strip(ref, rows, at, seg):
    shift = SEG * seg + HALF - at + 2 * LANES
    parts = [lane_roll(ref[rows * q : rows * (q + 1)], lax.rem(shift + GROUP * q, LANES)) for q in range(2)]
    return jnp.where(jnp.bitwise_and(lane_of(rows), GROUP) == 0, parts[0], parts[1])


def x_kernel(
    facts, kron, u0, b0, tracers, inner, pre_state, pre_u, pre_b,
    x_t, x_u, x_b, p_state, p_combo, p_u, p_b, state, adv,
):
    f = read_facts(facts)
    levels = u0.shape[0]
    half = levels // 2
    n = tracers.shape[0]
    gives = f["gives"] == 1
    lane = lane_of(levels)
    tile1 = inner[half : half + levels]
    tile2 = inner[half + levels :]
    start_tile(state, adv, 0, n, levels)

    rows = levels // GROUPS
    near, in_1, in_2, _ = patch_masks(f, rows)
    x_in_1 = jnp.logical_and(in_1, near)
    beyond = jnp.logical_and(in_2, near)
    face_open = jnp.where(lane == LANES - 1, 0.0, 1.0)

    def x_whole(patch, x):
        patch = jnp.where(x_in_1, fold(x, 1), patch)
        return jnp.where(in_2, fold(x, 2), patch)

    def with_far(patch, at):
        return jnp.where(beyond, from_strip(inner, rows, at, 2), patch)

    @pl.when(gives)
    def _():
        p_u[...] = with_far(pre_u[...], U_AT)
        p_b[...] = with_far(pre_b[...], B_AT)
        for j in range(1, n):
            p_state[j] = jnp.where(x_in_1, from_strip(inner, rows, 2 * j, 1), pre_state[j])
        p_state[0] = with_far(x_whole(pre_state[0], tile1), T0_AT)
        p_combo[...] = with_far(x_whole(pre_state[0], tile2), COMBO_AT)
        state[0, 0], state[1, 0] = tile1, tile2
        u, b = tile_of(u0, f["x_tile"]), tile_of(b0, f["x_tile"])
        for step in range(STEPS):
            light = absorbed_light(state[0, 0])
            b = b + HEATING * light
            u = new_velocity(u, lane_roll(u, 1), lane_roll(u, LANES - 1), b, lane_roll(b, LANES - 1))
            if step < STEPS - 1:
                pos, neg = face_parts(u, face_open)
                pos_left, neg_left = lane_roll(pos, 1), lane_roll(neg, 1)
                advect(state, adv, 0, 0, None, None, (1.0 - pos + neg_left, pos_left, -neg), 2, levels)
                kappa = diffusivity(u, b)
                mixed = []
                for i in range(2):
                    field = adv[i, 0, PAD : PAD + levels, :]
                    flux = kappa * (lower(field) - field)
                    row = lax.broadcasted_iota(jnp.int32, flux.shape, 0)
                    mixed.append(field + DT_MIX * (flux - jnp.where(row == 0, 0.0, pltpu.roll(flux, 1, 0))))
                warmth = KINETIC_DELTA * jnp.exp(THERMAL_GAIN * b)
                state[0, 0] = mixed[0] + warmth * mixed[1] + GROWTH * light
        x_u[...], x_b[...] = u, b

    @pl.when(jnp.logical_not(gives))
    def _():
        p_u[...] = with_far(x_whole(pre_u[...], tile1), U_AT)
        p_b[...] = with_far(x_whole(pre_b[...], tile2), B_AT)
        for j in range(n):
            p_state[j] = with_far(pre_state[j], 2 * j)
            state[j, 0] = slot_of(tracers, j, f["x_slot"])
        p_combo[...] = pre_state[0]

        def emit(r, values):
            if r is None:
                x_u[...], x_b[...] = values
            else:
                x_t[:, r : r + 16, :] = values

        advance_alone(state, adv, tile1, tile2, 1.0, face_open, kron, n, levels, emit, False)


def last_kernel(
    facts, kin, kron, outer, pre_state, p_combo, p_u, p_b, own_u, own_b, own_t, x_u, x_b, x_t,
    u_out, b_out, t_out, state, adv, whole_u, whole_b, merged, sems,
):
    f = read_facts(facts)
    rows = p_u.shape[0]
    levels = rows * GROUPS
    n = own_t.shape[0]
    gives, odd = f["gives"] == 1, f["odd"] == 1
    near, in_1, in_2, within = patch_masks(f, rows)
    halo = jnp.logical_not(jnp.logical_or(near, jnp.logical_or(in_1, in_2)))
    u = jnp.where(halo, from_strip(outer, rows, U_AT, 0), p_u[...])
    b = jnp.where(halo, from_strip(outer, rows, B_AT, 0), p_b[...])
    combo = None
    for j in range(n):
        x = jnp.where(halo, from_strip(outer, rows, 2 * j, 0), pre_state[j])
        state[j, 0] = x
        combo = kin[0:1, j : j + 1] * x if combo is None else combo + kin[0:1, j : j + 1] * x
    x_in_1 = jnp.logical_and(in_1, near)
    handed = jnp.logical_and(gives, jnp.logical_or(x_in_1, in_2))
    state[n, 0] = jnp.where(handed, p_combo[...], combo)

    def sides(here, there):
        return jnp.where(near, here.astype(F32), there.astype(F32))

    one = jnp.int32(1)
    heat = jnp.where(
        in_1,
        sides(one, f["beside_wet"]),
        jnp.where(in_2, sides(f["beyond_wet"], one), sides(f["outer_own_wet"], f["outer_far_wet"])),
    )
    outer_open = (f["outer_own_wet"] * f["outer_far_wet"]).astype(F32)
    boundary_open = jnp.where(
        in_1, f["beside_wet"].astype(F32), jnp.where(in_2, f["beyond_wet"].astype(F32), outer_open)
    )
    face_open = jnp.where(within == HALF - 1, boundary_open, 1.0)
    copies = []

    def send(src, dst):
        copies.append(pltpu.make_async_copy(src, dst, sems.at[len(copies)]))
        copies[-1].start()

    def at(index):
        return pl.ds(pl.multiple_of(index * LANES, LANES), LANES)

    def edge(count, at_left):
        lane = lane_of(count)
        return jnp.where(at_left, jnp.where(lane < FIX_FIRST, 1, 0), jnp.where(lane >= LANES - FIX_LAST, 1, 0)) == 1

    left, right = edge(rows, jnp.logical_not(odd)), edge(rows, odd)
    outer_fix = jnp.logical_and(left, f["outer_own_wet"] == 1)
    beside_fix = jnp.logical_and(right, f["beside_wet"] == 1)
    third = jnp.where(gives, 1, f["x_slot"])

    def emit(r, values):
        if r is None:
            for patch, own, x_ref, whole, out in (
                (values[0], own_u, x_u, whole_u, u_out),
                (values[1], own_b, x_b, whole_b, b_out),
            ):
                for t in range(OCEAN_DEV):
                    whole[:, LANES * t : LANES * (t + 1)] = own[t]
                for g in range(GROUPS):
                    s = slice(rows * g, rows * (g + 1))
                    seg0, seg1, seg2 = (unfold(patch, seg, g) for seg in range(3))
                    x = jnp.where(left, seg1, jnp.where(right, seg2, x_ref[s]))
                    whole[s, at(f["x_tile"])] = jnp.where(gives, x, own[f["x_tile"], s, :])
                    whole[s, at(f["outer_tile"])] = jnp.where(left, seg0, own[f["outer_tile"], s, :])
                    whole[s, at(f["beside_tile"])] = jnp.where(right, seg1, own[f["beside_tile"], s, :])
                send(whole, out)
            return
        for g in range(GROUPS):
            s = slice(rows * g, rows * (g + 1))
            seg0, seg1, seg2 = (unfold(values, seg, g) for seg in range(3))
            merged[:, 0, s, :] = jnp.where(outer_fix, seg0, own_t[:, f["outer_slot"], s, :]).astype(BF16)
            merged[:, 1, s, :] = jnp.where(beside_fix, seg1, own_t[:, f["beside_slot"], s, :]).astype(BF16)
            x = jnp.where(left, seg1, jnp.where(right, seg2, x_t[:, s, :]))
            merged[:, 2, s, :] = jnp.where(gives, own_t[:, 1, s, :], x).astype(BF16)

    advance_alone(state, adv, u, b, heat, face_open, kron, n, rows, emit, True, GROUPS)
    for i, slot in enumerate((f["outer_slot"], f["beside_slot"], third)):
        send(merged.at[:, i], t_out.at[:, :, at(slot)])
    for c in copies:
        c.wait()


def call(kernel, outs, scratch, args, spaces, out_spaces=None, aliases=None, flops=0, name=None):
    where = {"s": pltpu.SMEM, "v": pltpu.VMEM, "h": pltpu.HBM}
    out_spaces = out_spaces or "v" * len(outs)
    return pl.pallas_call(
        kernel,
        out_shape=tuple(
            pltpu.SMEM(s, d) if c == "s" else jax.ShapeDtypeStruct(s, d) for (s, d), c in zip(outs, out_spaces)
        ),
        in_specs=[pl.BlockSpec(memory_space=where[c]) for c in spaces],
        out_specs=tuple(pl.BlockSpec(memory_space=where[c]) for c in out_spaces),
        scratch_shapes=[pltpu.VMEM(s, F32) if isinstance(s, tuple) else s for s in scratch],
        input_output_aliases=aliases or {},
        compiler_params=pltpu.CompilerParams(vmem_limit_bytes=48 * 2**20),
        cost_estimate=pl.CostEstimate(flops=flops, bytes_accessed=0, transcendentals=0),
        name=name,
    )(*(pltpu.with_memory_space_constraint(a, pltpu.HBM) if c == "h" else a for a, c in zip(args, spaces)))


def on_device(ocean_u, ocean_b, tracers, wet_tiles, kinetic):
    axes = ("sec", "tile")
    devices = lax.axis_size("sec") * lax.axis_size("tile")
    levels, n = ocean_u.shape[0], tracers.shape[0]
    share = lax.axis_size("tile")
    dev = (lax.axis_index("sec") * share + lax.axis_index("tile")).astype(jnp.int32).reshape(1)
    strip = levels // 2
    fields = n + 1
    ocean, tile, patch = ocean_u.shape, (levels, LANES), (levels // GROUPS, LANES)
    wet_smem, kin_smem = pltpu.SMEM(wet_tiles.shape, jnp.int32), pltpu.SMEM(kinetic.shape, F32)
    inner, outer, u0, b0, t0, kinetic_v, facts = call(
        functools.partial(pack_kernel, share),
        [
            ((strip + 2 * levels, LANES), F32),
            ((strip, LANES), F32),
            (ocean, F32),
            (ocean, F32),
            (tracers.shape, BF16),
            (kinetic.shape, F32),
            ((len(FACTS),), jnp.int32),
        ],
        [wet_smem, kin_smem, pltpu.SemaphoreType.DMA((6,))],
        (dev, wet_tiles, kinetic, ocean_u, ocean_b, tracers),
        "shhhhh",
        "vvvvvvs",
        flops=10_000_000,
        name="pack",
    )
    in_pairs = [(i, i ^ 1) for i in range(devices)]
    across = [(i, (i + 1) % devices if i % 2 else (i - 1) % devices) for i in range(devices)]
    shapes = [
        ((OCEAN_DEV, *tile), F32),
        ((OCEAN_DEV, *tile), F32),
        ((n, WET_DEV, *tile), F32),
        ((2 * fields * 8, fields * 8), BF16),
        ((n, *patch), F32),
        (patch, F32),
        (patch, F32),
    ]
    adv = [(n, WET_DEV, levels + 2 * PAD, LANES)]
    *carried, inner, outer = call(
        functools.partial(own_kernel, 0),
        [*shapes, (inner.shape, F32), (outer.shape, F32)],
        adv,
        (facts, kinetic_v, u0, b0, t0, inner, outer),
        "svvvvvv",
        flops=1_000_000_000,
        name="own_tiles_early",
    )
    inner = lax.ppermute(inner, axes, in_pairs)
    outer, passed = call(
        gate_kernel,
        [(outer.shape, F32), ((8, LANES), F32)],
        [],
        (outer,),
        "v",
        flops=8_000_000_000,
        name="outer_strip",
    )
    outer = lax.ppermute(outer, axes, across)
    carried = call(
        functools.partial(own_kernel, 1),
        shapes,
        adv,
        (facts, kinetic_v, u0, b0, t0, *carried, passed),
        "svvvv" + "v" * len(carried) + "v",
        aliases={5 + i: i for i in range(len(carried))},
        flops=0,
        name="own_tiles",
    )
    own_u, own_b, own_t, kron, p_state, p_u, p_b = carried
    x_t, x_u, x_b, p_state, p_combo, p_u, p_b = call(
        x_kernel,
        [((n, *tile), F32), (tile, F32), (tile, F32), ((n, *patch), F32), (patch, F32), (patch, F32), (patch, F32)],
        [(n, 1, *tile), (n, 1, levels + 2 * PAD, LANES)],
        (facts, kron, u0, b0, t0, inner, p_state, p_u, p_b),
        "s" + "v" * 8,
        flops=0,
        name="x_tile",
    )
    return tuple(
        call(
            last_kernel,
            [(ocean, F32), (ocean, F32), (tracers.shape, BF16)],
            [
                (fields, 1, *patch),
                (fields, 1, levels // GROUPS + 2 * PAD, LANES),
                ocean,
                ocean,
                pltpu.VMEM((n, WET_DEV, *tile), BF16),
                pltpu.SemaphoreType.DMA((2 + WET_DEV * (levels // 16),)),
            ],
            (facts, kinetic_v, kron, outer, p_state, p_combo, p_u, p_b, own_u, own_b, own_t, x_u, x_b, x_t),
            "s" + "v" * 13,
            "hhh",
            flops=1_000_000_000,
            name="boundaries",
        )
    )


def solution(mesh):
    spread = P(None, ("sec", "tile"))
    tracer_spread = P(None, None, ("sec", "tile"))

    def program(ocean_u, ocean_b, tracers, wet_tiles, kinetic_matrix):
        u, b, t = jax.shard_map(
            on_device,
            mesh=mesh,
            in_specs=(spread, spread, tracer_spread, P(), P()),
            out_specs=(spread, spread, tracer_spread),
            check_vma=False,
        )(ocean_u, ocean_b, tracers, wet_tiles, kinetic_matrix)
        return t, u, b

    return program
```

```python
import functools

import jax
import jax.numpy as jnp
from jax import lax
from jax.experimental import pallas as pl
from jax.experimental.pallas import tpu as pltpu
from jax.sharding import PartitionSpec as P

LANES = 128
STEPS = 2
WET_DEV = 3
OCEAN_DEV = 4

DT_OCEAN = 0.25
PRESSURE = 1.0
HORIZ_VISC = 0.2
VERT_VISC = 0.2
HEATING = 0.2
KAPPA_BASE = 0.05
KAPPA_SPAN = 0.35
DT_TRACER = 0.3
DT_MIX = 1.0
KINETIC_DELTA = 0.5
SURFACE_LIGHT = 10.0
WATER_ATT = 0.04
PIGMENT_ATT = 0.08
GROWTH = 0.05
THERMAL_GAIN = 0.1

EARLY_STEPS = 1
GROUPS = 4
GROUP = LANES // GROUPS
SEG = 10
HALF = SEG // 2
FIX_FIRST, FIX_LAST = 3, 2
PAD = 8
F32, BF16 = jnp.float32, jnp.bfloat16


FACTS = (
    "odd",
    "gives",
    "x_slot",
    "x_tile",
    "outer_slot",
    "outer_tile",
    "beside_slot",
    "beside_tile",
    "outer_own_wet",
    "outer_far_wet",
    "beside_wet",
    "beyond_wet",
    "tile0",
    "tile1",
    "tile2",
    "joined0",
    "joined1",
    "early",
)


def find_facts(share, dev_ref, wet_ref, out_ref):
    k = dev_ref[0]
    odd = lax.rem(k, 2)
    first, base = WET_DEV * k, OCEAN_DEV * k
    listed = wet_ref.shape[0]
    tiles = listed // WET_DEV * OCEAN_DEV
    is_odd = odd == 1
    w = [wet_ref[first + s] for s in range(WET_DEV)]
    probe = wet_ref[first + jnp.where(is_odd, -1, 3)]
    gives = jnp.logical_and(probe >= base, probe < base + OCEAN_DEV)
    before = jnp.where(k == 0, listed - 1, first - 1)
    after = jnp.where(first + WET_DEV == listed, 0, first + WET_DEV)
    outer_far = jnp.where(
        is_odd,
        jnp.where(base + OCEAN_DEV == tiles, 0, base + OCEAN_DEV),
        jnp.where(k == 0, tiles - 1, base - 1),
    )
    far_listed = wet_ref[first + jnp.where(is_odd, -2, 4)] == base + jnp.where(is_odd, -1, 4)
    f = {"odd": odd, "early": lax.rem(k, share) == 0, "gives": gives, "x_slot": 2 - 2 * odd, "x_tile": 3 - 3 * odd}
    f["outer_slot"], f["outer_tile"] = 2 * odd, 3 * odd
    f["beside_slot"] = jnp.where(gives, 2 - 2 * odd, 1)
    f["beside_tile"] = jnp.where(gives, 2 - odd, 3 - 3 * odd)
    f["outer_own_wet"] = jnp.where(is_odd, w[2] == base + 3, w[0] == base)
    f["outer_far_wet"] = wet_ref[jnp.where(is_odd, after, before)] == outer_far
    f["beside_wet"] = jnp.logical_or(gives, w[1] == base + 3 - 3 * odd)
    f["beyond_wet"] = jnp.logical_or(jnp.logical_not(gives), far_listed)
    for s in range(WET_DEV):
        f[f"tile{s}"] = jnp.clip(w[s] - base, 0, OCEAN_DEV - 1)
    for s in range(WET_DEV - 1):
        x_here = jnp.logical_or(f["x_slot"] == s, f["x_slot"] == s + 1)
        f[f"joined{s}"] = jnp.logical_and(w[s + 1] - w[s] == 1, jnp.logical_or(gives, jnp.logical_not(x_here)))
    for i, name in enumerate(FACTS):
        out_ref[i] = f[name].astype(jnp.int32)


def read_facts(ref):
    return {name: ref[i] for i, name in enumerate(FACTS)}


def lane_of(rows):
    return lax.broadcasted_iota(jnp.int32, (rows, LANES), 1)


def lane_roll(x, shift):
    return pltpu.roll(x, shift, x.ndim - 1)


def row_of(x):
    return lax.broadcasted_iota(jnp.int32, x.shape, 0)


def upper(x, groups=1):
    row, rolled = row_of(x), pltpu.roll(x, 1, 0)
    if groups == 1:
        return jnp.where(row == 0, x, rolled)
    other = jnp.where(lane_of(x.shape[0]) < GROUP, x, lane_roll(rolled, GROUP))
    return jnp.where(row == 0, other, rolled)


def lower(x, groups=1):
    n = x.shape[0]
    row, rolled = row_of(x), pltpu.roll(x, n - 1, 0)
    if groups == 1:
        return jnp.where(row == n - 1, x, rolled)
    other = jnp.where(lane_of(n) >= LANES - GROUP, x, lane_roll(rolled, LANES - GROUP))
    return jnp.where(row == n - 1, other, rolled)


def at_top(x, groups):
    top = row_of(x) == 0
    return top if groups == 1 else jnp.logical_and(top, lane_of(x.shape[0]) < GROUP)


def at_bottom(x, groups):
    bottom = row_of(x) == x.shape[0] - 1
    return bottom if groups == 1 else jnp.logical_and(bottom, lane_of(x.shape[0]) >= LANES - GROUP)


def absorbed_light(pigment, groups=1):
    att = WATER_ATT + PIGMENT_ATT * pigment * pigment
    depth = att
    rows = att.shape[0]
    row = row_of(att)
    step = 1
    while step < rows:
        depth = depth + jnp.where(row >= step, pltpu.roll(depth, step, 0), 0.0)
        step *= 2
    if groups > 1:
        total = jnp.broadcast_to(depth[rows - 1 :], depth.shape)
        lane = lane_of(rows)
        for g in range(1, groups):
            depth = depth + jnp.where(lane >= GROUP * g, lane_roll(total, GROUP * g), 0.0)
    return SURFACE_LIGHT * (jnp.exp(att - depth) - jnp.exp(-depth))


def new_velocity(u, u_left, u_right, b, b_right, groups=1):
    horiz = u_left + u_right - 2.0 * u
    vert = upper(u, groups) + lower(u, groups) - 2.0 * u
    return u + DT_OCEAN * (HORIZ_VISC * horiz + VERT_VISC * vert - PRESSURE * (b_right - b))


def diffusivity(u, b, groups=1):
    shear = u - lower(u, groups)
    strat = b - lower(b, groups)
    kappa = KAPPA_BASE + KAPPA_SPAN * (1.0 / (1.0 + jnp.exp(-4.0 * (shear * shear - strat))))
    return jnp.where(at_bottom(kappa, groups), 0.0, kappa)


def face_parts(u, face_open):
    w = DT_TRACER * u * face_open
    return jnp.maximum(w, 0.0), jnp.minimum(w, 0.0)


def advect(state, adv, t, src, left, right, coeffs, fields, levels, groups=1):
    centre, from_left, from_right = coeffs
    chunk = 16
    lane = lane_of(chunk)
    for r in range(0, levels, chunk):
        s = slice(r, r + chunk)
        for f in range(fields):
            here = to_left = to_right = state[f, src, s, :]
            if right is not None:
                to_left = jnp.where(lane == 0, state[f, right, s, :], here)
            if left is not None:
                to_right = jnp.where(lane == LANES - 1, state[f, left, s, :], here)
            new = (
                here * centre[s] + lane_roll(to_left, LANES - 1) * from_right[s] + lane_roll(to_right, 1) * from_left[s]
            )
            adv[f, t, PAD + r : PAD + r + chunk, :] = new
            if groups > 1:
                assert levels == chunk
                adv[f, t, :PAD, :] = lane_roll(new[chunk - PAD :], GROUP)
                adv[f, t, PAD + chunk :, :] = lane_roll(new[:PAD], LANES - GROUP)


def mix_and_react(adv, t, kappa, warmth, light, kron, fields, levels, emit, groups=1):
    chunk = 16
    above = jnp.where(at_top(kappa, groups), 0.0, upper(kappa, groups))
    stay = 1.0 - DT_MIX * (kappa + above)
    rows = kron.shape[1]
    n = rows // 8 - 1
    k_hi, k_both = kron[:rows, :], kron[...]
    for r in range(0, levels, chunk):
        s = slice(r, r + chunk)
        at = PAD + r
        here = adv[:fields, t, at : at + chunk, :]
        up = adv[:fields, t, at - 1 : at - 1 + chunk, :]
        down = adv[:fields, t, at + 1 : at + 1 + chunk, :]
        mixed = here * stay[s] + (DT_MIX * kappa[s]) * down + (DT_MIX * above[s]) * up
        halves = []
        for h in range(2):
            part = mixed[:n, 8 * h : 8 * h + 8, :].reshape(n * 8, LANES)
            halves.append(jnp.concatenate([part, jnp.zeros((8, LANES), F32)], axis=0))
        wide = jnp.concatenate(halves, axis=1)
        hi = wide.astype(BF16)
        lo = (wide - hi.astype(F32)).astype(BF16)
        by_hi = jnp.dot(k_both, hi, preferred_element_type=F32)
        by_lo = jnp.dot(k_hi, lo, preferred_element_type=F32)
        drift = by_hi[:rows] + (by_hi[rows:] + by_lo)
        out = []
        for h in range(2):
            d = drift[:, LANES * h : LANES * h + LANES].reshape(n + 1, 8, LANES)
            part = mixed[:, 8 * h : 8 * h + 8, :]
            sh = slice(r + 8 * h, r + 8 * h + 8)
            first = part[:1] + warmth[sh] * (d[:1] if fields == n else part[n:]) + GROWTH * light[sh][None]
            out.append(jnp.concatenate([first, part[1:n] + warmth[sh] * d[1:n]], axis=0))
        emit(r, jnp.concatenate(out, axis=1))


def tile_of(ref, index):
    return ref[:, pl.ds(pl.multiple_of(index * LANES, LANES), LANES)]


def slot_as_stored(ref, j, index):
    return ref[j, :, pl.ds(pl.multiple_of(index * LANES, LANES), LANES)]


def slot_of(ref, j, index):
    return slot_as_stored(ref, j, index).astype(F32)


U_AT, B_AT, T0_AT, COMBO_AT, WIDE = 40, 44, 48, 50, 3


def pack_kernel(
    share, dev, wet_hbm, kin_hbm, u_hbm, b_hbm, t_hbm, inner, outer, u, b, tracers, kin_v, found, wet, kin, sems
):
    pairs = ((wet_hbm, wet), (kin_hbm, kin), (t_hbm, tracers), (u_hbm, u), (b_hbm, b), (kin_hbm, kin_v))
    copies = [pltpu.make_async_copy(src, dst, sems.at[i]) for i, (src, dst) in enumerate(pairs)]
    for c in copies:
        c.start()
    for c in copies:
        c.wait()
    find_facts(share, dev, wet, found)
    f = read_facts(found)
    levels = u.shape[0]
    half = levels // 2
    n = tracers.shape[0]
    lane = lane_of(half)

    def combo_of(index):
        total = None
        for j in range(n):
            term = kin[0, j] * slot_of(tracers, j, index)
            total = term if total is None else total + term
        return total

    def put(acc, value, at, width, right):
        for h in range(2):
            to = at + 64 * h
            here = jnp.bitwise_and(lane + right * width - to, LANES - 1) < width
            acc = jnp.where(here, lane_roll(value[half * h : half * (h + 1)], to), acc)
        return acc

    def strip(slot, tile, right):
        acc = jnp.zeros((half, LANES), F32)
        for j in range(n):
            acc = put(acc, slot_of(tracers, j, slot), 2 * j, 2, right)
        acc = put(acc, tile_of(u, tile), U_AT, WIDE, right)
        return put(acc, tile_of(b, tile), B_AT, WIDE, right)

    outer[...] = strip(f["outer_slot"], f["outer_tile"], f["odd"])
    x_combo = combo_of(f["x_slot"])
    acc = strip(f["x_slot"], f["beside_tile"], 1 - f["odd"])
    acc = put(acc, slot_of(tracers, 0, 1), T0_AT, 2, 1 - f["odd"])
    inner[:half] = put(acc, combo_of(1), COMBO_AT, 2, 1 - f["odd"])
    gives = f["gives"] == 1
    inner[half : half + levels] = jnp.where(gives, tile_of(u, f["x_tile"]), slot_of(tracers, 0, f["x_slot"]))
    inner[half + levels :] = jnp.where(gives, tile_of(b, f["x_tile"]), x_combo)


def near_half(f, rows):
    lane = lane_of(rows)
    return jnp.where(f["odd"] == 1, LANES - 1 - lane, lane) < LANES // 2


def patch_masks(f, rows):
    lane = jnp.bitwise_and(lane_of(rows), GROUP - 1)
    in_1 = jnp.logical_and(lane >= SEG, lane < 2 * SEG)
    in_2 = lane >= 2 * SEG
    within = lane - jnp.where(in_2, 2 * SEG, jnp.where(in_1, SEG, 0))
    near = jnp.where(f["odd"] == 1, SEG - 1 - within, within) >= HALF
    return near, in_1, in_2, within


def fold(x, seg):
    rows = x.shape[0] // GROUPS
    group = lane_of(rows) // GROUP
    out = None
    for g in range(GROUPS):
        part = lane_roll(x[rows * g : rows * (g + 1)], GROUP * g + SEG * seg + HALF)
        out = part if out is None else jnp.where(group == g, part, out)
    return out


def unfold(patch, seg, g):
    return lane_roll(patch, LANES - (GROUP * g + SEG * seg + HALF))


def expand_kinetics(kin, kron):
    n = kin.shape[0]
    rows = kron.shape[1]
    to_rows = lax.broadcasted_iota(jnp.int32, (rows, n), 0) // 8 == lax.broadcasted_iota(jnp.int32, (rows, n), 1)
    to_cols = lax.broadcasted_iota(jnp.int32, (n, rows), 1) // 8 == lax.broadcasted_iota(jnp.int32, (n, rows), 0)
    to_rows, to_cols = (jnp.where(m, 1.0, 0.0).astype(BF16) for m in (to_rows, to_cols))
    row = lax.broadcasted_iota(jnp.int32, (rows, rows), 0)
    col = lax.broadcasted_iota(jnp.int32, (rows, rows), 1)
    same = jnp.bitwise_and(row, 7) == jnp.bitwise_and(col, 7)
    hi = kin[...].astype(BF16)
    lo = (kin[...] - hi.astype(F32)).astype(BF16)
    for i, part in enumerate((hi, lo)):
        tall = jnp.dot(to_rows, part, preferred_element_type=F32).astype(BF16)
        full = jnp.dot(tall, to_cols, preferred_element_type=F32)
        kron[rows * i : rows * (i + 1), :] = jnp.where(same, full, 0.0).astype(BF16)


def start_tile(state, adv, t, fields, levels):
    for row in (0, PAD + levels):
        adv[:, t, row : row + 8, :] = jnp.zeros((fields, 8, LANES), F32)


def own_kernel(part, facts, kin, u0, b0, tracers, *refs):
    u, b, state, kron, p_state, p_u, p_b = refs[-10:-3] if part == 0 else refs[-8:-1]
    adv = refs[-1]
    if part == 0:
        refs[-3][...] = refs[0][...]
        refs[-2][...] = refs[1][...]
    f = read_facts(facts)
    levels = u0.shape[0]
    n = tracers.shape[0]
    lane = lane_of(levels)
    gives = f["gives"] == 1
    tile = [f[f"tile{s}"] for s in range(WET_DEV)]
    joined = [f["joined0"], f["joined1"]]

    def start():
        expand_kinetics(kin, kron)
        for t in range(OCEAN_DEV):
            u[t] = u0[:, LANES * t : LANES * (t + 1)]
            b[t] = b0[:, LANES * t : LANES * (t + 1)]
        for s in range(WET_DEV):
            state[:, s] = tracers[:, :, LANES * s : LANES * (s + 1)].astype(F32)

        _, in_1, in_2, _ = patch_masks(f, levels // GROUPS)
        near = near_half(f, levels)

        def lay(own, beside, x):
            seg1 = fold(jnp.where(near, x, beside), 1)
            return jnp.where(in_1, seg1, jnp.where(in_2, fold(x, 2), fold(own, 0)))

        for p, field in ((p_u, u), (p_b, b)):
            p[...] = lay(field[f["outer_tile"]], field[f["beside_tile"]], field[f["x_tile"]])
        for j in range(n):
            slots = [slot_as_stored(tracers, j, f[name]) for name in ("outer_slot", "beside_slot", "x_slot")]
            p_state[j] = lay(*slots).astype(F32)

    def one_step(count, first, tile, joined):
        light = []
        for s in range(count):
            start_tile(state, adv, s, n, levels)
            light.append(absorbed_light(state[0, first + s]))
            b[tile[s]] = b[tile[s]] + HEATING * light[s]
        us = [u[t] for t in range(OCEAN_DEV)]
        bs = [b[t] for t in range(OCEAN_DEV)]
        for t in range(OCEAN_DEV):
            nxt, prv = (t + 1) % OCEAN_DEV, (t - 1) % OCEAN_DEV
            u_right = lane_roll(jnp.where(lane == 0, us[nxt], us[t]), LANES - 1)
            u_left = lane_roll(jnp.where(lane == LANES - 1, us[prv], us[t]), 1)
            b_right = lane_roll(jnp.where(lane == 0, bs[nxt], bs[t]), LANES - 1)
            u[t] = new_velocity(us[t], u_left, u_right, bs[t], b_right)
        parts = []
        for s in range(count):
            shut = lane == LANES - 1
            if s < count - 1:
                shut = jnp.logical_and(shut, joined[s] == 0)
            parts.append(face_parts(u[tile[s]], jnp.where(shut, 0.0, 1.0)))
        for s in range(count):
            pos, neg = parts[s]
            before = parts[s - 1] if s else (jnp.zeros_like(pos), jnp.zeros_like(neg))
            pos_left = lane_roll(jnp.where(lane == LANES - 1, before[0], pos), 1)
            neg_left = lane_roll(jnp.where(lane == LANES - 1, before[1], neg), 1)
            coeffs = (1.0 - pos + neg_left, pos_left, -neg)
            left = first + s - 1 if s else None
            right = first + s + 1 if s < count - 1 else None
            advect(state, adv, s, first + s, left, right, coeffs, n, levels)
        for s in range(count):
            ub, bb = u[tile[s]], b[tile[s]]
            kappa = diffusivity(ub, bb)
            warmth = KINETIC_DELTA * jnp.exp(THERMAL_GAIN * bb)

            def emit(r, values, s=s):
                state[:, first + s, r : r + 16, :] = values

            mix_and_react(adv, s, kappa, warmth, light[s], kron, n, levels, emit)

    def steps(begin, end):
        @pl.when(gives)
        def _():
            pl.loop(begin, end)(lambda _: one_step(WET_DEV, 0, tile, joined))

        @pl.when(jnp.logical_not(gives))
        def _():
            odd = f["odd"]
            tiles = [jnp.where(odd == 1, tile[s + 1], tile[s]) for s in range(WET_DEV - 1)]
            pairs = [jnp.where(odd == 1, joined[1], joined[0])]
            pl.loop(begin, end)(lambda _: one_step(WET_DEV - 1, odd, tiles, pairs))

    if part == 0:

        @pl.when(f["early"] == 1)
        def _():
            start()
            steps(0, EARLY_STEPS)

    else:
        pl.when(f["early"] == 0)(start)
        steps(f["early"] * EARLY_STEPS, STEPS)


def gate_kernel(strip, out, passed):
    out[...] = strip[...]
    passed[...] = strip[:8]


def advance_alone(state, adv, u, b, heat, face_open, kron, n, levels, emit, combined, groups=1):
    for step in range(STEPS):
        last = step == STEPS - 1
        light = absorbed_light(state[0, 0], groups)
        b = b + HEATING * heat * light
        u = new_velocity(u, lane_roll(u, 1), lane_roll(u, LANES - 1), b, lane_roll(b, LANES - 1), groups)
        if last:
            emit(None, (u, b))
        by_field = combined and not last
        count = n + 1 if by_field else n
        pos, neg = face_parts(u, face_open)
        pos_left, neg_left = lane_roll(pos, 1), lane_roll(neg, 1)
        advect(state, adv, 0, 0, None, None, (1.0 - pos + neg_left, pos_left, -neg), count, levels, groups)
        kappa = diffusivity(u, b, groups)
        warmth = KINETIC_DELTA * jnp.exp(THERMAL_GAIN * b)

        def put(r, values):
            state[:n, 0, r : r + 16, :] = values

        mix_and_react(adv, 0, kappa, warmth, light, kron, count, levels, emit if last else put, groups)


def from_strip(ref, rows, at, seg):
    shift = SEG * seg + HALF - at + 2 * LANES
    parts = [lane_roll(ref[rows * q : rows * (q + 1)], lax.rem(shift + GROUP * q, LANES)) for q in range(2)]
    return jnp.where(jnp.bitwise_and(lane_of(rows), GROUP) == 0, parts[0], parts[1])


def x_kernel(
    facts, kron, u0, b0, tracers, inner, pre_state, pre_u, pre_b,
    x_t, x_u, x_b, p_state, p_combo, p_u, p_b, state, adv,
):
    f = read_facts(facts)
    levels = u0.shape[0]
    half = levels // 2
    n = tracers.shape[0]
    gives = f["gives"] == 1
    lane = lane_of(levels)
    tile1 = inner[half : half + levels]
    tile2 = inner[half + levels :]
    start_tile(state, adv, 0, n, levels)

    rows = levels // GROUPS
    near, in_1, in_2, _ = patch_masks(f, rows)
    x_in_1 = jnp.logical_and(in_1, near)
    beyond = jnp.logical_and(in_2, near)
    face_open = jnp.where(lane == LANES - 1, 0.0, 1.0)

    def x_whole(patch, x):
        patch = jnp.where(x_in_1, fold(x, 1), patch)
        return jnp.where(in_2, fold(x, 2), patch)

    def with_far(patch, at):
        return jnp.where(beyond, from_strip(inner, rows, at, 2), patch)

    @pl.when(gives)
    def _():
        p_u[...] = with_far(pre_u[...], U_AT)
        p_b[...] = with_far(pre_b[...], B_AT)
        for j in range(1, n):
            p_state[j] = jnp.where(x_in_1, from_strip(inner, rows, 2 * j, 1), pre_state[j])
        p_state[0] = with_far(x_whole(pre_state[0], tile1), T0_AT)
        p_combo[...] = with_far(x_whole(pre_state[0], tile2), COMBO_AT)
        state[0, 0], state[1, 0] = tile1, tile2
        u, b = tile_of(u0, f["x_tile"]), tile_of(b0, f["x_tile"])
        for step in range(STEPS):
            light = absorbed_light(state[0, 0])
            b = b + HEATING * light
            u = new_velocity(u, lane_roll(u, 1), lane_roll(u, LANES - 1), b, lane_roll(b, LANES - 1))
            if step < STEPS - 1:
                pos, neg = face_parts(u, face_open)
                pos_left, neg_left = lane_roll(pos, 1), lane_roll(neg, 1)
                advect(state, adv, 0, 0, None, None, (1.0 - pos + neg_left, pos_left, -neg), 2, levels)
                kappa = diffusivity(u, b)
                mixed = []
                for i in range(2):
                    field = adv[i, 0, PAD : PAD + levels, :]
                    flux = kappa * (lower(field) - field)
                    row = lax.broadcasted_iota(jnp.int32, flux.shape, 0)
                    mixed.append(field + DT_MIX * (flux - jnp.where(row == 0, 0.0, pltpu.roll(flux, 1, 0))))
                warmth = KINETIC_DELTA * jnp.exp(THERMAL_GAIN * b)
                state[0, 0] = mixed[0] + warmth * mixed[1] + GROWTH * light
        x_u[...], x_b[...] = u, b

    @pl.when(jnp.logical_not(gives))
    def _():
        p_u[...] = with_far(x_whole(pre_u[...], tile1), U_AT)
        p_b[...] = with_far(x_whole(pre_b[...], tile2), B_AT)
        for j in range(n):
            p_state[j] = with_far(pre_state[j], 2 * j)
            state[j, 0] = slot_of(tracers, j, f["x_slot"])
        p_combo[...] = pre_state[0]

        def emit(r, values):
            if r is None:
                x_u[...], x_b[...] = values
            else:
                x_t[:, r : r + 16, :] = values

        advance_alone(state, adv, tile1, tile2, 1.0, face_open, kron, n, levels, emit, False)


def last_kernel(
    facts, kin, kron, outer, pre_state, p_combo, p_u, p_b, own_u, own_b, own_t, x_u, x_b, x_t,
    u_out, b_out, t_out, state, adv, whole_u, whole_b, merged, sems,
):
    f = read_facts(facts)
    rows = p_u.shape[0]
    levels = rows * GROUPS
    n = own_t.shape[0]
    gives, odd = f["gives"] == 1, f["odd"] == 1
    near, in_1, in_2, within = patch_masks(f, rows)
    halo = jnp.logical_not(jnp.logical_or(near, jnp.logical_or(in_1, in_2)))
    u = jnp.where(halo, from_strip(outer, rows, U_AT, 0), p_u[...])
    b = jnp.where(halo, from_strip(outer, rows, B_AT, 0), p_b[...])
    combo = None
    for j in range(n):
        x = jnp.where(halo, from_strip(outer, rows, 2 * j, 0), pre_state[j])
        state[j, 0] = x
        combo = kin[0:1, j : j + 1] * x if combo is None else combo + kin[0:1, j : j + 1] * x
    x_in_1 = jnp.logical_and(in_1, near)
    handed = jnp.logical_and(gives, jnp.logical_or(x_in_1, in_2))
    state[n, 0] = jnp.where(handed, p_combo[...], combo)

    def sides(here, there):
        return jnp.where(near, here.astype(F32), there.astype(F32))

    one = jnp.int32(1)
    heat = jnp.where(
        in_1,
        sides(one, f["beside_wet"]),
        jnp.where(in_2, sides(f["beyond_wet"], one), sides(f["outer_own_wet"], f["outer_far_wet"])),
    )
    outer_open = (f["outer_own_wet"] * f["outer_far_wet"]).astype(F32)
    boundary_open = jnp.where(
        in_1, f["beside_wet"].astype(F32), jnp.where(in_2, f["beyond_wet"].astype(F32), outer_open)
    )
    face_open = jnp.where(within == HALF - 1, boundary_open, 1.0)
    copies = []

    def send(src, dst):
        copies.append(pltpu.make_async_copy(src, dst, sems.at[len(copies)]))
        copies[-1].start()

    def at(index):
        return pl.ds(pl.multiple_of(index * LANES, LANES), LANES)

    def edge(count, at_left):
        lane = lane_of(count)
        return jnp.where(at_left, jnp.where(lane < FIX_FIRST, 1, 0), jnp.where(lane >= LANES - FIX_LAST, 1, 0)) == 1

    left, right = edge(rows, jnp.logical_not(odd)), edge(rows, odd)
    outer_fix = jnp.logical_and(left, f["outer_own_wet"] == 1)
    beside_fix = jnp.logical_and(right, f["beside_wet"] == 1)

    def emit(r, values):
        if r is None:
            for patch, own, x_ref, whole, out in (
                (values[0], own_u, x_u, whole_u, u_out),
                (values[1], own_b, x_b, whole_b, b_out),
            ):
                for t in range(OCEAN_DEV):
                    whole[:, LANES * t : LANES * (t + 1)] = own[t]
                for g in range(GROUPS):
                    s = slice(rows * g, rows * (g + 1))
                    seg0, seg1, seg2 = (unfold(patch, seg, g) for seg in range(3))
                    x = jnp.where(left, seg1, jnp.where(right, seg2, x_ref[s]))
                    whole[s, at(f["x_tile"])] = jnp.where(gives, x, own[f["x_tile"], s, :])
                    whole[s, at(f["outer_tile"])] = jnp.where(left, seg0, own[f["outer_tile"], s, :])
                    whole[s, at(f["beside_tile"])] = jnp.where(right, seg1, own[f["beside_tile"], s, :])
                send(whole, out)
            return
        rounded = values.astype(BF16)
        parts = [slice(rows * g, rows * (g + 1)) for g in range(GROUPS)]
        for g, s in enumerate(parts):
            own = own_t[:, f["outer_slot"], s, :].astype(BF16)
            merged[:, 0, s, :] = jnp.where(outer_fix, unfold(rounded, 0, g), own)
        send(merged.at[:, 0], t_out.at[:, :, at(f["outer_slot"])])
        for g, s in enumerate(parts):
            own = own_t[:, f["beside_slot"], s, :].astype(BF16)
            merged[:, 1, s, :] = jnp.where(beside_fix, unfold(rounded, 1, g), own)
        send(merged.at[:, 1], t_out.at[:, :, at(f["beside_slot"])])
        for g, s in enumerate(parts):
            x = jnp.where(right, unfold(rounded, 2, g), x_t[:, s, :].astype(BF16))
            x = jnp.where(left, unfold(rounded, 1, g), x)
            merged[:, 2, s, :] = jnp.where(gives, own_t[:, 1, s, :].astype(BF16), x)
        send(merged.at[:, 2], t_out.at[:, :, at(jnp.where(gives, 1, f["x_slot"]))])

    advance_alone(state, adv, u, b, heat, face_open, kron, n, rows, emit, True, GROUPS)
    for c in copies:
        c.wait()


def call(kernel, outs, scratch, args, spaces, out_spaces=None, aliases=None, flops=0, name=None):
    where = {"s": pltpu.SMEM, "v": pltpu.VMEM, "h": pltpu.HBM}
    out_spaces = out_spaces or "v" * len(outs)
    return pl.pallas_call(
        kernel,
        out_shape=tuple(
            pltpu.SMEM(s, d) if c == "s" else jax.ShapeDtypeStruct(s, d) for (s, d), c in zip(outs, out_spaces)
        ),
        in_specs=[pl.BlockSpec(memory_space=where[c]) for c in spaces],
        out_specs=tuple(pl.BlockSpec(memory_space=where[c]) for c in out_spaces),
        scratch_shapes=[pltpu.VMEM(s, F32) if isinstance(s, tuple) else s for s in scratch],
        input_output_aliases=aliases or {},
        compiler_params=pltpu.CompilerParams(vmem_limit_bytes=48 * 2**20),
        cost_estimate=pl.CostEstimate(flops=flops, bytes_accessed=0, transcendentals=0),
        name=name,
    )(*(pltpu.with_memory_space_constraint(a, pltpu.HBM) if c == "h" else a for a, c in zip(args, spaces)))


def on_device(ocean_u, ocean_b, tracers, wet_tiles, kinetic):
    axes = ("sec", "tile")
    devices = lax.axis_size("sec") * lax.axis_size("tile")
    levels, n = ocean_u.shape[0], tracers.shape[0]
    share = lax.axis_size("tile")
    dev = (lax.axis_index("sec") * share + lax.axis_index("tile")).astype(jnp.int32).reshape(1)
    strip = levels // 2
    fields = n + 1
    ocean, tile, patch = ocean_u.shape, (levels, LANES), (levels // GROUPS, LANES)
    wet_smem, kin_smem = pltpu.SMEM(wet_tiles.shape, jnp.int32), pltpu.SMEM(kinetic.shape, F32)
    inner, outer, u0, b0, t0, kinetic_v, facts = call(
        functools.partial(pack_kernel, share),
        [
            ((strip + 2 * levels, LANES), F32),
            ((strip, LANES), F32),
            (ocean, F32),
            (ocean, F32),
            (tracers.shape, BF16),
            (kinetic.shape, F32),
            ((len(FACTS),), jnp.int32),
        ],
        [wet_smem, kin_smem, pltpu.SemaphoreType.DMA((6,))],
        (dev, wet_tiles, kinetic, ocean_u, ocean_b, tracers),
        "shhhhh",
        "vvvvvvs",
        flops=10_000_000,
        name="pack",
    )
    in_pairs = [(i, i ^ 1) for i in range(devices)]
    across = [(i, (i + 1) % devices if i % 2 else (i - 1) % devices) for i in range(devices)]
    shapes = [
        ((OCEAN_DEV, *tile), F32),
        ((OCEAN_DEV, *tile), F32),
        ((n, WET_DEV, *tile), F32),
        ((2 * fields * 8, fields * 8), BF16),
        ((n, *patch), F32),
        (patch, F32),
        (patch, F32),
    ]
    adv = [(n, WET_DEV, levels + 2 * PAD, LANES)]
    *carried, inner, outer = call(
        functools.partial(own_kernel, 0),
        [*shapes, (inner.shape, F32), (outer.shape, F32)],
        adv,
        (facts, kinetic_v, u0, b0, t0, inner, outer),
        "svvvvvv",
        flops=1_000_000_000,
        name="own_tiles_early",
    )
    inner = lax.ppermute(inner, axes, in_pairs)
    outer, passed = call(
        gate_kernel,
        [(outer.shape, F32), ((8, LANES), F32)],
        [],
        (outer,),
        "v",
        flops=8_000_000_000,
        name="outer_strip",
    )
    outer = lax.ppermute(outer, axes, across)
    carried = call(
        functools.partial(own_kernel, 1),
        shapes,
        adv,
        (facts, kinetic_v, u0, b0, t0, *carried, passed),
        "svvvv" + "v" * len(carried) + "v",
        aliases={5 + i: i for i in range(len(carried))},
        flops=0,
        name="own_tiles",
    )
    own_u, own_b, own_t, kron, p_state, p_u, p_b = carried
    x_t, x_u, x_b, p_state, p_combo, p_u, p_b = call(
        x_kernel,
        [((n, *tile), F32), (tile, F32), (tile, F32), ((n, *patch), F32), (patch, F32), (patch, F32), (patch, F32)],
        [(n, 1, *tile), (n, 1, levels + 2 * PAD, LANES)],
        (facts, kron, u0, b0, t0, inner, p_state, p_u, p_b),
        "s" + "v" * 8,
        flops=0,
        name="x_tile",
    )
    return tuple(
        call(
            last_kernel,
            [(ocean, F32), (ocean, F32), (tracers.shape, BF16)],
            [
                (fields, 1, *patch),
                (fields, 1, levels // GROUPS + 2 * PAD, LANES),
                ocean,
                ocean,
                pltpu.VMEM((n, WET_DEV, *tile), BF16),
                pltpu.SemaphoreType.DMA((2 + WET_DEV,)),
            ],
            (facts, kinetic_v, kron, outer, p_state, p_combo, p_u, p_b, own_u, own_b, own_t, x_u, x_b, x_t),
            "s" + "v" * 13,
            "hhh",
            flops=1_000_000_000,
            name="boundaries",
        )
    )


def solution(mesh):
    spread = P(None, ("sec", "tile"))
    tracer_spread = P(None, None, ("sec", "tile"))

    def program(ocean_u, ocean_b, tracers, wet_tiles, kinetic_matrix):
        u, b, t = jax.shard_map(
            on_device,
            mesh=mesh,
            in_specs=(spread, spread, tracer_spread, P(), P()),
            out_specs=(spread, spread, tracer_spread),
            check_vma=False,
        )(ocean_u, ocean_b, tracers, wet_tiles, kinetic_matrix)
        return t, u, b

    return program
```

```python
import functools

import jax
import jax.numpy as jnp
from jax import lax
from jax.experimental import pallas as pl
from jax.experimental.pallas import tpu as pltpu
from jax.sharding import PartitionSpec as P

LANES = 128
STEPS = 2
WET_DEV = 3
OCEAN_DEV = 4

DT_OCEAN = 0.25
PRESSURE = 1.0
HORIZ_VISC = 0.2
VERT_VISC = 0.2
HEATING = 0.2
KAPPA_BASE = 0.05
KAPPA_SPAN = 0.35
DT_TRACER = 0.3
DT_MIX = 1.0
KINETIC_DELTA = 0.5
SURFACE_LIGHT = 10.0
WATER_ATT = 0.04
PIGMENT_ATT = 0.08
GROWTH = 0.05
THERMAL_GAIN = 0.1

EARLY_STEPS = 1
GROUPS = 4
GROUP = LANES // GROUPS
SEG = 10
HALF = SEG // 2
FIX_FIRST, FIX_LAST = 3, 2
PAD = 8
F32, BF16 = jnp.float32, jnp.bfloat16


FACTS = (
    "odd",
    "gives",
    "x_slot",
    "x_tile",
    "outer_slot",
    "outer_tile",
    "beside_slot",
    "beside_tile",
    "outer_own_wet",
    "outer_far_wet",
    "beside_wet",
    "beyond_wet",
    "tile0",
    "tile1",
    "tile2",
    "joined0",
    "joined1",
    "early",
)


def find_facts(share, dev_ref, wet_ref, out_ref):
    k = dev_ref[0]
    odd = lax.rem(k, 2)
    first, base = WET_DEV * k, OCEAN_DEV * k
    listed = wet_ref.shape[0]
    tiles = listed // WET_DEV * OCEAN_DEV
    is_odd = odd == 1
    w = [wet_ref[first + s] for s in range(WET_DEV)]
    probe = wet_ref[first + jnp.where(is_odd, -1, 3)]
    gives = jnp.logical_and(probe >= base, probe < base + OCEAN_DEV)
    before = jnp.where(k == 0, listed - 1, first - 1)
    after = jnp.where(first + WET_DEV == listed, 0, first + WET_DEV)
    outer_far = jnp.where(
        is_odd,
        jnp.where(base + OCEAN_DEV == tiles, 0, base + OCEAN_DEV),
        jnp.where(k == 0, tiles - 1, base - 1),
    )
    far_listed = wet_ref[first + jnp.where(is_odd, -2, 4)] == base + jnp.where(is_odd, -1, 4)
    f = {"odd": odd, "early": lax.rem(k, share) == 0, "gives": gives, "x_slot": 2 - 2 * odd, "x_tile": 3 - 3 * odd}
    f["outer_slot"], f["outer_tile"] = 2 * odd, 3 * odd
    f["beside_slot"] = jnp.where(gives, 2 - 2 * odd, 1)
    f["beside_tile"] = jnp.where(gives, 2 - odd, 3 - 3 * odd)
    f["outer_own_wet"] = jnp.where(is_odd, w[2] == base + 3, w[0] == base)
    f["outer_far_wet"] = wet_ref[jnp.where(is_odd, after, before)] == outer_far
    f["beside_wet"] = jnp.logical_or(gives, w[1] == base + 3 - 3 * odd)
    f["beyond_wet"] = jnp.logical_or(jnp.logical_not(gives), far_listed)
    for s in range(WET_DEV):
        f[f"tile{s}"] = jnp.clip(w[s] - base, 0, OCEAN_DEV - 1)
    for s in range(WET_DEV - 1):
        x_here = jnp.logical_or(f["x_slot"] == s, f["x_slot"] == s + 1)
        f[f"joined{s}"] = jnp.logical_and(w[s + 1] - w[s] == 1, jnp.logical_or(gives, jnp.logical_not(x_here)))
    for i, name in enumerate(FACTS):
        out_ref[i] = f[name].astype(jnp.int32)


def read_facts(ref):
    return {name: ref[i] for i, name in enumerate(FACTS)}


def lane_of(rows):
    return lax.broadcasted_iota(jnp.int32, (rows, LANES), 1)


def lane_roll(x, shift):
    return pltpu.roll(x, shift, x.ndim - 1)


def row_of(x):
    return lax.broadcasted_iota(jnp.int32, x.shape, 0)


def upper(x, groups=1):
    row, rolled = row_of(x), pltpu.roll(x, 1, 0)
    if groups == 1:
        return jnp.where(row == 0, x, rolled)
    other = jnp.where(lane_of(x.shape[0]) < GROUP, x, lane_roll(rolled, GROUP))
    return jnp.where(row == 0, other, rolled)


def lower(x, groups=1):
    n = x.shape[0]
    row, rolled = row_of(x), pltpu.roll(x, n - 1, 0)
    if groups == 1:
        return jnp.where(row == n - 1, x, rolled)
    other = jnp.where(lane_of(n) >= LANES - GROUP, x, lane_roll(rolled, LANES - GROUP))
    return jnp.where(row == n - 1, other, rolled)


def at_top(x, groups):
    top = row_of(x) == 0
    return top if groups == 1 else jnp.logical_and(top, lane_of(x.shape[0]) < GROUP)


def at_bottom(x, groups):
    bottom = row_of(x) == x.shape[0] - 1
    return bottom if groups == 1 else jnp.logical_and(bottom, lane_of(x.shape[0]) >= LANES - GROUP)


def absorbed_light(pigment, groups=1):
    att = WATER_ATT + PIGMENT_ATT * pigment * pigment
    depth = att
    rows = att.shape[0]
    row = row_of(att)
    step = 1
    while step < rows:
        depth = depth + jnp.where(row >= step, pltpu.roll(depth, step, 0), 0.0)
        step *= 2
    if groups > 1:
        lane = lane_of(rows)
        over = [jnp.where(lane >= GROUP * g, lane_roll(att, GROUP * g), 0.0) for g in range(1, groups)]
        depth = depth + jnp.sum(sum(over[1:], over[0]), axis=0, keepdims=True)
    return SURFACE_LIGHT * (jnp.exp(att - depth) - jnp.exp(-depth))


def new_velocity(u, u_left, u_right, b, b_right, groups=1):
    horiz = u_left + u_right - 2.0 * u
    vert = upper(u, groups) + lower(u, groups) - 2.0 * u
    return u + DT_OCEAN * (HORIZ_VISC * horiz + VERT_VISC * vert - PRESSURE * (b_right - b))


def diffusivity(u, b, groups=1):
    shear = u - lower(u, groups)
    strat = b - lower(b, groups)
    kappa = KAPPA_BASE + KAPPA_SPAN * (1.0 / (1.0 + jnp.exp(-4.0 * (shear * shear - strat))))
    return jnp.where(at_bottom(kappa, groups), 0.0, kappa)


def face_parts(u, face_open):
    w = DT_TRACER * u * face_open
    return jnp.maximum(w, 0.0), jnp.minimum(w, 0.0)


def advect(state, adv, t, src, left, right, coeffs, fields, levels, groups=1):
    centre, from_left, from_right = coeffs
    chunk = 16
    lane = lane_of(chunk)
    for r in range(0, levels, chunk):
        s = slice(r, r + chunk)
        for f in range(fields):
            here = to_left = to_right = state[f, src, s, :]
            if right is not None:
                to_left = jnp.where(lane == 0, state[f, right, s, :], here)
            if left is not None:
                to_right = jnp.where(lane == LANES - 1, state[f, left, s, :], here)
            new = (
                here * centre[s] + lane_roll(to_left, LANES - 1) * from_right[s] + lane_roll(to_right, 1) * from_left[s]
            )
            adv[f, t, PAD + r : PAD + r + chunk, :] = new
            if groups > 1:
                assert levels == chunk
                adv[f, t, :PAD, :] = lane_roll(new[chunk - PAD :], GROUP)
                adv[f, t, PAD + chunk :, :] = lane_roll(new[:PAD], LANES - GROUP)


def mix_and_react(adv, t, kappa, warmth, light, kron, fields, levels, emit, groups=1):
    chunk = 16
    above = jnp.where(at_top(kappa, groups), 0.0, upper(kappa, groups))
    stay = 1.0 - DT_MIX * (kappa + above)
    rows = kron.shape[1]
    n = rows // 8 - 1
    k_hi, k_both = kron[:rows, :], kron[...]
    for r in range(0, levels, chunk):
        s = slice(r, r + chunk)
        at = PAD + r
        here = adv[:fields, t, at : at + chunk, :]
        up = adv[:fields, t, at - 1 : at - 1 + chunk, :]
        down = adv[:fields, t, at + 1 : at + 1 + chunk, :]
        mixed = here * stay[s] + (DT_MIX * kappa[s]) * down + (DT_MIX * above[s]) * up
        halves = []
        for h in range(2):
            part = mixed[:n, 8 * h : 8 * h + 8, :].reshape(n * 8, LANES)
            halves.append(jnp.concatenate([part, jnp.zeros((8, LANES), F32)], axis=0))
        wide = jnp.concatenate(halves, axis=1)
        hi = wide.astype(BF16)
        lo = (wide - hi.astype(F32)).astype(BF16)
        by_hi = jnp.dot(k_both, hi, preferred_element_type=F32)
        by_lo = jnp.dot(k_hi, lo, preferred_element_type=F32)
        drift = by_hi[:rows] + (by_hi[rows:] + by_lo)
        out = []
        for h in range(2):
            d = drift[:, LANES * h : LANES * h + LANES].reshape(n + 1, 8, LANES)
            part = mixed[:, 8 * h : 8 * h + 8, :]
            sh = slice(r + 8 * h, r + 8 * h + 8)
            first = part[:1] + warmth[sh] * (d[:1] if fields == n else part[n:]) + GROWTH * light[sh][None]
            out.append(jnp.concatenate([first, part[1:n] + warmth[sh] * d[1:n]], axis=0))
        emit(r, jnp.concatenate(out, axis=1))


def tile_of(ref, index):
    return ref[:, pl.ds(pl.multiple_of(index * LANES, LANES), LANES)]


def slot_as_stored(ref, j, index):
    return ref[j, :, pl.ds(pl.multiple_of(index * LANES, LANES), LANES)]


def slot_of(ref, j, index):
    return slot_as_stored(ref, j, index).astype(F32)


U_AT, B_AT, T0_AT, COMBO_AT, WIDE = 40, 44, 48, 50, 3


def pack_kernel(
    share, dev, wet_hbm, kin_hbm, u_hbm, b_hbm, t_hbm, inner, outer, u, b, tracers, kin_v, found, wet, kin, sems
):
    pairs = ((wet_hbm, wet), (kin_hbm, kin), (t_hbm, tracers), (u_hbm, u), (b_hbm, b), (kin_hbm, kin_v))
    copies = [pltpu.make_async_copy(src, dst, sems.at[i]) for i, (src, dst) in enumerate(pairs)]
    for c in copies:
        c.start()
    for c in copies:
        c.wait()
    find_facts(share, dev, wet, found)
    f = read_facts(found)
    levels = u.shape[0]
    half = levels // 2
    n = tracers.shape[0]
    lane = lane_of(half)

    def combo_of(index):
        total = None
        for j in range(n):
            term = kin[0, j] * slot_of(tracers, j, index)
            total = term if total is None else total + term
        return total

    def put(acc, value, at, width, right):
        for h in range(2):
            to = at + 64 * h
            here = jnp.bitwise_and(lane + right * width - to, LANES - 1) < width
            acc = jnp.where(here, lane_roll(value[half * h : half * (h + 1)], to), acc)
        return acc

    def strip(slot, tile, right):
        acc = jnp.zeros((half, LANES), F32)
        for j in range(n):
            acc = put(acc, slot_of(tracers, j, slot), 2 * j, 2, right)
        acc = put(acc, tile_of(u, tile), U_AT, WIDE, right)
        return put(acc, tile_of(b, tile), B_AT, WIDE, right)

    outer[...] = strip(f["outer_slot"], f["outer_tile"], f["odd"])
    x_combo = combo_of(f["x_slot"])
    acc = strip(f["x_slot"], f["beside_tile"], 1 - f["odd"])
    acc = put(acc, slot_of(tracers, 0, 1), T0_AT, 2, 1 - f["odd"])
    inner[:half] = put(acc, combo_of(1), COMBO_AT, 2, 1 - f["odd"])
    gives = f["gives"] == 1
    inner[half : half + levels] = jnp.where(gives, tile_of(u, f["x_tile"]), slot_of(tracers, 0, f["x_slot"]))
    inner[half + levels :] = jnp.where(gives, tile_of(b, f["x_tile"]), x_combo)


def near_half(f, rows):
    lane = lane_of(rows)
    return jnp.where(f["odd"] == 1, LANES - 1 - lane, lane) < LANES // 2


def patch_masks(f, rows):
    lane = jnp.bitwise_and(lane_of(rows), GROUP - 1)
    in_1 = jnp.logical_and(lane >= SEG, lane < 2 * SEG)
    in_2 = lane >= 2 * SEG
    within = lane - jnp.where(in_2, 2 * SEG, jnp.where(in_1, SEG, 0))
    near = jnp.where(f["odd"] == 1, SEG - 1 - within, within) >= HALF
    return near, in_1, in_2, within


def fold(x, seg):
    rows = x.shape[0] // GROUPS
    group = lane_of(rows) // GROUP
    out = None
    for g in range(GROUPS):
        part = lane_roll(x[rows * g : rows * (g + 1)], GROUP * g + SEG * seg + HALF)
        out = part if out is None else jnp.where(group == g, part, out)
    return out


def unfold(patch, seg, g):
    return lane_roll(patch, LANES - (GROUP * g + SEG * seg + HALF))


def expand_kinetics(kin, kron):
    n = kin.shape[0]
    rows = kron.shape[1]
    to_rows = lax.broadcasted_iota(jnp.int32, (rows, n), 0) // 8 == lax.broadcasted_iota(jnp.int32, (rows, n), 1)
    to_cols = lax.broadcasted_iota(jnp.int32, (n, rows), 1) // 8 == lax.broadcasted_iota(jnp.int32, (n, rows), 0)
    to_rows, to_cols = (jnp.where(m, 1.0, 0.0).astype(BF16) for m in (to_rows, to_cols))
    row = lax.broadcasted_iota(jnp.int32, (rows, rows), 0)
    col = lax.broadcasted_iota(jnp.int32, (rows, rows), 1)
    same = jnp.bitwise_and(row, 7) == jnp.bitwise_and(col, 7)
    hi = kin[...].astype(BF16)
    lo = (kin[...] - hi.astype(F32)).astype(BF16)
    for i, part in enumerate((hi, lo)):
        tall = jnp.dot(to_rows, part, preferred_element_type=F32).astype(BF16)
        full = jnp.dot(tall, to_cols, preferred_element_type=F32)
        kron[rows * i : rows * (i + 1), :] = jnp.where(same, full, 0.0).astype(BF16)


def start_tile(state, adv, t, fields, levels):
    for row in (0, PAD + levels):
        adv[:, t, row : row + 8, :] = jnp.zeros((fields, 8, LANES), F32)


def own_kernel(part, facts, kin, u0, b0, tracers, *refs):
    u, b, state, kron, p_state, p_u, p_b = refs[-10:-3] if part == 0 else refs[-8:-1]
    adv = refs[-1]
    if part == 0:
        refs[-3][...] = refs[0][...]
        refs[-2][...] = refs[1][...]
    f = read_facts(facts)
    levels = u0.shape[0]
    n = tracers.shape[0]
    lane = lane_of(levels)
    gives = f["gives"] == 1
    tile = [f[f"tile{s}"] for s in range(WET_DEV)]
    joined = [f["joined0"], f["joined1"]]

    def start():
        expand_kinetics(kin, kron)
        for t in range(OCEAN_DEV):
            u[t] = u0[:, LANES * t : LANES * (t + 1)]
            b[t] = b0[:, LANES * t : LANES * (t + 1)]
        for s in range(WET_DEV):
            state[:, s] = tracers[:, :, LANES * s : LANES * (s + 1)].astype(F32)

        _, in_1, in_2, _ = patch_masks(f, levels // GROUPS)
        near = near_half(f, levels)

        def lay(own, beside, x):
            seg1 = fold(jnp.where(near, x, beside), 1)
            return jnp.where(in_1, seg1, jnp.where(in_2, fold(x, 2), fold(own, 0)))

        for p, field in ((p_u, u), (p_b, b)):
            p[...] = lay(field[f["outer_tile"]], field[f["beside_tile"]], field[f["x_tile"]])
        for j in range(n):
            slots = [slot_as_stored(tracers, j, f[name]) for name in ("outer_slot", "beside_slot", "x_slot")]
            p_state[j] = lay(*slots).astype(F32)

    def one_step(count, first, tile, joined):
        light = []
        for s in range(count):
            start_tile(state, adv, s, n, levels)
            light.append(absorbed_light(state[0, first + s]))
            b[tile[s]] = b[tile[s]] + HEATING * light[s]
        us = [u[t] for t in range(OCEAN_DEV)]
        bs = [b[t] for t in range(OCEAN_DEV)]
        for t in range(OCEAN_DEV):
            nxt, prv = (t + 1) % OCEAN_DEV, (t - 1) % OCEAN_DEV
            u_right = lane_roll(jnp.where(lane == 0, us[nxt], us[t]), LANES - 1)
            u_left = lane_roll(jnp.where(lane == LANES - 1, us[prv], us[t]), 1)
            b_right = lane_roll(jnp.where(lane == 0, bs[nxt], bs[t]), LANES - 1)
            u[t] = new_velocity(us[t], u_left, u_right, bs[t], b_right)
        parts = []
        for s in range(count):
            shut = lane == LANES - 1
            if s < count - 1:
                shut = jnp.logical_and(shut, joined[s] == 0)
            parts.append(face_parts(u[tile[s]], jnp.where(shut, 0.0, 1.0)))
        for s in range(count):
            pos, neg = parts[s]
            before = parts[s - 1] if s else (jnp.zeros_like(pos), jnp.zeros_like(neg))
            pos_left = lane_roll(jnp.where(lane == LANES - 1, before[0], pos), 1)
            neg_left = lane_roll(jnp.where(lane == LANES - 1, before[1], neg), 1)
            coeffs = (1.0 - pos + neg_left, pos_left, -neg)
            left = first + s - 1 if s else None
            right = first + s + 1 if s < count - 1 else None
            advect(state, adv, s, first + s, left, right, coeffs, n, levels)
        for s in range(count):
            ub, bb = u[tile[s]], b[tile[s]]
            kappa = diffusivity(ub, bb)
            warmth = KINETIC_DELTA * jnp.exp(THERMAL_GAIN * bb)

            def emit(r, values, s=s):
                state[:, first + s, r : r + 16, :] = values

            mix_and_react(adv, s, kappa, warmth, light[s], kron, n, levels, emit)

    def steps(begin, end):
        @pl.when(gives)
        def _():
            pl.loop(begin, end)(lambda _: one_step(WET_DEV, 0, tile, joined))

        @pl.when(jnp.logical_not(gives))
        def _():
            odd = f["odd"]
            tiles = [jnp.where(odd == 1, tile[s + 1], tile[s]) for s in range(WET_DEV - 1)]
            pairs = [jnp.where(odd == 1, joined[1], joined[0])]
            pl.loop(begin, end)(lambda _: one_step(WET_DEV - 1, odd, tiles, pairs))

    if part == 0:

        @pl.when(f["early"] == 1)
        def _():
            start()
            steps(0, EARLY_STEPS)

    else:
        pl.when(f["early"] == 0)(start)
        steps(f["early"] * EARLY_STEPS, STEPS)


def gate_kernel(strip, out, passed):
    out[...] = strip[...]
    passed[...] = strip[:8]


def advance_alone(state, adv, u, b, heat, face_open, kron, n, levels, emit, combined, groups=1):
    for step in range(STEPS):
        last = step == STEPS - 1
        light = absorbed_light(state[0, 0], groups)
        b = b + HEATING * heat * light
        u = new_velocity(u, lane_roll(u, 1), lane_roll(u, LANES - 1), b, lane_roll(b, LANES - 1), groups)
        if last:
            emit(None, (u, b))
        by_field = combined and not last
        count = n + 1 if by_field else n
        pos, neg = face_parts(u, face_open)
        pos_left, neg_left = lane_roll(pos, 1), lane_roll(neg, 1)
        advect(state, adv, 0, 0, None, None, (1.0 - pos + neg_left, pos_left, -neg), count, levels, groups)
        kappa = diffusivity(u, b, groups)
        warmth = KINETIC_DELTA * jnp.exp(THERMAL_GAIN * b)

        def put(r, values):
            state[:n, 0, r : r + 16, :] = values

        mix_and_react(adv, 0, kappa, warmth, light, kron, count, levels, emit if last else put, groups)


def from_strip(ref, rows, at, seg):
    shift = SEG * seg + HALF - at + 2 * LANES
    parts = [lane_roll(ref[rows * q : rows * (q + 1)], lax.rem(shift + GROUP * q, LANES)) for q in range(2)]
    return jnp.where(jnp.bitwise_and(lane_of(rows), GROUP) == 0, parts[0], parts[1])


def x_kernel(
    facts, kron, u0, b0, tracers, inner, pre_state, pre_u, pre_b,
    x_t, x_u, x_b, p_state, p_combo, p_u, p_b, state, adv,
):
    f = read_facts(facts)
    levels = u0.shape[0]
    half = levels // 2
    n = tracers.shape[0]
    gives = f["gives"] == 1
    lane = lane_of(levels)
    tile1 = inner[half : half + levels]
    tile2 = inner[half + levels :]
    start_tile(state, adv, 0, n, levels)

    rows = levels // GROUPS
    near, in_1, in_2, _ = patch_masks(f, rows)
    x_in_1 = jnp.logical_and(in_1, near)
    beyond = jnp.logical_and(in_2, near)
    face_open = jnp.where(lane == LANES - 1, 0.0, 1.0)

    def x_whole(patch, x):
        patch = jnp.where(x_in_1, fold(x, 1), patch)
        return jnp.where(in_2, fold(x, 2), patch)

    def with_far(patch, at):
        return jnp.where(beyond, from_strip(inner, rows, at, 2), patch)

    @pl.when(gives)
    def _():
        p_u[...] = with_far(pre_u[...], U_AT)
        p_b[...] = with_far(pre_b[...], B_AT)
        for j in range(1, n):
            p_state[j] = jnp.where(x_in_1, from_strip(inner, rows, 2 * j, 1), pre_state[j])
        p_state[0] = with_far(x_whole(pre_state[0], tile1), T0_AT)
        p_combo[...] = with_far(x_whole(pre_state[0], tile2), COMBO_AT)
        state[0, 0], state[1, 0] = tile1, tile2
        u, b = tile_of(u0, f["x_tile"]), tile_of(b0, f["x_tile"])
        for step in range(STEPS):
            light = absorbed_light(state[0, 0])
            b = b + HEATING * light
            u = new_velocity(u, lane_roll(u, 1), lane_roll(u, LANES - 1), b, lane_roll(b, LANES - 1))
            if step < STEPS - 1:
                pos, neg = face_parts(u, face_open)
                pos_left, neg_left = lane_roll(pos, 1), lane_roll(neg, 1)
                advect(state, adv, 0, 0, None, None, (1.0 - pos + neg_left, pos_left, -neg), 2, levels)
                kappa = diffusivity(u, b)
                mixed = []
                for i in range(2):
                    field = adv[i, 0, PAD : PAD + levels, :]
                    flux = kappa * (lower(field) - field)
                    row = lax.broadcasted_iota(jnp.int32, flux.shape, 0)
                    mixed.append(field + DT_MIX * (flux - jnp.where(row == 0, 0.0, pltpu.roll(flux, 1, 0))))
                warmth = KINETIC_DELTA * jnp.exp(THERMAL_GAIN * b)
                state[0, 0] = mixed[0] + warmth * mixed[1] + GROWTH * light
        x_u[...], x_b[...] = u, b

    @pl.when(jnp.logical_not(gives))
    def _():
        p_u[...] = with_far(x_whole(pre_u[...], tile1), U_AT)
        p_b[...] = with_far(x_whole(pre_b[...], tile2), B_AT)
        for j in range(n):
            p_state[j] = with_far(pre_state[j], 2 * j)
            state[j, 0] = slot_of(tracers, j, f["x_slot"])
        p_combo[...] = pre_state[0]

        def emit(r, values):
            if r is None:
                x_u[...], x_b[...] = values
            else:
                x_t[:, r : r + 16, :] = values

        advance_alone(state, adv, tile1, tile2, 1.0, face_open, kron, n, levels, emit, False)


def last_kernel(
    facts, kin, kron, outer, pre_state, p_combo, p_u, p_b, own_u, own_b, own_t, x_u, x_b, x_t,
    u_out, b_out, t_out, state, adv, whole_u, whole_b, merged, sems,
):
    f = read_facts(facts)
    rows = p_u.shape[0]
    levels = rows * GROUPS
    n = own_t.shape[0]
    gives, odd = f["gives"] == 1, f["odd"] == 1
    near, in_1, in_2, within = patch_masks(f, rows)
    halo = jnp.logical_not(jnp.logical_or(near, jnp.logical_or(in_1, in_2)))
    u = jnp.where(halo, from_strip(outer, rows, U_AT, 0), p_u[...])
    b = jnp.where(halo, from_strip(outer, rows, B_AT, 0), p_b[...])
    combo = None
    for j in range(n):
        x = jnp.where(halo, from_strip(outer, rows, 2 * j, 0), pre_state[j])
        state[j, 0] = x
        combo = kin[0:1, j : j + 1] * x if combo is None else combo + kin[0:1, j : j + 1] * x
    x_in_1 = jnp.logical_and(in_1, near)
    handed = jnp.logical_and(gives, jnp.logical_or(x_in_1, in_2))
    state[n, 0] = jnp.where(handed, p_combo[...], combo)

    def sides(here, there):
        return jnp.where(near, here.astype(F32), there.astype(F32))

    one = jnp.int32(1)
    heat = jnp.where(
        in_1,
        sides(one, f["beside_wet"]),
        jnp.where(in_2, sides(f["beyond_wet"], one), sides(f["outer_own_wet"], f["outer_far_wet"])),
    )
    outer_open = (f["outer_own_wet"] * f["outer_far_wet"]).astype(F32)
    boundary_open = jnp.where(
        in_1, f["beside_wet"].astype(F32), jnp.where(in_2, f["beyond_wet"].astype(F32), outer_open)
    )
    face_open = jnp.where(within == HALF - 1, boundary_open, 1.0)
    copies = []

    def send(src, dst):
        copies.append(pltpu.make_async_copy(src, dst, sems.at[len(copies)]))
        copies[-1].start()

    def at(index):
        return pl.ds(pl.multiple_of(index * LANES, LANES), LANES)

    def edge(count, at_left):
        lane = lane_of(count)
        return jnp.where(at_left, jnp.where(lane < FIX_FIRST, 1, 0), jnp.where(lane >= LANES - FIX_LAST, 1, 0)) == 1

    left, right = edge(rows, jnp.logical_not(odd)), edge(rows, odd)
    outer_fix = jnp.logical_and(left, f["outer_own_wet"] == 1)
    beside_fix = jnp.logical_and(right, f["beside_wet"] == 1)

    def emit(r, values):
        if r is None:
            for patch, own, x_ref, whole, out in (
                (values[0], own_u, x_u, whole_u, u_out),
                (values[1], own_b, x_b, whole_b, b_out),
            ):
                for t in range(OCEAN_DEV):
                    whole[:, LANES * t : LANES * (t + 1)] = own[t]
                for g in range(GROUPS):
                    s = slice(rows * g, rows * (g + 1))
                    seg0, seg1, seg2 = (unfold(patch, seg, g) for seg in range(3))
                    x = jnp.where(left, seg1, jnp.where(right, seg2, x_ref[s]))
                    whole[s, at(f["x_tile"])] = jnp.where(gives, x, own[f["x_tile"], s, :])
                    whole[s, at(f["outer_tile"])] = jnp.where(left, seg0, own[f["outer_tile"], s, :])
                    whole[s, at(f["beside_tile"])] = jnp.where(right, seg1, own[f["beside_tile"], s, :])
                send(whole, out)
            return
        rounded = values.astype(BF16)
        parts = [slice(rows * g, rows * (g + 1)) for g in range(GROUPS)]
        for g, s in enumerate(parts):
            own = own_t[:, f["outer_slot"], s, :].astype(BF16)
            merged[:, 0, s, :] = jnp.where(outer_fix, unfold(rounded, 0, g), own)
        send(merged.at[:, 0], t_out.at[:, :, at(f["outer_slot"])])
        for g, s in enumerate(parts):
            own = own_t[:, f["beside_slot"], s, :].astype(BF16)
            merged[:, 1, s, :] = jnp.where(beside_fix, unfold(rounded, 1, g), own)
        send(merged.at[:, 1], t_out.at[:, :, at(f["beside_slot"])])
        for g, s in enumerate(parts):
            x = jnp.where(right, unfold(rounded, 2, g), x_t[:, s, :].astype(BF16))
            x = jnp.where(left, unfold(rounded, 1, g), x)
            merged[:, 2, s, :] = jnp.where(gives, own_t[:, 1, s, :].astype(BF16), x)
        send(merged.at[:, 2], t_out.at[:, :, at(jnp.where(gives, 1, f["x_slot"]))])

    advance_alone(state, adv, u, b, heat, face_open, kron, n, rows, emit, True, GROUPS)
    for c in copies:
        c.wait()


def call(kernel, outs, scratch, args, spaces, out_spaces=None, aliases=None, flops=0, name=None):
    where = {"s": pltpu.SMEM, "v": pltpu.VMEM, "h": pltpu.HBM}
    out_spaces = out_spaces or "v" * len(outs)
    return pl.pallas_call(
        kernel,
        out_shape=tuple(
            pltpu.SMEM(s, d) if c == "s" else jax.ShapeDtypeStruct(s, d) for (s, d), c in zip(outs, out_spaces)
        ),
        in_specs=[pl.BlockSpec(memory_space=where[c]) for c in spaces],
        out_specs=tuple(pl.BlockSpec(memory_space=where[c]) for c in out_spaces),
        scratch_shapes=[pltpu.VMEM(s, F32) if isinstance(s, tuple) else s for s in scratch],
        input_output_aliases=aliases or {},
        compiler_params=pltpu.CompilerParams(vmem_limit_bytes=48 * 2**20),
        cost_estimate=pl.CostEstimate(flops=flops, bytes_accessed=0, transcendentals=0),
        name=name,
    )(*(pltpu.with_memory_space_constraint(a, pltpu.HBM) if c == "h" else a for a, c in zip(args, spaces)))


def on_device(ocean_u, ocean_b, tracers, wet_tiles, kinetic):
    axes = ("sec", "tile")
    devices = lax.axis_size("sec") * lax.axis_size("tile")
    levels, n = ocean_u.shape[0], tracers.shape[0]
    share = lax.axis_size("tile")
    dev = (lax.axis_index("sec") * share + lax.axis_index("tile")).astype(jnp.int32).reshape(1)
    strip = levels // 2
    fields = n + 1
    ocean, tile, patch = ocean_u.shape, (levels, LANES), (levels // GROUPS, LANES)
    wet_smem, kin_smem = pltpu.SMEM(wet_tiles.shape, jnp.int32), pltpu.SMEM(kinetic.shape, F32)
    inner, outer, u0, b0, t0, kinetic_v, facts = call(
        functools.partial(pack_kernel, share),
        [
            ((strip + 2 * levels, LANES), F32),
            ((strip, LANES), F32),
            (ocean, F32),
            (ocean, F32),
            (tracers.shape, BF16),
            (kinetic.shape, F32),
            ((len(FACTS),), jnp.int32),
        ],
        [wet_smem, kin_smem, pltpu.SemaphoreType.DMA((6,))],
        (dev, wet_tiles, kinetic, ocean_u, ocean_b, tracers),
        "shhhhh",
        "vvvvvvs",
        flops=10_000_000,
        name="pack",
    )
    in_pairs = [(i, i ^ 1) for i in range(devices)]
    across = [(i, (i + 1) % devices if i % 2 else (i - 1) % devices) for i in range(devices)]
    shapes = [
        ((OCEAN_DEV, *tile), F32),
        ((OCEAN_DEV, *tile), F32),
        ((n, WET_DEV, *tile), F32),
        ((2 * fields * 8, fields * 8), BF16),
        ((n, *patch), F32),
        (patch, F32),
        (patch, F32),
    ]
    adv = [(n, WET_DEV, levels + 2 * PAD, LANES)]
    *carried, inner, outer = call(
        functools.partial(own_kernel, 0),
        [*shapes, (inner.shape, F32), (outer.shape, F32)],
        adv,
        (facts, kinetic_v, u0, b0, t0, inner, outer),
        "svvvvvv",
        flops=1_000_000_000,
        name="own_tiles_early",
    )
    inner = lax.ppermute(inner, axes, in_pairs)
    outer, passed = call(
        gate_kernel,
        [(outer.shape, F32), ((8, LANES), F32)],
        [],
        (outer,),
        "v",
        flops=8_000_000_000,
        name="outer_strip",
    )
    outer = lax.ppermute(outer, axes, across)
    carried = call(
        functools.partial(own_kernel, 1),
        shapes,
        adv,
        (facts, kinetic_v, u0, b0, t0, *carried, passed),
        "svvvv" + "v" * len(carried) + "v",
        aliases={5 + i: i for i in range(len(carried))},
        flops=0,
        name="own_tiles",
    )
    own_u, own_b, own_t, kron, p_state, p_u, p_b = carried
    x_t, x_u, x_b, p_state, p_combo, p_u, p_b = call(
        x_kernel,
        [((n, *tile), F32), (tile, F32), (tile, F32), ((n, *patch), F32), (patch, F32), (patch, F32), (patch, F32)],
        [(n, 1, *tile), (n, 1, levels + 2 * PAD, LANES)],
        (facts, kron, u0, b0, t0, inner, p_state, p_u, p_b),
        "s" + "v" * 8,
        flops=0,
        name="x_tile",
    )
    return tuple(
        call(
            last_kernel,
            [(ocean, F32), (ocean, F32), (tracers.shape, BF16)],
            [
                (fields, 1, *patch),
                (fields, 1, levels // GROUPS + 2 * PAD, LANES),
                ocean,
                ocean,
                pltpu.VMEM((n, WET_DEV, *tile), BF16),
                pltpu.SemaphoreType.DMA((2 + WET_DEV,)),
            ],
            (facts, kinetic_v, kron, outer, p_state, p_combo, p_u, p_b, own_u, own_b, own_t, x_u, x_b, x_t),
            "s" + "v" * 13,
            "hhh",
            flops=1_000_000_000,
            name="boundaries",
        )
    )


def solution(mesh):
    spread = P(None, ("sec", "tile"))
    tracer_spread = P(None, None, ("sec", "tile"))

    def program(ocean_u, ocean_b, tracers, wet_tiles, kinetic_matrix):
        u, b, t = jax.shard_map(
            on_device,
            mesh=mesh,
            in_specs=(spread, spread, tracer_spread, P(), P()),
            out_specs=(spread, spread, tracer_spread),
            check_vma=False,
        )(ocean_u, ocean_b, tracers, wet_tiles, kinetic_matrix)
        return t, u, b

    return program
```
